32 devices in a mesh: dp: 4 (over x, core), seq: 8 (over z, y).
Axes of the slice: x: 2, y: 2, z: 4, core: 2. Of those that a mesh axis runs over, the one named last changes fastest.
Arguments:
- tokens: bfloat16 [16384, 768], P(('dp', 'seq')), may hold values from -6 to 6
- cotangent: bfloat16 [16384, 768], P(('dp', 'seq')), may hold values from -6 to 6
- document_bounds: int32 [4, 2], replicated, may hold values from 1 to 4095, as said below
- routes: int32 [3, 2048], P(None, ('dp', 'seq')), may hold values from -1 to 511, as said below
- attention_gain: float32 [768], replicated, may hold values from 0.5 to 1.5
- feedforward_gain: float32 [768], replicated, may hold values from 0.5 to 1.5
- router: float32 [3, 768], replicated, may hold values from -0.21875 to 0.21875
- light_query: bfloat16 [768, 768], replicated, may hold values from -0.3125 to 0.3125
- light_keyval: bfloat16 [768, 1536], replicated, may hold values from -0.21875 to 0.21875
- light_output: bfloat16 [768, 768], replicated, may hold values from -0.875 to 0.875
- heavy_query: bfloat16 [768, 768], replicated, may hold values from -0.3125 to 0.3125
- heavy_keyval: bfloat16 [768, 1536], replicated, may hold values from -0.21875 to 0.21875
- heavy_output_weight: bfloat16 [768, 768], replicated, may hold values from -0.875 to 0.875
- light_expand: bfloat16 [768, 2048], replicated, may hold values from -0.21875 to 0.21875
- light_reduce: bfloat16 [1024, 768], replicated, may hold values from -0.1875 to 0.1875
- heavy_expand: bfloat16 [768, 8192], replicated, may hold values from -0.21875 to 0.21875
- heavy_reduce: bfloat16 [4096, 768], replicated, may hold values from -0.09375 to 0.09375
Outputs:
- output: bfloat16 [16384, 768], P(('dp', 'seq'))
- tokens_grad: bfloat16 [16384, 768], P(('dp', 'seq'))
- attention_gain_grad: float32 [768], P('seq')
- feedforward_gain_grad: float32 [768], P('seq')
- router_grad: float32 [3, 768], P(None, 'seq')
- light_query_grad: float32 [768, 768], P('seq', 'dp')
- light_keyval_grad: float32 [768, 1536], P('seq', 'dp')
- light_output_grad: float32 [768, 768], P('seq', 'dp')
- heavy_query_grad: float32 [768, 768], P('seq', 'dp')
- heavy_keyval_grad: float32 [768, 1536], P('seq', 'dp')
- heavy_output_grad: float32 [768, 768], P('seq', 'dp')
- light_expand_grad: float32 [768, 2048], P('seq', 'dp')
- light_reduce_grad: float32 [1024, 768], P('seq', 'dp')
- heavy_expand_grad: float32 [768, 8192], P('seq', 'dp')
- heavy_reduce_grad: float32 [4096, 768], P('seq', 'dp')
The draws below stay inside these ranges and needn't reach their ends.
Inputs may be any that keep to these rules, and one draw needn't show every extreme that they name: For each group, document_bounds holds (start, end) with 1 <= start <= 256 and 3840 <= end <= 4095. `routes`: within each block of 64 slots of a router the named tokens are distinct and come first, followed by -1 entries; each block names 32 to 64 tokens, and for each router some block names 64.
All inputs are finite; a program needn't handle non-finite values.
Results may differ from the reference program's by a relative error of at most 0.018.
Values may be sent and summed in bfloat16 or wider, within the bound.
No kernel may reach another device: no remote copies, remote signals or barrier semaphores. Data moves between devices by JAX's collectives and lax.ppermute only.
A program may use at most 320 MiB of HBM per device.

```python
import jax
import jax.numpy as jnp
from jax import lax

D = 768
LH = 8
HH = 12
HHS = 64
HD = 768
FFL = 1024
FFH = 4096
WINDOW = 128
TOK_DEV = 512
ROUTE_SLOTS = 64
SEQ_TOK = 4096
GROUPS = 4
BLOCKS = 32
TOKENS = 16384
N_SEQ = 8


def draw_document_bounds(key, part):
    start_key, end_key = jax.random.split(key)
    starting = jax.random.randint(start_key, (GROUPS,), 1, TOK_DEV // 2 + 1)
    ending = jax.random.randint(end_key, (GROUPS,), SEQ_TOK - TOK_DEV // 2, SEQ_TOK)
    return jnp.stack([starting, ending], 1).astype(jnp.int32)


def draw_routes(key, part):
    count_key, full_key, order_key = jax.random.split(key, 3)
    counts = jax.random.randint(count_key, (3, BLOCKS), ROUTE_SLOTS // 2, ROUTE_SLOTS + 1)
    fullest = jax.random.randint(full_key, (3, 1), 0, BLOCKS)
    counts = jnp.where(jnp.arange(BLOCKS)[None, :] == fullest, ROUTE_SLOTS, counts)
    noise_bits = jax.random.randint(order_key, (3, BLOCKS, TOK_DEV), 0, 2 ** 18)
    ranking = noise_bits * TOK_DEV + jnp.arange(TOK_DEV, dtype=jnp.int32)[None, None, :]
    ordered = jnp.argsort(ranking, axis=-1, stable=True)[:, :, :ROUTE_SLOTS].astype(jnp.int32)
    slot_lane = jnp.arange(ROUTE_SLOTS, dtype=jnp.int32)[None, None, :]
    picked = jnp.where(slot_lane < counts[:, :, None], ordered, -1)
    return picked.reshape(3, BLOCKS * ROUTE_SLOTS).astype(jnp.int32)


def shard_levels(rng, shape, shards, least, high):
    factor_of, own = 1.0, jax.random.fold_in(rng, 6)
    for dim, parts in shards:
        steps = jnp.exp(jax.random.uniform(jax.random.fold_in(own, dim), (parts,), jnp.float32, least / len(shards), high / len(shards)))
        factor_of = factor_of * jnp.repeat(steps, shape[dim] // parts).reshape([-1 if axis == dim else 1 for axis in range(len(shape))])
    return factor_of


def noise(stream_key, shape, width, most, cuts=(), kind=jnp.bfloat16):
    values = width * jax.random.normal(stream_key, shape, jnp.float32)
    if cuts:
        values = values * shard_levels(stream_key, shape, cuts, -0.22, 0.18)
    return jnp.clip(values, -most, most).astype(kind)


def setup_inputs(seed: int = 0) -> dict:
    keys = jax.random.split(jax.random.key(seed), 18)
    tokens = noise(keys[0], (TOKENS, D), 1.0, 6.0, ((0, 32),))
    cotangent = noise(keys[1], (TOKENS, D), 1.0, 6.0, ((0, 32),))
    document_bounds = draw_document_bounds(jax.random.fold_in(keys[17], 71), 0)
    routes = draw_routes(jax.random.fold_in(keys[17], 71), 0)
    attention_gain = jnp.clip(1.0 + 0.1 * jax.random.normal(keys[4], (D,), jnp.float32), 0.5, 1.5)
    feedforward_gain = jnp.clip(1.0 + 0.1 * jax.random.normal(keys[5], (D,), jnp.float32), 0.5, 1.5)
    router = noise(keys[6], (3, D), D ** -0.5, 0.21875, (), jnp.float32)
    light_query = noise(keys[7], (D, D), (D // 2) ** -0.5, 0.3125)
    light_keyval = noise(keys[8], (D, 2 * D), D ** -0.5, 0.21875)
    light_output = noise(keys[9], (D, D), (D // 16) ** -0.5, 0.875)
    heavy_query = noise(keys[10], (D, HD), (D // 2) ** -0.5, 0.3125)
    heavy_keyval = noise(keys[11], (D, 2 * HD), D ** -0.5, 0.21875)
    heavy_output_weight = noise(keys[12], (HD, D), (HD // 16) ** -0.5, 0.875)
    light_expand = noise(keys[13], (D, 2 * FFL), D ** -0.5, 0.21875)
    light_reduce = noise(keys[14], (FFL, D), FFL ** -0.5, 0.1875)
    heavy_expand = noise(keys[15], (D, 2 * FFH), D ** -0.5, 0.21875)
    heavy_reduce = noise(keys[16], (FFH, D), FFH ** -0.5, 0.09375)
    return dict(tokens=tokens, cotangent=cotangent, document_bounds=document_bounds, routes=routes, attention_gain=attention_gain, feedforward_gain=feedforward_gain, router=router, light_query=light_query, light_keyval=light_keyval, light_output=light_output, heavy_query=heavy_query, heavy_keyval=heavy_keyval, heavy_output_weight=heavy_output_weight, light_expand=light_expand, light_reduce=light_reduce, heavy_expand=heavy_expand, heavy_reduce=heavy_reduce)


EPSILON = 1e-06
MASKED = -1e+30
HIGHEST = lax.Precision.HIGHEST

@jax.custom_vjp
def low(v):
    return lax.optimization_barrier(v.astype(jnp.bfloat16)).astype(jnp.float32)

@jax.custom_vjp
def low_back(v):
    return v

def low_keep(v):
    return (low(v), None)

def low_pass(kept, grad):
    return (grad,)

def back_keep(v):
    return (v, None)

def back_low(kept, grad):
    return (low(grad),)
low.defvjp(low_keep, low_pass)
low_back.defvjp(back_keep, back_low)

def rounded(signal):
    return low_back(low(signal))

def elementwise_product(former, latter):
    return jnp.dot(former, latter, precision=HIGHEST)

def rms_norm(signal, scaling):
    return signal * lax.rsqrt(lax.optimization_barrier(jnp.mean(signal * signal, -1, keepdims=True)) + EPSILON) * scaling

def gated_gelu(paired):
    halfway = paired.shape[-1] // 2
    return jax.nn.gelu(paired[:, :halfway]) * paired[:, halfway:]

def segment_of(token_positions, bounds):
    return (token_positions >= bounds[0]).astype(jnp.int32) + (token_positions >= bounds[1]).astype(jnp.int32)

def light_attention(queries, keyvals, bounds):
    length = queries.shape[0]
    rows_block = min(512, TOK_DEV)
    window_span = rows_block + 2 * WINDOW
    head_size = D // LH
    padded = jnp.pad(keyvals, ((WINDOW, WINDOW), (0, 0)))

    def one_block(offset):
        query_part = lax.dynamic_slice_in_dim(queries, offset, rows_block, 0).reshape(rows_block, LH, head_size)
        keyval_part = lax.dynamic_slice_in_dim(padded, offset, window_span, 0)
        key_part = keyval_part[:, :D].reshape(window_span, LH, head_size)
        value_part = keyval_part[:, D:].reshape(window_span, LH, head_size)
        scores = low_back(jnp.einsum('qhd,khd->hqk', query_part, key_part, precision=HIGHEST) * head_size ** (-0.5))
        query_place = offset + jnp.arange(rows_block, dtype=jnp.int32)
        key_place = offset - WINDOW + jnp.arange(window_span, dtype=jnp.int32)
        allowed = (key_place[None, :] >= 0) & (key_place[None, :] < length)
        allowed = allowed & (jnp.abs(query_place[:, None] - key_place[None, :]) <= WINDOW)
        allowed = allowed & (segment_of(query_place, bounds)[:, None] == segment_of(key_place, bounds)[None, :])
        masked = jnp.where(allowed[None], scores, MASKED)
        exponent = jnp.exp(masked - lax.optimization_barrier(jnp.max(masked, -1, keepdims=True)))
        weights = low(exponent / lax.optimization_barrier(jnp.sum(exponent, -1, keepdims=True)))
        return jnp.einsum('hqk,khd->qhd', weights, value_part, precision=HIGHEST).reshape(rows_block, D)
    offsets = jnp.arange(0, length, rows_block, dtype=jnp.int32)
    return lax.map(jax.checkpoint(one_block), offsets).reshape(length, D)

def heavy_attention(queries, keys_in, values_in, query_places, key_places, bounds):
    counted = queries.shape[0]
    rows_block = min(512, counted)
    key_segment = segment_of(key_places, bounds)
    key_valid = key_places >= 0
    key_heads = keys_in.reshape(counted, HH, HHS)
    value_heads = values_in.reshape(counted, HH, HHS)

    def one_block(offset):
        query_part = lax.dynamic_slice_in_dim(queries, offset, rows_block, 0).reshape(rows_block, HH, HHS)
        query_segment = segment_of(lax.dynamic_slice_in_dim(query_places, offset, rows_block, 0), bounds)
        scores = low_back(jnp.einsum('qhd,khd->hqk', query_part, key_heads, precision=HIGHEST) * HHS ** (-0.5))
        allowed = key_valid[None, :] & (query_segment[:, None] == key_segment[None, :])
        masked = jnp.where(allowed[None], scores, MASKED)
        exponent = jnp.where(allowed[None], jnp.exp(masked - lax.optimization_barrier(jnp.max(masked, -1, keepdims=True))), 0.0)
        row_total = lax.optimization_barrier(jnp.sum(exponent, -1, keepdims=True))
        weights = low(exponent / jnp.where(row_total > 0, row_total, 1.0))
        return jnp.einsum('hqk,khd->qhd', weights, value_heads, precision=HIGHEST).reshape(rows_block, HD)
    offsets = jnp.arange(0, counted, rows_block, dtype=jnp.int32)
    return lax.map(jax.checkpoint(one_block), offsets).reshape(counted, HD)

def group_forward(inputs, bounds, routes, attention_gain, feedforward_gain, router, light_query, light_keyval, light_output, heavy_query, heavy_keyval, heavy_output_weight, light_expand, light_reduce, heavy_expand, heavy_reduce):
    normed_mixer = rms_norm(inputs, attention_gain)
    attention_lower = low(normed_mixer)
    query_light = rounded(elementwise_product(attention_lower, light_query))
    keyval_light = rounded(elementwise_product(attention_lower, light_keyval))
    attended = rounded(light_attention(query_light, keyval_light, bounds))
    residual = inputs + low_back(elementwise_product(attended, light_output))
    owners = jnp.arange(routes.shape[1], dtype=jnp.int32) // ROUTE_SLOTS
    token_positions = jnp.where(routes >= 0, owners[None, :] * TOK_DEV + routes, -1)
    alive_flags = (token_positions >= 0).astype(jnp.float32)
    clamped_scores = jnp.maximum(token_positions, 0)
    score_query = jax.nn.sigmoid(jnp.take(elementwise_product(normed_mixer, router[0]), clamped_scores[0]))
    score_keyval = jax.nn.sigmoid(jnp.take(elementwise_product(normed_mixer, router[1]), clamped_scores[1]))
    query_row_index = jnp.take(attention_lower, clamped_scores[0], axis=0) * alive_flags[0][:, None]
    keyvalue_row_index = jnp.take(attention_lower, clamped_scores[1], axis=0) * alive_flags[1][:, None]
    query_heavy = rounded(elementwise_product(query_row_index, heavy_query))
    raw_keyval = low_back(elementwise_product(keyvalue_row_index, heavy_keyval))
    keys_heavy = rounded(raw_keyval[:, :HD])
    values_heavy = rounded(score_keyval[:, None] * raw_keyval[:, HD:])
    heavy_attended = low_back(heavy_attention(query_heavy, keys_heavy, values_heavy, token_positions[0], token_positions[1], bounds))
    heavy_rescaled = low(score_query[:, None] * heavy_attended)
    heavy_token_rows = low_back(elementwise_product(heavy_rescaled, heavy_output_weight)) * alive_flags[0][:, None]
    residual = residual + jnp.zeros_like(inputs).at[clamped_scores[0]].add(heavy_token_rows)
    normed_feed = rms_norm(residual, feedforward_gain)
    feedforward_lower = low(normed_feed)
    pair_light = low_back(elementwise_product(feedforward_lower, light_expand))
    gated_light = low(gated_gelu(pair_light))
    feedforward_router_scores = jax.nn.sigmoid(jnp.take(elementwise_product(normed_feed, router[2]), clamped_scores[2]))
    feedforward_row_index = jnp.take(feedforward_lower, clamped_scores[2], axis=0) * alive_flags[2][:, None]
    pair_heavy = low_back(elementwise_product(feedforward_row_index, heavy_expand))
    gated_heavy = low(gated_gelu(pair_heavy))
    unnormed_feedforward = low_back(elementwise_product(gated_heavy, heavy_reduce))
    feedforward_rows = (feedforward_router_scores * alive_flags[2])[:, None] * unnormed_feedforward
    return residual + elementwise_product(gated_light, light_reduce) + jnp.zeros_like(inputs).at[clamped_scores[2]].add(feedforward_rows)

def reference(tokens, cotangent, document_bounds, routes, attention_gain, feedforward_gain, router, light_query, light_keyval, light_output, heavy_query, heavy_keyval, heavy_output_weight, light_expand, light_reduce, heavy_expand, heavy_reduce):
    slot_count = ROUTE_SLOTS * N_SEQ
    checked = jax.checkpoint(group_forward)

    def forward(inputs, *weights):
        pieces = []
        for group_index in range(GROUPS):
            pieces.append(checked(inputs[group_index * SEQ_TOK:(group_index + 1) * SEQ_TOK], document_bounds[group_index], routes[:, group_index * slot_count:(group_index + 1) * slot_count], *weights))
        return jnp.concatenate(pieces, 0)
    floats = [tokens.astype(jnp.float32), attention_gain.astype(jnp.float32), feedforward_gain.astype(jnp.float32), router.astype(jnp.float32)]
    floats = floats + [matrix.astype(jnp.float32) for matrix in (light_query, light_keyval, light_output, heavy_query, heavy_keyval, heavy_output_weight, light_expand, light_reduce, heavy_expand, heavy_reduce)]
    result, backward = jax.vjp(forward, *floats)
    gradients = backward(cotangent.astype(jnp.float32))
    return (result.astype(jnp.bfloat16), gradients[0].astype(jnp.bfloat16), gradients[1], gradients[2], gradients[3], gradients[4], gradients[5], gradients[6], gradients[7], gradients[8], gradients[9], gradients[10], gradients[11], gradients[12], gradients[13])
```

```python
import jax
import jax.numpy as jnp
from jax import lax
from jax.sharding import PartitionSpec as P

LH = 8
HHS = 64
WINDOW = 128


EPSILON = 1e-06
MASKED = -1e30
HIGHEST = lax.Precision.HIGHEST


def with_halo(cells, sides, width):
    for axis, dim in sides:
        count = lax.axis_size(axis)
        ends = count - 1
        head = lax.slice_in_dim(cells, 0, width, axis=dim)
        tail = lax.slice_in_dim(cells, cells.shape[dim] - width, cells.shape[dim], axis=dim)
        cells = jnp.concatenate(
            [
                lax.ppermute(tail, axis, [(i, (i + 1) % count) for i in range(ends)]),
                cells,
                lax.ppermute(head, axis, [((i + 1) % count, i) for i in range(ends)]),
            ],
            axis=dim,
        )
    return cells


def from_behind(block, axis, distance):
    devices = range(lax.axis_size(axis))
    route = [(i - distance, i) for i in devices if i - distance in devices]
    return lax.ppermute(block, axis, route)


def rms_norm(signal, scaling):
    return signal * lax.rsqrt(jnp.mean(signal * signal, -1, keepdims=True) + EPSILON) * scaling


def gated_gelu(paired):
    halfway = paired.shape[-1] // 2
    return jax.nn.gelu(paired[:, :halfway]) * paired[:, halfway:]


def segment_of(token_positions, bounds):
    return (token_positions >= bounds[0]).astype(jnp.int32) + (token_positions >= bounds[1]).astype(
        jnp.int32
    )


def matmul(former, latter):
    return jnp.dot(former, latter, preferred_element_type=jnp.float32)


def matmul_left(former, latter):
    return lax.dot_general(
        former, latter, (((0,), (0,)), ((), ())), preferred_element_type=jnp.float32
    )


def matmul_right(former, latter):
    return lax.dot_general(
        former, latter, (((1,), (1,)), ((), ())), preferred_element_type=jnp.float32
    )


def scatter_rows(chosen_row, slot_rows):
    return lax.dot_general(
        chosen_row.astype(jnp.float32), slot_rows, (((0,), (0,)), ((), ())), precision=HIGHEST
    )


def pick_values(chosen_row, token_values):
    return jnp.sum(jnp.where(chosen_row, token_values[None, :], 0.0), 1)


def pick_back(chosen_row, slot_values):
    return jnp.sum(jnp.where(chosen_row, slot_values[:, None], 0.0), 0)


def light_scores(queries, padded, offset, rows_block, leading_position, length, bounds):
    model_width = queries.shape[1]
    head_size = model_width // LH
    window_span = rows_block + 2 * WINDOW
    query_part = queries.reshape(rows_block, LH, head_size)
    key_part = padded[:, :model_width].reshape(window_span, LH, head_size)
    value_part = padded[:, model_width:].reshape(window_span, LH, head_size)
    scores = jnp.einsum(
        "qhd,khd->hqk", query_part, key_part, preferred_element_type=jnp.float32
    ) * head_size ** (-0.5)
    query_place = leading_position + offset + jnp.arange(rows_block, dtype=jnp.int32)
    key_place = leading_position + offset - WINDOW + jnp.arange(window_span, dtype=jnp.int32)
    allowed = (key_place[None, :] >= 0) & (key_place[None, :] < length)
    allowed = allowed & (jnp.abs(query_place[:, None] - key_place[None, :]) <= WINDOW)
    allowed = allowed & (
        segment_of(query_place, bounds)[:, None] == segment_of(key_place, bounds)[None, :]
    )
    return (scores, allowed, query_part, key_part, value_part)


def light_softmax(scores, allowed):
    masked = jnp.where(allowed[None], scores, MASKED)
    row_peak = jnp.max(masked, -1, keepdims=True)
    exponent = jnp.exp(masked - row_peak)
    row_total = jnp.sum(exponent, -1, keepdims=True)
    return (exponent / row_total, row_peak, row_total)


def heavy_softmax(scores, allowed):
    masked = jnp.where(allowed[None], scores, MASKED)
    row_peak = jnp.max(masked, -1, keepdims=True)
    exponent = jnp.where(allowed[None], jnp.exp(masked - row_peak), 0.0)
    row_total = jnp.sum(exponent, -1, keepdims=True)
    row_guard = jnp.where(row_total > 0, row_total, 1.0)
    return (exponent / row_guard, row_peak, row_guard)


def heavy_weights(scores, allowed, row_peak, row_guard):
    masked = jnp.where(allowed[None], scores, MASKED)
    return jnp.where(allowed[None], jnp.exp(masked - row_peak), 0.0) / row_guard


def head_slices(queries, keyvals, group_index, group_cols, heavy_width):
    column = group_index * group_cols
    heads_here = group_cols // HHS
    query_group = queries[:, column : column + group_cols].reshape(
        queries.shape[0], heads_here, HHS
    )
    key_group = keyvals[:, column : column + group_cols].reshape(keyvals.shape[0], heads_here, HHS)
    value_group = keyvals[:, heavy_width + column : heavy_width + column + group_cols].reshape(
        keyvals.shape[0], heads_here, HHS
    )
    return (query_group, key_group, value_group)


def softmax_back(weights, grad_part, value_part):
    grad_weights = jnp.einsum(
        "qhd,khd->hqk", grad_part, value_part, preferred_element_type=jnp.float32
    )
    inner = jnp.sum(weights * grad_weights, -1, keepdims=True)
    return ((weights * (grad_weights - inner)).astype(jnp.bfloat16), inner)


def stages(count):
    found, stride = [], 1
    while count > 1:
        size = 4 if count % 4 == 0 and count != 8 else 2
        found.append((size, stride))
        stride, count = stride * size, count // size
    return found


def shifted(block, axis, size, stride, step):
    count = lax.axis_size(axis)
    route = []
    for i in range(count):
        member = (i // stride) % size
        route.append((i, i + ((member + step) % size - member) * stride))
    return lax.ppermute(block, axis, route)


def member_of(axis, size, stride):
    return (lax.axis_index(axis) // stride) % size


def pick(block, index, dim):
    return lax.dynamic_index_in_dim(block, index, dim, keepdims=False)


def reduce_stage(block, axis, size, stride, dim):
    me = member_of(axis, size, stride)
    total = pick(block, me, dim).astype(jnp.float32)
    for step in range(1, size):
        sent = pick(block, (me + step) % size, dim).astype(jnp.bfloat16)
        total = total + shifted(sent, axis, size, stride, step).astype(jnp.float32)
    return total


def reduce_dp(block):
    rows, columns = block.shape[1:]
    block = reduce_stage(block.reshape(2, 2, rows, columns), "dp", 2, 1, 1)
    return reduce_stage(block, "dp", 2, 2, 0)


def reduce_seq(block, skip=0):
    for size, stride in stages(lax.axis_size("seq"))[skip:]:
        count = lax.axis_size("seq") // stride
        block = block.reshape(count // size, size, block.shape[0] // count, block.shape[1])
        block = reduce_stage(block, "seq", size, stride, 1)
        block = block.reshape(-1, block.shape[-1])
    return block


def gather_seq(block):
    for size, stride in stages(lax.axis_size("seq")):
        block = jnp.concatenate(
            [block] + [shifted(block, "seq", size, stride, step) for step in range(1, size)], 0
        )
    return block


def gather_dp(former, latter):
    rows, columns = latter.shape
    latter = latter.reshape(rows, 2, 2, columns // 4)
    core, x = member_of("dp", 2, 1), member_of("dp", 2, 2)
    mine = pick(latter, core, 2)
    other = pick(latter, 1 - core, 2).reshape(rows, columns // 2)
    got = shifted(jnp.concatenate([former, other], 1), "dp", 2, 1, 1)
    width = former.shape[1]
    former = jnp.concatenate([former, got[:, :width]], 0)
    latter = jnp.concatenate([mine, got[:, width:].reshape(rows, 2, columns // 4)], 0)
    mine, other = pick(latter, x, 1), pick(latter, 1 - x, 1)
    got = shifted(jnp.concatenate([former, other], 1), "dp", 2, 2, 1)
    former = jnp.concatenate([former, got[:, :width]], 0)
    latter = jnp.concatenate([mine, got[:, width:]], 0)
    return former, latter


def quarters(former, latter):
    parts = latter.reshape(latter.shape[0], 4, latter.shape[1] // 4)
    return jnp.stack([matmul_left(former, parts[:, i]) for i in range(4)]).astype(jnp.bfloat16)


def light_gradient(former, latter):
    return reduce_seq(reduce_dp(quarters(former, latter)))


def heavy_gradient(former, latter):
    former, latter = gather_dp(former, latter)
    return reduce_seq(matmul_left(former, latter))


def expand_gradient(former, latter):
    former, latter = gather_dp(former, latter)
    rows, width = former.shape
    size, stride = stages(lax.axis_size("seq"))[0]
    count = lax.axis_size("seq")
    former = former.reshape(rows, count // size, size, width // count)
    me = member_of("seq", size, stride)
    formers, latters = [pick(former, me, 2).reshape(rows, width // size)], [latter]
    for step in range(1, size):
        other = pick(former, (me + step) % size, 2).reshape(rows, width // size)
        got = shifted(jnp.concatenate([other, latter], 1), "seq", size, stride, step)
        formers.append(got[:, : width // size])
        latters.append(got[:, width // size :])
    product = matmul_left(jnp.concatenate(formers, 0), jnp.concatenate(latters, 0))
    return reduce_seq(product, 1)


def reduce_gradient(former, latter):
    for size, stride in stages(lax.axis_size("seq")):
        rows, width = former.shape
        count = lax.axis_size("seq") // stride
        former = former.reshape(rows, count // size, size, width // count)
        me = member_of("seq", size, stride)
        formers, latters = [pick(former, me, 2).reshape(rows, width // size)], [latter]
        for step in range(1, size):
            other = pick(former, (me + step) % size, 2).reshape(rows, width // size)
            got = shifted(jnp.concatenate([other, latter], 1), "seq", size, stride, step)
            formers.append(got[:, : width // size])
            latters.append(got[:, width // size :])
        former, latter = jnp.concatenate(formers, 0), jnp.concatenate(latters, 0)
    return reduce_dp(quarters(former, latter))


def reduce_small(block):
    for stride in (1, 2):
        block = block + shifted(block, "dp", 2, stride, 1)
    for size, stride in stages(lax.axis_size("seq")):
        count = lax.axis_size("seq") // stride
        block = block.reshape(block.shape[0], count // size, size, block.shape[1] // count)
        me = member_of("seq", size, stride)
        total = pick(block, me, 2)
        for step in range(1, size):
            total = total + shifted(pick(block, (me + step) % size, 2), "seq", size, stride, step)
        block = total.reshape(total.shape[0], -1)
    return block


def high_low(values):
    high = lax.reduce_precision(values, 8, 7)
    return high.astype(jnp.bfloat16), (values - high).astype(jnp.bfloat16)


def on_device(
    tokens,
    cotangent,
    document_bounds,
    routes,
    attention_gain,
    feedforward_gain,
    router,
    light_query,
    light_keyval,
    light_output,
    heavy_query,
    heavy_keyval,
    heavy_output_weight,
    light_expand,
    light_reduce,
    heavy_expand,
    heavy_reduce,
):
    tok_rows, model_width = tokens.shape
    slot_rows = routes.shape[1]
    heavy_width = heavy_query.shape[1]
    leading_position = lax.axis_index("seq") * tok_rows
    length = tok_rows * lax.axis_size("seq")
    bounds = lax.dynamic_index_in_dim(document_bounds, lax.axis_index("dp"), 0, keepdims=False)
    rows_block = min(512, tok_rows)
    window_span = rows_block + 2 * WINDOW
    light_size = model_width // LH
    group_cols = 4 * HHS
    heads_here = group_cols // HHS
    head_groups = heavy_width // group_cols
    heavy_scale = HHS ** (-0.5)
    inputs = tokens.astype(jnp.float32)
    normed_mixer = rms_norm(inputs, attention_gain)
    attention_lower = normed_mixer.astype(jnp.bfloat16)
    query_light = matmul(attention_lower, light_query).astype(jnp.bfloat16)
    keyval_light = matmul(attention_lower, light_keyval).astype(jnp.bfloat16)
    padded = with_halo(keyval_light, (("seq", 0),), WINDOW)
    offset = 0
    scores, allowed, query_part, key_part, value_part = light_scores(
        query_light, padded, offset, rows_block, leading_position, length, bounds
    )
    weights, row_peak, row_total = light_softmax(scores, allowed)
    light_parts = jnp.einsum(
        "hqk,khd->qhd", weights.astype(jnp.bfloat16), value_part, preferred_element_type=jnp.float32
    ).reshape(rows_block, model_width)
    light_stats = [(row_peak, row_total)]
    attended = light_parts.astype(jnp.bfloat16)
    residual = inputs + matmul(attended, light_output)
    alive_flags = routes >= 0
    lanes = jnp.arange(tok_rows, dtype=jnp.int32)
    chosen = routes[:, :, None] == lanes[None, None, :]
    chosen_low = chosen.astype(jnp.bfloat16)
    score_query = jax.nn.sigmoid(
        pick_values(chosen[0], jnp.dot(normed_mixer, router[0], precision=HIGHEST))
    )
    score_keyval = jax.nn.sigmoid(
        pick_values(chosen[1], jnp.dot(normed_mixer, router[1], precision=HIGHEST))
    )
    query_row_index = matmul(chosen_low[0], attention_lower).astype(jnp.bfloat16)
    keyvalue_row_index = matmul(chosen_low[1], attention_lower).astype(jnp.bfloat16)
    query_heavy = matmul(query_row_index, heavy_query).astype(jnp.bfloat16)
    raw_keyval = matmul(keyvalue_row_index, heavy_keyval)
    keyval_heavy = jnp.concatenate(
        [raw_keyval[:, :heavy_width], score_keyval[:, None] * raw_keyval[:, heavy_width:]], 1
    ).astype(jnp.bfloat16)
    slot_token_positions = jnp.where(alive_flags, leading_position + routes, -1)
    key_segment = jnp.where(alive_flags[1], segment_of(slot_token_positions[1], bounds), -1)
    tag = jnp.pad(key_segment[:, None].astype(jnp.bfloat16), ((0, 0), (0, 127)))
    gathered = gather_seq(jnp.concatenate([keyval_heavy, tag], 1))
    gathered_keyval = gathered[:, : 2 * heavy_width]
    gathered_segment = gathered[:, 2 * heavy_width].astype(jnp.int32)
    query_segment = segment_of(slot_token_positions[0], bounds)
    heavy_allowed = query_segment[:, None] == gathered_segment[None, :]
    heavy_parts = []
    heavy_stats = []
    for group_index in range(head_groups):
        query_group, key_group, value_group = head_slices(
            query_heavy, gathered_keyval, group_index, group_cols, heavy_width
        )
        scores = (
            jnp.einsum("qhd,khd->hqk", query_group, key_group, preferred_element_type=jnp.float32)
            * heavy_scale
        )
        weights, row_peak, row_guard = heavy_softmax(scores, heavy_allowed)
        heavy_parts.append(
            jnp.einsum(
                "hqk,khd->qhd",
                weights.astype(jnp.bfloat16),
                value_group,
                preferred_element_type=jnp.float32,
            ).reshape(slot_rows, group_cols)
        )
        heavy_stats.append((row_peak, row_guard))
    heavy_attended = jnp.concatenate(heavy_parts, 1)
    heavy_rescaled = (score_query[:, None] * heavy_attended).astype(jnp.bfloat16)
    residual = residual + scatter_rows(chosen[0], matmul(heavy_rescaled, heavy_output_weight))
    normed_feed = rms_norm(residual, feedforward_gain)
    feedforward_lower = normed_feed.astype(jnp.bfloat16)
    pair_light = matmul(feedforward_lower, light_expand)
    gated_light = gated_gelu(pair_light).astype(jnp.bfloat16)
    feedforward_router_scores = jax.nn.sigmoid(
        pick_values(chosen[2], jnp.dot(normed_feed, router[2], precision=HIGHEST))
    )
    feedforward_row_index = matmul(chosen_low[2], feedforward_lower).astype(jnp.bfloat16)
    pair_heavy = matmul(feedforward_row_index, heavy_expand)
    gated_heavy = gated_gelu(pair_heavy).astype(jnp.bfloat16)
    unnormed_feedforward = matmul(gated_heavy, heavy_reduce)
    output = (
        residual
        + matmul(gated_light, light_reduce)
        + scatter_rows(chosen[2], feedforward_router_scores[:, None] * unnormed_feedforward)
    ).astype(jnp.bfloat16)
    grad_gated_light = matmul_right(cotangent, light_reduce)
    grad_light_reduce = light_gradient(gated_light, cotangent)
    grad_pair_light = jax.vjp(gated_gelu, pair_light)[1](grad_gated_light)[0].astype(jnp.bfloat16)
    grad_light_expand = light_gradient(feedforward_lower, grad_pair_light)
    grad_feed = matmul_right(grad_pair_light, light_expand)
    grad_feed_rows = matmul(chosen_low[2], cotangent)
    grad_score_feed = jnp.sum(grad_feed_rows * unnormed_feedforward, 1)
    grad_raw_feed = (feedforward_router_scores[:, None] * grad_feed_rows).astype(jnp.bfloat16)
    grad_heavy_reduce = reduce_gradient(gated_heavy, grad_raw_feed)
    grad_gated_heavy = matmul_right(grad_raw_feed, heavy_reduce)
    grad_pair_heavy = jax.vjp(gated_gelu, pair_heavy)[1](grad_gated_heavy)[0].astype(jnp.bfloat16)
    grad_heavy_expand = expand_gradient(feedforward_row_index, grad_pair_heavy)
    grad_feed = grad_feed + scatter_rows(chosen[2], matmul_right(grad_pair_heavy, heavy_expand))
    token_logit_feed = pick_back(
        chosen[2], grad_score_feed * feedforward_router_scores * (1.0 - feedforward_router_scores)
    )
    grad_feed = grad_feed + token_logit_feed[:, None] * router[2][None, :]
    router_feed = jnp.dot(token_logit_feed, normed_feed, precision=HIGHEST)
    grad_residual_norm, grad_feed_gain = jax.vjp(rms_norm, residual, feedforward_gain)[1](grad_feed)
    grad_residual = cotangent.astype(jnp.float32) + grad_residual_norm
    grad_residual_low = grad_residual.astype(jnp.bfloat16)
    grad_light_output = light_gradient(attended, grad_residual_low)
    grad_attended = matmul_right(grad_residual_low, light_output).astype(jnp.bfloat16)
    grad_heavy_rows = matmul(chosen_low[0], grad_residual_low).astype(jnp.bfloat16)
    grad_heavy_output = heavy_gradient(heavy_rescaled, grad_heavy_rows)
    grad_scaled = matmul_right(grad_heavy_rows, heavy_output_weight)
    grad_score_query = jnp.sum(grad_scaled * heavy_attended, 1)
    grad_heavy_attended = (score_query[:, None] * grad_scaled).astype(jnp.bfloat16)
    query_parts = []
    inner_parts = []
    for group_index in range(head_groups):
        query_group, key_group, value_group = head_slices(
            query_heavy, gathered_keyval, group_index, group_cols, heavy_width
        )
        row_peak, row_guard = heavy_stats[group_index]
        scores = (
            jnp.einsum("qhd,khd->hqk", query_group, key_group, preferred_element_type=jnp.float32)
            * heavy_scale
        )
        weights = heavy_weights(scores, heavy_allowed, row_peak, row_guard)
        grad_group = grad_heavy_attended[
            :, group_index * group_cols : (group_index + 1) * group_cols
        ].reshape(slot_rows, heads_here, HHS)
        grad_scores, inner = softmax_back(weights, grad_group, value_group)
        query_parts.append(
            (
                jnp.einsum(
                    "hqk,khd->qhd", grad_scores, key_group, preferred_element_type=jnp.float32
                )
                * heavy_scale
            ).reshape(slot_rows, group_cols)
        )
        inner_parts.append(inner)
    stats = []
    for group_index in range(head_groups):
        row_peak, row_guard = heavy_stats[group_index]
        stats.append((row_peak + jnp.log(row_guard))[:, :, 0].T)
    for group_index in range(head_groups):
        stats.append(inner_parts[group_index][:, :, 0].T)
    stat_high, stat_low = high_low(jnp.concatenate(stats, 1))
    heads = heavy_width // HHS
    packet = jnp.concatenate(
        [
            query_heavy,
            grad_heavy_attended,
            stat_high,
            stat_low,
            query_segment[:, None].astype(jnp.bfloat16),
            jnp.zeros((slot_rows, 127 - 4 * heads), jnp.bfloat16),
        ],
        1,
    )
    packet = gather_seq(packet)
    every_query = packet[:, :heavy_width].reshape(-1, heads, HHS)
    every_grad = packet[:, heavy_width : 2 * heavy_width].reshape(-1, heads, HHS)
    column = 2 * heavy_width
    every_stat = packet[:, column : column + 2 * heads].astype(jnp.float32) + packet[
        :, column + 2 * heads : column + 4 * heads
    ].astype(jnp.float32)
    every_segment = packet[:, column + 4 * heads].astype(jnp.int32)
    own_key = keyval_heavy[:, :heavy_width].reshape(slot_rows, heads, HHS)
    own_value = keyval_heavy[:, heavy_width:].reshape(slot_rows, heads, HHS)
    own_allowed = every_segment[:, None] == key_segment[None, :]
    scores = (
        jnp.einsum("qhd,khd->hqk", every_query, own_key, preferred_element_type=jnp.float32)
        * heavy_scale
    )
    weights = jnp.where(
        own_allowed[None], jnp.exp(jnp.where(own_allowed[None], scores - every_stat[:, :heads].T[:, :, None], 0.0)), 0.0
    )
    grad_weights = jnp.einsum(
        "qhd,khd->hqk", every_grad, own_value, preferred_element_type=jnp.float32
    )
    grad_scores = (weights * (grad_weights - every_stat[:, heads:].T[:, :, None])).astype(jnp.bfloat16)
    key_grads = jnp.concatenate(
        [
            (
                jnp.einsum(
                    "hqk,qhd->khd", grad_scores, every_query, preferred_element_type=jnp.float32
                )
                * heavy_scale
            ).reshape(slot_rows, heavy_width),
            jnp.einsum(
                "hqk,qhd->khd",
                weights.astype(jnp.bfloat16),
                every_grad,
                preferred_element_type=jnp.float32,
            ).reshape(slot_rows, heavy_width),
        ],
        1,
    )
    grad_keys = key_grads[:, :heavy_width].astype(jnp.bfloat16)
    grad_values = key_grads[:, heavy_width:].astype(jnp.bfloat16)
    grad_score_keyval = jnp.sum(grad_values.astype(jnp.float32) * raw_keyval[:, heavy_width:], 1)
    grad_raw_keyval = jnp.concatenate(
        [grad_keys, (score_keyval[:, None] * grad_values.astype(jnp.float32)).astype(jnp.bfloat16)],
        1,
    )
    grad_heavy_keyval = heavy_gradient(keyvalue_row_index, grad_raw_keyval)
    grad_query_heavy = jnp.concatenate(query_parts, 1).astype(jnp.bfloat16)
    grad_heavy_query = heavy_gradient(query_row_index, grad_query_heavy)
    grad_mixer = scatter_rows(
        chosen[0], matmul_right(grad_query_heavy, heavy_query)
    ) + scatter_rows(chosen[1], matmul_right(grad_raw_keyval, heavy_keyval))
    grad_padded = jnp.zeros((tok_rows + 2 * WINDOW, 2 * model_width), jnp.float32)
    light_query_parts = []
    for block_index, offset in enumerate(range(0, tok_rows, rows_block)):
        scores, allowed, query_part, key_part, value_part = light_scores(
            query_light, padded, offset, rows_block, leading_position, length, bounds
        )
        row_peak, row_total = light_stats[block_index]
        weights = jnp.exp(jnp.where(allowed[None], scores, MASKED) - row_peak) / row_total
        grad_part = grad_attended.reshape(rows_block, LH, light_size)
        grad_scores, inner = softmax_back(weights, grad_part, value_part)
        light_query_parts.append(
            (
                jnp.einsum(
                    "hqk,khd->qhd", grad_scores, key_part, preferred_element_type=jnp.float32
                )
                * light_size ** (-0.5)
            ).reshape(rows_block, model_width)
        )
        key_grad = (
            jnp.einsum("hqk,qhd->khd", grad_scores, query_part, preferred_element_type=jnp.float32)
            * light_size ** (-0.5)
        ).reshape(window_span, model_width)
        value_grad = jnp.einsum(
            "hqk,qhd->khd",
            weights.astype(jnp.bfloat16),
            grad_part,
            preferred_element_type=jnp.float32,
        ).reshape(window_span, model_width)
        grad_padded = grad_padded.at[offset : offset + window_span].add(
            jnp.concatenate([key_grad, value_grad], 1)
        )
    from_above = from_behind(grad_padded[:WINDOW].astype(jnp.bfloat16), "seq", -1).astype(
        jnp.float32
    )
    from_below = from_behind(
        grad_padded[tok_rows + WINDOW :].astype(jnp.bfloat16), "seq", 1
    ).astype(jnp.float32)
    grad_keyval_light = grad_padded[WINDOW : WINDOW + tok_rows]
    grad_keyval_light = (
        grad_keyval_light.at[:WINDOW].add(from_below).at[tok_rows - WINDOW :].add(from_above)
    )
    grad_keyval_low = grad_keyval_light.astype(jnp.bfloat16)
    grad_query_low = light_query_parts[0].astype(jnp.bfloat16)
    grad_light_query = light_gradient(attention_lower, grad_query_low)
    grad_light_keyval = light_gradient(attention_lower, grad_keyval_low)
    grad_mixer = (
        grad_mixer
        + matmul_right(grad_query_low, light_query)
        + matmul_right(grad_keyval_low, light_keyval)
    )
    token_logit_query = pick_back(chosen[0], grad_score_query * score_query * (1.0 - score_query))
    token_logit_keyval = pick_back(
        chosen[1], grad_score_keyval * score_keyval * (1.0 - score_keyval)
    )
    grad_mixer = (
        grad_mixer
        + token_logit_query[:, None] * router[0][None, :]
        + token_logit_keyval[:, None] * router[1][None, :]
    )
    grad_router = jnp.stack(
        [
            jnp.dot(token_logit_query, normed_mixer, precision=HIGHEST),
            jnp.dot(token_logit_keyval, normed_mixer, precision=HIGHEST),
            router_feed,
        ]
    )
    grad_inputs_norm, grad_attention_gain = jax.vjp(rms_norm, inputs, attention_gain)[1](grad_mixer)
    grad_tokens = (grad_residual + grad_inputs_norm).astype(jnp.bfloat16)
    small = reduce_small(
        jnp.concatenate([grad_attention_gain[None], grad_feed_gain[None], grad_router], 0)
    )
    return (
        output,
        grad_tokens,
        small[0],
        small[1],
        small[2:],
        grad_light_query,
        grad_light_keyval,
        grad_light_output,
        grad_heavy_query,
        grad_heavy_keyval,
        grad_heavy_output,
        grad_light_expand,
        grad_light_reduce,
        grad_heavy_expand,
        grad_heavy_reduce,
    )


def solution(mesh):
    placed = (
        P(("dp", "seq"), None),
        P(("dp", "seq"), None),
        P(),
        P(None, ("dp", "seq")),
        P(),
        P(),
        P(),
        P(),
        P(),
        P(),
        P(),
        P(),
        P(),
        P(),
        P(),
        P(),
        P(),
    )
    return jax.shard_map(
        on_device,
        mesh=mesh,
        in_specs=placed,
        out_specs=(
            P(("dp", "seq"), None),
            P(("dp", "seq"), None),
            P("seq"),
            P("seq"),
            P(None, "seq"),
            P("seq", "dp"),
            P("seq", "dp"),
            P("seq", "dp"),
            P("seq", "dp"),
            P("seq", "dp"),
            P("seq", "dp"),
            P("seq", "dp"),
            P("seq", "dp"),
            P("seq", "dp"),
            P("seq", "dp"),
        ),
        check_vma=False,
    )
```

```python
import functools
import math

import jax
import jax.numpy as jnp
from jax import lax
from jax.experimental import pallas as pl
from jax.experimental.pallas import tpu as pltpu
from jax.sharding import PartitionSpec as P

LH = 8
HHS = 64
WINDOW = 128
EPSILON = 1e-06
MASKED = -1e30
HIGHEST = lax.Precision.HIGHEST
F32, BF16 = jnp.float32, jnp.bfloat16
MIB = 1 << 20


def dot(former, latter):
    return jnp.dot(former, latter, preferred_element_type=F32)


def dot_left(former, latter):
    return lax.dot_general(former, latter, (((0,), (0,)), ((), ())), preferred_element_type=F32)


def dot_right(former, latter):
    return lax.dot_general(former, latter, (((1,), (1,)), ((), ())), preferred_element_type=F32)


def dot_exact(former, latter):
    return jnp.dot(former, latter, preferred_element_type=F32, precision=HIGHEST)


def column_of(row):
    count = row.shape[1]
    same = lax.broadcasted_iota(jnp.int32, (count, count), 0) == lax.broadcasted_iota(
        jnp.int32, (count, count), 1
    )
    return jnp.sum(jnp.where(same, row.astype(F32), 0.0), axis=1, keepdims=True)


def slots_by_tokens(route_row, tokens):
    column = column_of(route_row).astype(jnp.int32)
    lanes = lax.broadcasted_iota(jnp.int32, (route_row.shape[1], tokens), 1)
    return (column == lanes).astype(F32)


def tokens_by_slots(route_row, tokens):
    rows = lax.broadcasted_iota(jnp.int32, (tokens, route_row.shape[1]), 0)
    return (rows == route_row).astype(F32)


def normed(rows, gain):
    return rows * lax.rsqrt(jnp.mean(rows * rows, -1, keepdims=True) + EPSILON) * gain


def norm_back(rows, gain, grad):
    inverse = lax.rsqrt(jnp.mean(rows * rows, -1, keepdims=True) + EPSILON)
    plain = rows * inverse
    scaled = grad * gain
    inner = jnp.mean(scaled * plain, -1, keepdims=True)
    return inverse * (scaled - plain * inner), jnp.sum(grad * plain, 0, keepdims=True)


def sigmoid(value):
    return 1.0 / (1.0 + jnp.exp(-value))


def segment(place, first, last):
    return (place >= first).astype(F32) + (place >= last).astype(F32)


def gelu_parts(value):
    slope = math.sqrt(2.0 / math.pi)
    square = value * value
    bent = jnp.tanh(slope * value * (1.0 + 0.044715 * square))
    half = 0.5 * (1.0 + bent)
    rise = half + 0.5 * value * (1.0 - bent * bent) * slope * (1.0 + 3 * 0.044715 * square)
    return value * half, rise


def place(tok_rows, bounds):
    lead = lax.axis_index("seq") * tok_rows
    group = lax.axis_index("dp")
    return lead, bounds[group, 0], bounds[group, 1]


def select_kernel(bounds, routes, tokens, packet):
    count, width = tokens.shape
    lead, first, last = place(count, bounds)
    row = routes[1:2, :]
    chosen = slots_by_tokens(row, count).astype(BF16)
    packet[:, :width] = dot(chosen, tokens[...]).astype(BF16)
    column = column_of(row)
    tag = jnp.where(column >= 0, segment(column.astype(jnp.int32) + lead, first, last), -1.0)
    packet[:, width:] = jnp.broadcast_to(tag, (tag.shape[0], 128)).astype(BF16)


def project_kernel(
    routes, tokens, gain, router, light_query, light_keyval, heavy_query,
    low, query, keyval, rows_query, rows_keyval, query_heavy, score_query,
):
    count = tokens.shape[0]
    low[...] = normed(tokens[...].astype(F32), gain[...]).astype(BF16)
    query[...] = dot(low[...], light_query[...]).astype(BF16)
    keyval[...] = dot(low[...], light_keyval[...]).astype(BF16)
    chosen = slots_by_tokens(routes[0:1, :], count).astype(BF16)
    raw = dot(chosen, tokens[...])
    rows = normed(raw, gain[...])
    logit = jnp.sum(rows * router[0:1, :], -1, keepdims=True)
    score_query[...] = jnp.broadcast_to(sigmoid(logit), score_query.shape)
    rows_query[...] = dot(chosen, low[...]).astype(BF16)
    query_heavy[...] = dot(rows_query[...], heavy_query[...]).astype(BF16)
    chosen = slots_by_tokens(routes[1:2, :], count).astype(BF16)
    rows_keyval[...] = dot(chosen, low[...]).astype(BF16)


def light_mask(tok_rows, length, bounds, step):
    lead, first, last = place(tok_rows, bounds)
    query_place = lead + step * WINDOW + lax.broadcasted_iota(jnp.int32, (WINDOW, 3 * WINDOW), 0)
    key_place = (
        lead + (step - 1) * WINDOW + lax.broadcasted_iota(jnp.int32, (WINDOW, 3 * WINDOW), 1)
    )
    allowed = (key_place >= 0) & (key_place < length)
    allowed = allowed & (jnp.abs(query_place - key_place) <= WINDOW)
    return allowed & (segment(query_place, first, last) == segment(key_place, first, last))


def light_forward_kernel(
    length, bounds, query, keyval, above, below, gain, light_keyval,
    attended, peaks, halo_low, halo_keyval, span,
):
    tok_rows, width = query.shape
    size = width // LH
    halo_low[:WINDOW] = normed(above[...].astype(F32), gain[...]).astype(BF16)
    halo_low[WINDOW:] = normed(below[...].astype(F32), gain[...]).astype(BF16)
    halo_keyval[...] = dot(halo_low[...], light_keyval[...]).astype(BF16)
    span[:WINDOW] = halo_keyval[:WINDOW]
    span[WINDOW : WINDOW + tok_rows] = keyval[...]
    span[WINDOW + tok_rows :] = halo_keyval[WINDOW:]
    lanes = lax.broadcasted_iota(jnp.int32, (WINDOW, 128), 1)
    for step in range(tok_rows // WINDOW):
        rows = slice(step * WINDOW, (step + 1) * WINDOW)
        keys = slice(step * WINDOW, (step + 3) * WINDOW)
        allowed = light_mask(tok_rows, length, bounds, step)
        kept = jnp.zeros((WINDOW, 128), F32)
        for head in range(LH):
            columns = slice(head * size, (head + 1) * size)
            values = slice(width + head * size, width + (head + 1) * size)
            scores = dot_right(query[rows, columns], span[keys, columns]) * size ** (-0.5)
            scores = jnp.where(allowed, scores, MASKED)
            peak = jnp.max(scores, -1, keepdims=True)
            exponent = jnp.exp(scores - peak)
            total = jnp.sum(exponent, -1, keepdims=True)
            weights = (exponent * (1.0 / total)).astype(BF16)
            attended[rows, columns] = dot(weights, span[keys, values]).astype(BF16)
            kept = jnp.where(lanes == head, peak + jnp.log(total), kept)
        peaks[rows, :] = kept


def light_backward_kernel(
    length, bounds, query, keyval, halo_keyval, low, halo_low, peaks, grad, attended, grad_residual,
    grad_query, grad_own, grad_above, grad_below, products, span, grad_span,
):
    tok_rows, width = query.shape
    size = width // LH
    span[:WINDOW] = halo_keyval[:WINDOW]
    span[WINDOW : WINDOW + tok_rows] = keyval[...]
    span[WINDOW + tok_rows :] = halo_keyval[WINDOW:]
    grad_span[...] = jnp.zeros_like(grad_span)
    lanes = lax.broadcasted_iota(jnp.int32, (WINDOW, 128), 1)
    for step in range(tok_rows // WINDOW):
        rows = slice(step * WINDOW, (step + 1) * WINDOW)
        keys = slice(step * WINDOW, (step + 3) * WINDOW)
        allowed = light_mask(tok_rows, length, bounds, step)
        kept = peaks[rows, :]
        for head in range(LH):
            columns = slice(head * size, (head + 1) * size)
            values = slice(width + head * size, width + (head + 1) * size)
            scores = dot_right(query[rows, columns], span[keys, columns]) * size ** (-0.5)
            peak = jnp.sum(jnp.where(lanes == head, kept, 0.0), -1, keepdims=True)
            weights = jnp.exp(jnp.where(allowed, scores, MASKED) - peak)
            grad_weights = dot_right(grad[rows, columns], span[keys, values])
            inner = jnp.sum(weights * grad_weights, -1, keepdims=True)
            grad_scores = (weights * (grad_weights - inner)).astype(BF16)
            grad_query[rows, columns] = (
                dot(grad_scores, span[keys, columns]) * size ** (-0.5)
            ).astype(BF16)
            grad_span[keys, columns] += dot_left(grad_scores, query[rows, columns]) * size ** (-0.5)
            grad_span[keys, values] += dot_left(weights.astype(BF16), grad[rows, columns])
    grad_own[...] = grad_span[WINDOW : WINDOW + tok_rows]
    grad_above[...] = grad_span[:WINDOW].astype(BF16)
    grad_below[...] = grad_span[WINDOW + tok_rows :].astype(BF16)
    span[...] = grad_span[...].astype(BF16)
    own = low[...]
    quarter = width // 4
    for part in range(4):
        core, base = part % 2, (part // 2) * width
        columns = slice(part * quarter, (part + 1) * quarter)
        pairs = slice(2 * part * quarter, 2 * (part + 1) * quarter)
        product = dot_left(own, span[WINDOW : WINDOW + tok_rows, pairs])
        product += dot_left(halo_low[:WINDOW], span[:WINDOW, pairs])
        product += dot_left(halo_low[WINDOW:], span[WINDOW + tok_rows :, pairs])
        products[core, :, base : base + 2 * quarter] = product.astype(BF16)
        product = dot_left(own, grad_query[:, columns])
        products[core, :, base + 2 * quarter : base + 3 * quarter] = product.astype(BF16)
        product = dot_left(attended[...], grad_residual[:, columns])
        products[core, :, base + 3 * quarter : base + 4 * quarter] = product.astype(BF16)


def heavy_forward_kernel(
    count, bounds, routes, gathered, query_heavy, score_query, gain, router, heavy_keyval,
    keyval, attended, scaled, peaks, own_values, score_keyval,
):
    width = query_heavy.shape[1]
    slots = query_heavy.shape[0]
    total_rows = gathered.shape[0]
    part = min(512, total_rows)
    for start in range(0, total_rows, part):
        rows = slice(start, start + part)
        signal = normed(gathered[rows, :width].astype(F32), gain[...])
        logit = jnp.sum(signal * router[1:2, :], -1, keepdims=True)
        score = sigmoid(logit)
        raw = dot(signal.astype(BF16), heavy_keyval[...])
        keyval[rows, :width] = raw[:, :width].astype(BF16)
        keyval[rows, width:] = (score * raw[:, width:]).astype(BF16)
        if start == 0:
            own_values[...] = raw[:slots, width:]
            score_keyval[...] = jnp.broadcast_to(score[:slots], score_keyval.shape)
    allowed = heavy_mask(count, bounds, routes, gathered, width)
    lanes = lax.broadcasted_iota(jnp.int32, (slots, 128), 1)
    kept = jnp.zeros((slots, 128), F32)
    for head in range(width // HHS):
        columns = slice(head * HHS, (head + 1) * HHS)
        values = slice(width + head * HHS, width + (head + 1) * HHS)
        scores = dot_right(query_heavy[:, columns], keyval[:, columns]) * HHS ** (-0.5)
        scores = jnp.where(allowed, scores, MASKED)
        peak = jnp.max(scores, -1, keepdims=True)
        exponent = jnp.where(allowed, jnp.exp(scores - peak), 0.0)
        total = jnp.sum(exponent, -1, keepdims=True)
        total = jnp.where(total > 0, total, 1.0)
        weights = (exponent * (1.0 / total)).astype(BF16)
        result = dot(weights, keyval[:, values])
        attended[:, columns] = result
        scaled[:, columns] = (score_query[:, :1] * result).astype(BF16)
        kept = jnp.where(lanes == head, peak + jnp.log(total), kept)
    peaks[...] = kept


def heavy_mask(count, bounds, routes, gathered, width):
    lead, first, last = place(count, bounds)
    pickers = (lax.broadcasted_iota(jnp.int32, (8, 128), 1) == 0).astype(BF16)
    key_segment = dot_right(pickers, gathered[:, width:])[:1]
    return own_segment(routes, lead, first, last) == key_segment


def own_segment(routes, lead, first, last):
    column = column_of(routes[0:1, :])
    spot = jnp.where(column >= 0, column.astype(jnp.int32) + lead, -1)
    return segment(spot, first, last)


def residual_kernel(
    routes, tokens, attended, light_output, scaled, heavy_output, gain, router, cotangent,
    residual, low, rows_feed, score_feed, cotangent_rows, grad_raw,
):
    count = tokens.shape[0]
    spread = tokens_by_slots(routes[0:1, :], count).astype(BF16)
    scattered = dot(spread, scaled[...]).astype(BF16)
    residual[...] = (
        tokens[...].astype(F32)
        + dot(attended[...], light_output[...])
        + dot(scattered, heavy_output[...])
    )
    signal = normed(residual[...], gain[...])
    low[...] = signal.astype(BF16)
    logit = jnp.sum(signal * router[2:3, :], -1, keepdims=True)
    chosen = slots_by_tokens(routes[2:3, :], count)
    logit = dot_exact(chosen, jnp.broadcast_to(logit, (count, 128)))
    score = sigmoid(logit)
    score_feed[...] = score
    chosen = chosen.astype(BF16)
    rows_feed[...] = dot(chosen, low[...]).astype(BF16)
    rows = dot(chosen, cotangent[...])
    cotangent_rows[...] = rows
    grad_raw[...] = (score[:, :1] * rows).astype(BF16)


def heavy_feed_kernel(
    rows_feed, grad_raw, gate_weight, up_weight, reduce_weight,
    gated, grad_gate, grad_up, raw, grad_rows,
):
    @pl.when(pl.program_id(0) == 0)
    def _():
        raw[...] = jnp.zeros_like(raw)
        grad_rows[...] = jnp.zeros_like(grad_rows)

    gate = dot(rows_feed[...], gate_weight[...])
    up = dot(rows_feed[...], up_weight[...])
    bent, rise = gelu_parts(gate)
    gated_low = (bent * up).astype(BF16)
    gated[...] = gated_low
    raw[...] += dot(gated_low, reduce_weight[...])
    grad_gated = dot_right(grad_raw[...], reduce_weight[...])
    gate_low = (grad_gated * up * rise).astype(BF16)
    up_low = (grad_gated * bent).astype(BF16)
    grad_gate[...] = gate_low
    grad_up[...] = up_low
    grad_rows[...] += dot_right(gate_low, gate_weight[...]) + dot_right(up_low, up_weight[...])


def light_feed_kernel(
    low, cotangent, gate_weight, up_weight, reduce_weight,
    result, grad_low, expand_products, reduce_products, turned,
):
    @pl.when(pl.program_id(0) == 0)
    def _():
        result[...] = jnp.zeros_like(result)
        grad_low[...] = jnp.zeros_like(grad_low)
        quarter = cotangent.shape[1] // 4
        for part in range(4):
            spot = (part % 2) * 2 + part // 2
            turned[:, spot * quarter : (spot + 1) * quarter] = cotangent[
                :, part * quarter : (part + 1) * quarter
            ]

    gate = dot(low[...], gate_weight[...])
    up = dot(low[...], up_weight[...])
    bent, rise = gelu_parts(gate)
    gated_low = (bent * up).astype(BF16)
    result[...] += dot(gated_low, reduce_weight[...])
    grad_gated = dot_right(cotangent[...], reduce_weight[...])
    gate_low = (grad_gated * up * rise).astype(BF16)
    up_low = (grad_gated * bent).astype(BF16)
    grad_low[...] += dot_right(gate_low, gate_weight[...]) + dot_right(up_low, up_weight[...])
    hidden = gate_low.shape[1]
    expand_products[0, :, :hidden] = dot_left(low[...], gate_low).astype(BF16)
    expand_products[0, :, hidden:] = dot_left(low[...], up_low).astype(BF16)
    half = turned.shape[1] // 2
    product = dot_left(gated_low, turned[...]).astype(BF16)
    reduce_products[0] = product[:, :half]
    reduce_products[1] = product[:, half:]


def turn_kernel(
    routes, residual, gain, result, grad_low, raw, grad_rows, score_feed, cotangent_rows, cotangent,
    router, light_output, heavy_output, heavy_attended, score_query,
    output, grad_residual, grad_residual_low, grad_attended, grad_heavy_rows, grad_heavy_attended,
    logit_query, small,
):
    count = residual.shape[0]
    spread = tokens_by_slots(routes[2:3, :], count)
    score = score_feed[:, :1]
    output[...] = (
        residual[...] + result[...] + dot_exact(spread, score * raw[...])
    ).astype(BF16)
    logit = score * (1.0 - score) * jnp.sum(cotangent_rows[...] * raw[...], -1, keepdims=True)
    grad = grad_low[...] + dot_exact(spread, grad_rows[...] + logit * router[2:3, :])
    back, gain_grad = norm_back(residual[...], gain[...], grad)
    token_logit = dot_exact(spread, jnp.broadcast_to(logit, (logit.shape[0], 128)))[:, :1]
    signal = normed(residual[...], gain[...])
    small[0:1] = gain_grad
    small[1:2] = jnp.sum(token_logit * signal, 0, keepdims=True)
    total = cotangent[...].astype(F32) + back
    grad_residual[...] = total
    grad_residual_low[...] = total.astype(BF16)
    grad_attended[...] = dot_right(grad_residual_low[...], light_output[...]).astype(BF16)
    chosen = slots_by_tokens(routes[0:1, :], count).astype(BF16)
    grad_heavy_rows[...] = dot(chosen, grad_residual_low[...]).astype(BF16)
    scaled = dot_right(grad_heavy_rows[...], heavy_output[...])
    score = score_query[:, :1]
    logit = score * (1.0 - score) * jnp.sum(scaled * heavy_attended[...], -1, keepdims=True)
    logit_query[...] = jnp.broadcast_to(logit, logit_query.shape)
    grad_heavy_attended[...] = (score * scaled).astype(BF16)


def heavy_query_kernel(
    count, bounds, routes, gathered, query_heavy, keyval, peaks, grad, grad_query, packet
):
    slots, width = query_heavy.shape
    heads = width // HHS
    allowed = heavy_mask(count, bounds, routes, gathered, width)
    lanes = lax.broadcasted_iota(jnp.int32, (slots, 128), 1)
    kept = peaks[...]
    lead, first, last = place(count, bounds)
    tag = jnp.where(lanes == 4 * heads, own_segment(routes, lead, first, last), 0.0)
    for head in range(heads):
        columns = slice(head * HHS, (head + 1) * HHS)
        values = slice(width + head * HHS, width + (head + 1) * HHS)
        scores = dot_right(query_heavy[:, columns], keyval[:, columns]) * HHS ** (-0.5)
        peak = jnp.sum(jnp.where(lanes == head, kept, 0.0), -1, keepdims=True)
        weights = jnp.where(allowed, jnp.exp(scores - peak), 0.0)
        grad_weights = dot_right(grad[:, columns], keyval[:, values])
        inner = jnp.sum(weights * grad_weights, -1, keepdims=True)
        grad_scores = (weights * (grad_weights - inner)).astype(BF16)
        grad_query[:, columns] = (dot(grad_scores, keyval[:, columns]) * HHS ** (-0.5)).astype(BF16)
        for lane, value in ((head, peak), (heads + head, inner)):
            high = value.astype(BF16).astype(F32)
            tag = jnp.where(lanes == lane, high, tag)
            tag = jnp.where(lanes == 2 * heads + lane, value - high, tag)
    packet[:, :width] = query_heavy[...]
    packet[:, width : 2 * width] = grad[...]
    packet[:, 2 * width :] = tag.astype(BF16)


def heavy_key_kernel(
    count, bounds, routes, packets, keyval, own_values, score_keyval, grad_raw, logit_keyval
):
    slots = own_values.shape[0]
    width = own_values.shape[1]
    heads = width // HHS
    lead, first, last = place(count, bounds)
    column = column_of(routes[1:2, :])
    key_segment = jnp.where(
        column >= 0, segment(column.astype(jnp.int32) + lead, first, last), -1.0
    )
    same = lax.broadcasted_iota(jnp.int32, (128, 128), 0) == lax.broadcasted_iota(
        jnp.int32, (128, 128), 1
    )
    tags = dot_right(same.astype(BF16), packets[:, 2 * width :])
    allowed = key_segment == tags[4 * heads : 4 * heads + 1]
    score = score_keyval[:, :1]
    logit = jnp.zeros((slots, 1), F32)
    for head in range(heads):
        columns = slice(head * HHS, (head + 1) * HHS)
        values = slice(width + head * HHS, width + (head + 1) * HHS)
        peak = tags[head : head + 1] + tags[2 * heads + head : 2 * heads + head + 1]
        inner = tags[heads + head : heads + head + 1] + tags[3 * heads + head : 3 * heads + head + 1]
        scores = dot_right(keyval[:slots, columns], packets[:, columns]) * HHS ** (-0.5)
        weights = jnp.where(allowed, jnp.exp(scores - peak), 0.0)
        grad_weights = dot_right(keyval[:slots, values], packets[:, values])
        grad_scores = (weights * (grad_weights - inner)).astype(BF16)
        key_grad = dot(grad_scores, packets[:, columns]) * HHS ** (-0.5)
        value_grad = dot(weights.astype(BF16), packets[:, values]).astype(BF16).astype(F32)
        logit += jnp.sum(value_grad * own_values[:, columns], -1, keepdims=True)
        grad_raw[:, columns] = key_grad.astype(BF16)
        grad_raw[:, values] = (score * value_grad).astype(BF16)
    logit_keyval[...] = jnp.broadcast_to(score * (1.0 - score) * logit, logit_keyval.shape)


def mixer_kernel(
    routes, tokens, gain, router, grad_residual, grad_query, grad_own, from_below, from_above,
    grad_heavy_query, grad_raw_keyval, logit_query, logit_keyval, light_query, light_keyval,
    heavy_query, heavy_keyval, feed_small, tokens_grad, small, total_keyval,
):
    count = tokens.shape[0]
    total_keyval[...] = grad_own[...].astype(BF16)
    total_keyval[:WINDOW] = (grad_own[:WINDOW] + from_below[...].astype(F32)).astype(BF16)
    total_keyval[count - WINDOW :] = (
        grad_own[count - WINDOW :] + from_above[...].astype(F32)
    ).astype(BF16)
    spread_query = tokens_by_slots(routes[0:1, :], count)
    spread_keyval = tokens_by_slots(routes[1:2, :], count)
    query_rows = dot_right(grad_heavy_query[...], heavy_query[...])
    query_rows += logit_query[:, :1] * router[0:1, :]
    keyval_rows = dot_right(grad_raw_keyval[...], heavy_keyval[...])
    keyval_rows += logit_keyval[:, :1] * router[1:2, :]
    grad = (
        dot_right(grad_query[...], light_query[...])
        + dot_right(total_keyval[...], light_keyval[...])
        + dot_exact(spread_query, query_rows)
        + dot_exact(spread_keyval, keyval_rows)
    )
    signal = tokens[...].astype(F32)
    back, gain_grad = norm_back(signal, gain[...], grad)
    tokens_grad[...] = (grad_residual[...] + back).astype(BF16)
    signal = normed(signal, gain[...])
    small[0:1] = gain_grad
    small[1:2] = feed_small[0:1]
    small[2:3] = jnp.sum(dot_exact(spread_query, logit_query[...])[:, :1] * signal, 0, keepdims=True)
    small[3:4] = jnp.sum(dot_exact(spread_keyval, logit_keyval[...])[:, :1] * signal, 0, keepdims=True)
    small[4:5] = feed_small[1:2]
    small[5:8] = jnp.zeros((3, small.shape[1]), F32)


def run(body, outs, ins, limit, gflops=0.0, scratch=(), smem=0):
    vmem = pl.BlockSpec(memory_space=pltpu.VMEM)
    size = sum(v.size * v.dtype.itemsize for v in ins) + sum(
        math.prod(shape) * jnp.dtype(kind).itemsize for shape, kind in outs
    )
    return pl.pallas_call(
        body,
        out_shape=[jax.ShapeDtypeStruct(shape, kind) for shape, kind in outs],
        in_specs=[pl.BlockSpec(memory_space=pltpu.SMEM)] * smem + [vmem] * (len(ins) - smem),
        out_specs=[vmem] * len(outs),
        scratch_shapes=list(scratch),
        compiler_params=pltpu.CompilerParams(vmem_limit_bytes=int(limit * MIB)),
        cost_estimate=pl.CostEstimate(
            flops=int(gflops * 1e9), bytes_accessed=size, transcendentals=0
        ),
    )(*ins)


def heavy_feed(rows_feed, grad_raw, heavy_expand, heavy_reduce):
    slots, width = rows_feed.shape
    hidden = heavy_reduce.shape[0]
    part = 512
    steps = hidden // part
    fixed = pl.BlockSpec((slots, width), lambda j: (0, 0))
    moving = pl.BlockSpec((slots, part), lambda j: (0, j))
    return pl.pallas_call(
        heavy_feed_kernel,
        grid=(steps,),
        out_shape=[jax.ShapeDtypeStruct((slots, hidden), BF16)] * 3
        + [jax.ShapeDtypeStruct((slots, width), F32)] * 2,
        in_specs=[
            fixed,
            fixed,
            pl.BlockSpec((width, part), lambda j: (0, j)),
            pl.BlockSpec((width, part), lambda j: (0, steps + j)),
            pl.BlockSpec((part, width), lambda j: (j, 0)),
        ],
        out_specs=[moving] * 3 + [fixed] * 2,
        compiler_params=pltpu.CompilerParams(vmem_limit_bytes=24 * MIB),
        cost_estimate=pl.CostEstimate(
            flops=12 * slots * width * hidden, bytes_accessed=20 << 20, transcendentals=0
        ),
    )(rows_feed, grad_raw, heavy_expand, heavy_expand, heavy_reduce)


def light_feed(low, cotangent, light_expand, light_reduce):
    count, width = low.shape
    hidden = light_reduce.shape[0]
    part = hidden // 2
    fixed = pl.BlockSpec((count, width), lambda j: (0, 0))
    return pl.pallas_call(
        light_feed_kernel,
        grid=(2,),
        out_shape=[
            jax.ShapeDtypeStruct((count, width), F32),
            jax.ShapeDtypeStruct((count, width), F32),
            jax.ShapeDtypeStruct((2, width, hidden), BF16),
            jax.ShapeDtypeStruct((2, hidden, width // 2), BF16),
        ],
        in_specs=[
            fixed,
            fixed,
            pl.BlockSpec((width, part), lambda j: (0, j)),
            pl.BlockSpec((width, part), lambda j: (0, 2 + j)),
            pl.BlockSpec((part, width), lambda j: (j, 0)),
        ],
        out_specs=[
            fixed,
            fixed,
            pl.BlockSpec((1, width, hidden), lambda j: (j, 0, 0)),
            pl.BlockSpec((2, part, width // 2), lambda j: (0, j, 0)),
        ],
        scratch_shapes=[pltpu.VMEM((count, width), BF16)],
        compiler_params=pltpu.CompilerParams(vmem_limit_bytes=40 * MIB),
        cost_estimate=pl.CostEstimate(
            flops=18 * count * width * hidden, bytes_accessed=20 << 20, transcendentals=0
        ),
    )(low, cotangent, light_expand, light_expand, light_reduce)


def products_kernel(formers, latters, small, products):
    width = formers.shape[1] // 3
    quarter = width // 4
    offsets = ((0, 0, quarter), (1, quarter, quarter), (2, 2 * quarter, 2 * quarter))
    for part, start, columns in offsets:
        products[:, start : start + columns] = dot_left(
            formers[:, part * width : (part + 1) * width], latters[:, start : start + columns]
        ).astype(BF16)
    rows = small.shape[0]
    high = small[...].astype(BF16)
    low = (small[...] - high.astype(F32)).astype(BF16)
    same = (
        lax.broadcasted_iota(jnp.int32, (rows, 128), 0)
        == lax.broadcasted_iota(jnp.int32, (rows, 128), 1)
    ).astype(BF16)
    products[:, width:] = (dot_left(high, same) + dot_left(low, same)).astype(BF16)


def outer_kernel(former, latter, product):
    product[...] = dot_left(former[...], latter[...]).astype(BF16)


def stages(count):
    found, stride = [], 1
    while count > 1:
        size = 4 if count % 4 == 0 and count != 8 else 2
        found.append((size, stride))
        stride, count = stride * size, count // size
    return found


def shifted(block, axis, size, stride, step):
    route = []
    for i in range(lax.axis_size(axis)):
        member = (i // stride) % size
        route.append((i, i + ((member + step) % size - member) * stride))
    return lax.ppermute(block, axis, route)


def neighbours(block, distance):
    devices = range(lax.axis_size("seq"))
    return lax.ppermute(
        block, "seq", [(i - distance, i) for i in devices if i - distance in devices]
    )


def member_of(axis, size, stride):
    return (lax.axis_index(axis) // stride) % size


def pick(block, index, dim):
    return lax.dynamic_index_in_dim(block, index, dim, keepdims=False)


def reduce_stage(block, axis, size, stride, dim):
    me = member_of(axis, size, stride)
    total = pick(block, me, dim).astype(F32)
    for step in range(1, size):
        sent = pick(block, (me + step) % size, dim)
        total = total + shifted(sent, axis, size, stride, step).astype(F32)
    return total.astype(BF16)


def reduce_dp(block):
    block = reduce_stage(block, "dp", 2, 1, 0)
    half = block.shape[1] // 2
    first, second = block[:, :half], block[:, half:]
    x = member_of("dp", 2, 2)
    got = shifted(jnp.where(x == 0, second, first), "dp", 2, 2, 1)
    return (jnp.where(x == 0, first, second).astype(F32) + got.astype(F32)).astype(BF16)


def reduce_seq(block, skip=0):
    for size, stride in stages(lax.axis_size("seq"))[skip:]:
        count = lax.axis_size("seq") // stride
        block = block.reshape(count // size, size, block.shape[0] // count, block.shape[1])
        block = reduce_stage(block, "seq", size, stride, 1)
        block = block.reshape(-1, block.shape[-1])
    return block


def gather_seq(block):
    for size, stride in stages(lax.axis_size("seq"))[::-1]:
        block = jnp.concatenate(
            [block] + [shifted(block, "seq", size, stride, step) for step in range(1, size)], 0
        )
    return block


def swap_rows(axis, stride, whole, mine, other):
    got = shifted(jnp.concatenate([whole, other], 1), axis, 2, stride, 1)
    width = whole.shape[1]
    return (
        jnp.concatenate([whole, got[:, :width]], 0),
        jnp.concatenate([mine, got[:, width:]], 0),
    )


def gather_dp(former, first, second):
    core, x = member_of("dp", 2, 1), member_of("dp", 2, 2)
    half = first.shape[1] // 2

    def both(low, high):
        return jnp.concatenate([low, high], 1)

    lows = both(first[:, :half], second[:, :half])
    highs = both(first[:, half:], second[:, half:])
    former, latter = swap_rows(
        "dp", 1, former, jnp.where(core == 0, lows, highs), jnp.where(core == 0, highs, lows)
    )
    low, high = latter[:, :half], latter[:, half:]
    return swap_rows(
        "dp", 2, former, jnp.where(x == 0, low, high), jnp.where(x == 0, high, low)
    )


def split_rows(former, latter, size, stride):
    rows, width = former.shape
    count = lax.axis_size("seq") // stride
    former = former.reshape(rows, count // size, size, width // count)
    me = member_of("seq", size, stride)
    formers, latters = [pick(former, me, 2).reshape(rows, width // size)], [latter]
    for step in range(1, size):
        other = pick(former, (me + step) % size, 2).reshape(rows, width // size)
        got = shifted(jnp.concatenate([other, latter], 1), "seq", size, stride, step)
        formers.append(got[:, : width // size])
        latters.append(got[:, width // size :])
    return jnp.concatenate(formers, 0), jnp.concatenate(latters, 0)


def outer(former, latter):
    rows, width = former.shape
    columns = latter.shape[1]
    return run(
        outer_kernel, [((width, columns), BF16)], [former, latter], 24, 2e-9 * rows * width * columns
    )[0]


def expand_gradient(former, gate, up):
    former, latter = gather_dp(former, gate, up)
    size, stride = stages(lax.axis_size("seq"))[0]
    former, latter = split_rows(former, latter, size, stride)
    return reduce_seq(outer(former, latter), 1)


def reduce_gradient(former, latter):
    for size, stride in stages(lax.axis_size("seq")):
        former, latter = split_rows(former, latter, size, stride)
    quarter = latter.shape[1] // 4
    parts = [latter[:, i * quarter : (i + 1) * quarter] for i in (0, 2, 1, 3)]
    product = outer(former, jnp.concatenate(parts, 1))
    half = product.shape[1] // 2
    return reduce_dp(jnp.stack([product[:, :half], product[:, half:]]))


def sum_dp(block):
    for stride in (1, 2):
        block = block + shifted(block, "dp", 2, stride, 1)
    return block


def on_device(
    tokens,
    cotangent,
    document_bounds,
    routes,
    attention_gain,
    feedforward_gain,
    router,
    light_query,
    light_keyval,
    light_output,
    heavy_query,
    heavy_keyval,
    heavy_output_weight,
    light_expand,
    light_reduce,
    heavy_expand,
    heavy_reduce,
):
    count, width = tokens.shape
    slots = routes.shape[1]
    seq = lax.axis_size("seq")
    length = count * seq
    gain, feed_gain = attention_gain[None], feedforward_gain[None]
    heavy_width = heavy_query.shape[1]

    above = neighbours(tokens[count - WINDOW :], 1)
    below = neighbours(tokens[:WINDOW], -1)
    (packet,) = run(
        select_kernel,
        [((slots, width + 128), BF16)],
        [document_bounds, routes, tokens],
        8,
        0.1,
        smem=1,
    )
    gathered = gather_seq(packet)
    low, query, keyval, rows_query, rows_keyval, query_heavy, score_query = run(
        project_kernel,
        [
            ((count, width), BF16),
            ((count, width), BF16),
            ((count, 2 * width), BF16),
            ((slots, width), BF16),
            ((slots, width), BF16),
            ((slots, heavy_width), BF16),
            ((slots, 128), F32),
        ],
        [routes, tokens, gain, router, light_query, light_keyval, heavy_query],
        24,
        2.5,
    )
    span = (count + 2 * WINDOW, 2 * width)
    attended, peaks, halo_low, halo_keyval = run(
        functools.partial(light_forward_kernel, length),
        [
            ((count, width), BF16),
            ((count, 128), F32),
            ((2 * WINDOW, width), BF16),
            ((2 * WINDOW, 2 * width), BF16),
        ],
        [document_bounds, query, keyval, above, below, gain, light_keyval],
        24,
        3.0,
        [pltpu.VMEM(span, BF16)],
        smem=1,
    )
    keyval_heavy, heavy_attended, heavy_scaled, heavy_peaks, own_values, score_keyval = run(
        functools.partial(heavy_forward_kernel, count),
        [
            ((seq * slots, 2 * heavy_width), BF16),
            ((slots, heavy_width), F32),
            ((slots, heavy_width), BF16),
            ((slots, 128), F32),
            ((slots, heavy_width), F32),
            ((slots, 128), F32),
        ],
        [document_bounds, routes, gathered, query_heavy, score_query, gain, router, heavy_keyval],
        24 if seq <= 8 else 48,
        2.0,
        smem=1,
    )
    residual, feed_low, rows_feed, score_feed, cotangent_rows, grad_raw = run(
        residual_kernel,
        [
            ((count, width), F32),
            ((count, width), BF16),
            ((slots, width), BF16),
            ((slots, 128), F32),
            ((slots, width), F32),
            ((slots, width), BF16),
        ],
        [
            routes, tokens, attended, light_output, heavy_scaled, heavy_output_weight, feed_gain,
            router, cotangent,
        ],
        24,
        1.5,
    )
    gated_heavy, grad_gate, grad_up, raw_feed, grad_rows = heavy_feed(
        rows_feed, grad_raw, heavy_expand, heavy_reduce
    )
    grad_heavy_expand = expand_gradient(rows_feed, grad_gate, grad_up)
    grad_heavy_reduce = reduce_gradient(gated_heavy, grad_raw)
    light_result, grad_low, expand_products, reduce_products = light_feed(
        feed_low, cotangent, light_expand, light_reduce
    )
    grad_light_expand = reduce_seq(reduce_dp(expand_products))
    grad_light_reduce = reduce_seq(reduce_dp(reduce_products))
    (
        output,
        grad_residual,
        grad_residual_low,
        grad_attended,
        grad_heavy_rows,
        grad_heavy_attended,
        logit_query,
        feed_small,
    ) = run(
        turn_kernel,
        [
            ((count, width), BF16),
            ((count, width), F32),
            ((count, width), BF16),
            ((count, width), BF16),
            ((slots, width), BF16),
            ((slots, heavy_width), BF16),
            ((slots, 128), F32),
            ((2, width), F32),
        ],
        [
            routes, residual, feed_gain, light_result, grad_low, raw_feed, grad_rows, score_feed,
            cotangent_rows, cotangent, router, light_output, heavy_output_weight, heavy_attended,
            score_query,
        ],
        32,
        1.5,
    )
    grad_heavy_query, packet = run(
        functools.partial(heavy_query_kernel, count),
        [((slots, heavy_width), BF16), ((slots, 2 * heavy_width + 128), BF16)],
        [
            document_bounds, routes, gathered, query_heavy, keyval_heavy, heavy_peaks,
            grad_heavy_attended,
        ],
        16 if seq <= 8 else 48,
        0.3,
        smem=1,
    )
    packets = gather_seq(packet)
    grad_query, grad_own, grad_above, grad_below, mixer_products = run(
        functools.partial(light_backward_kernel, length),
        [
            ((count, width), BF16),
            ((count, 2 * width), F32),
            ((WINDOW, 2 * width), BF16),
            ((WINDOW, 2 * width), BF16),
            ((2, width, 2 * width), BF16),
        ],
        [
            document_bounds, query, keyval, halo_keyval, low, halo_low, peaks, grad_attended,
            attended, grad_residual_low,
        ],
        40,
        6.0,
        [pltpu.VMEM(span, BF16), pltpu.VMEM(span, F32)],
        smem=1,
    )
    from_above = neighbours(grad_above, -1)
    from_below = neighbours(grad_below, 1)
    mixer_sums = reduce_seq(reduce_dp(mixer_products))
    grad_raw_keyval, logit_keyval = run(
        functools.partial(heavy_key_kernel, count),
        [((slots, 2 * heavy_width), BF16), ((slots, 128), F32)],
        [document_bounds, routes, packets, keyval_heavy[:slots], own_values, score_keyval],
        16 if seq <= 8 else 48,
        0.3,
        smem=1,
    )
    tokens_grad, small = run(
        mixer_kernel,
        [((count, width), BF16), ((8, width), F32)],
        [
            routes, tokens, gain, router, grad_residual, grad_query, grad_own, from_below,
            from_above, grad_heavy_query, grad_raw_keyval, logit_query, logit_keyval, light_query,
            light_keyval, heavy_query, heavy_keyval, feed_small,
        ],
        40,
        3.0,
        [pltpu.VMEM((count, 2 * width), BF16)],
    )
    quarter = heavy_width // 4
    formers = jnp.concatenate([rows_query, heavy_scaled, rows_keyval], 1)

    def mine(part):
        low_columns = slice(part * quarter, (part + 1) * quarter)
        high_columns = slice(2 * part * quarter, 2 * (part + 1) * quarter)
        return [
            grad_heavy_query[:, low_columns],
            grad_heavy_rows[:, low_columns],
            grad_raw_keyval[:, high_columns],
        ]

    first = jnp.concatenate(mine(0) + mine(1), 1)
    second = jnp.concatenate(mine(2) + mine(3), 1)
    formers, latters = gather_dp(formers, first, second)
    (heavy_products,) = run(
        products_kernel,
        [((width, width + 128), BF16)],
        [formers, latters, sum_dp(small)],
        16,
        0.6,
    )
    heavy_sums = reduce_seq(heavy_products).astype(F32)
    mixer_sums = mixer_sums.astype(F32)
    quarter = width // 4
    return (
        output,
        tokens_grad,
        heavy_sums[:, width],
        heavy_sums[:, width + 1],
        heavy_sums[:, width + 2 : width + 5].T,
        mixer_sums[:, 2 * quarter : 3 * quarter],
        mixer_sums[:, : 2 * quarter],
        mixer_sums[:, 3 * quarter :],
        heavy_sums[:, :quarter],
        heavy_sums[:, 2 * quarter : 4 * quarter],
        heavy_sums[:, quarter : 2 * quarter],
        grad_light_expand.astype(F32),
        grad_light_reduce.astype(F32),
        grad_heavy_expand.astype(F32),
        grad_heavy_reduce.astype(F32),
    )


def solution(mesh):
    whole, rows = P(), P(("dp", "seq"), None)
    return jax.shard_map(
        on_device,
        mesh=mesh,
        in_specs=(rows, rows, whole, P(None, ("dp", "seq"))) + (whole,) * 13,
        out_specs=(rows, rows, P("seq"), P("seq"), P(None, "seq")) + (P("seq", "dp"),) * 10,
        check_vma=False,
    )
```

```python
import functools
import math

import jax
import jax.numpy as jnp
from jax import lax
from jax.experimental import pallas as pl
from jax.experimental.pallas import tpu as pltpu
from jax.sharding import PartitionSpec as P

LH = 8
HHS = 64
WINDOW = 128
EPSILON = 1e-06
MASKED = -1e30
HIGHEST = lax.Precision.HIGHEST
F32, BF16 = jnp.float32, jnp.bfloat16
MIB = 1 << 20


def dot(former, latter):
    return jnp.dot(former, latter, preferred_element_type=F32)


def dot_left(former, latter):
    return lax.dot_general(former, latter, (((0,), (0,)), ((), ())), preferred_element_type=F32)


def dot_right(former, latter):
    return lax.dot_general(former, latter, (((1,), (1,)), ((), ())), preferred_element_type=F32)


def dot_exact(former, latter):
    return jnp.dot(former, latter, preferred_element_type=F32, precision=HIGHEST)


def column_of(row):
    count = row.shape[1]
    same = lax.broadcasted_iota(jnp.int32, (count, count), 0) == lax.broadcasted_iota(
        jnp.int32, (count, count), 1
    )
    return jnp.sum(jnp.where(same, row.astype(F32), 0.0), axis=1, keepdims=True)


def slots_by_tokens(route_row, tokens):
    column = column_of(route_row).astype(jnp.int32)
    lanes = lax.broadcasted_iota(jnp.int32, (route_row.shape[1], tokens), 1)
    return (column == lanes).astype(F32)


def tokens_by_slots(route_row, tokens):
    rows = lax.broadcasted_iota(jnp.int32, (tokens, route_row.shape[1]), 0)
    return (rows == route_row).astype(F32)


def normed(rows, gain):
    return rows * lax.rsqrt(jnp.mean(rows * rows, -1, keepdims=True) + EPSILON) * gain


def norm_back(rows, gain, grad):
    inverse = lax.rsqrt(jnp.mean(rows * rows, -1, keepdims=True) + EPSILON)
    plain = rows * inverse
    scaled = grad * gain
    inner = jnp.mean(scaled * plain, -1, keepdims=True)
    return inverse * (scaled - plain * inner), jnp.sum(grad * plain, 0, keepdims=True)


def sigmoid(value):
    return 1.0 / (1.0 + jnp.exp(-value))


def segment(place, first, last):
    return (place >= first).astype(F32) + (place >= last).astype(F32)


def gelu_parts(value):
    slope = math.sqrt(2.0 / math.pi)
    square = value * value
    bent = jnp.tanh(slope * value * (1.0 + 0.044715 * square))
    half = 0.5 * (1.0 + bent)
    rise = half + 0.5 * value * (1.0 - bent * bent) * slope * (1.0 + 3 * 0.044715 * square)
    return value * half, rise


def place(tok_rows, bounds):
    lead = lax.axis_index("seq") * tok_rows
    group = lax.axis_index("dp")
    return lead, bounds[group, 0], bounds[group, 1]


def select_kernel(bounds, routes, tokens, packet):
    count, width = tokens.shape
    lead, first, last = place(count, bounds)
    row = routes[1:2, :]
    chosen = slots_by_tokens(row, count).astype(BF16)
    packet[:, :width] = dot(chosen, tokens[...]).astype(BF16)
    column = column_of(row)
    tag = jnp.where(column >= 0, segment(column.astype(jnp.int32) + lead, first, last), -1.0)
    packet[:, width:] = jnp.broadcast_to(tag, (tag.shape[0], 128)).astype(BF16)


def project_kernel(
    routes, tokens, gain, router, light_query, light_keyval, heavy_query,
    low, query, keyval, rows_query, rows_keyval, query_heavy, score_query,
):
    count = tokens.shape[0]
    width = tokens.shape[1]
    low[...] = normed(tokens[...].astype(F32), gain[...]).astype(BF16)
    widen(query, slice(None), 0, dot(low[...], light_query[...]).astype(BF16), 0.0)
    pair = dot(low[...], light_keyval[...]).astype(BF16)
    widen(keyval, slice(None), 0, pair[:, :width], 0.0)
    widen(keyval, slice(None), LH * 128, pair[:, width:], 1.0)
    chosen = slots_by_tokens(routes[0:1, :], count).astype(BF16)
    raw = dot(chosen, tokens[...])
    rows = normed(raw, gain[...])
    logit = jnp.sum(rows * router[0:1, :], -1, keepdims=True)
    score_query[...] = jnp.broadcast_to(sigmoid(logit), score_query.shape)
    rows_query[...] = dot(chosen, low[...]).astype(BF16)
    query_heavy[...] = dot(rows_query[...], heavy_query[...]).astype(BF16)
    chosen = slots_by_tokens(routes[1:2, :], count).astype(BF16)
    rows_keyval[...] = dot(chosen, low[...]).astype(BF16)


def widen(ref, rows, start, value, filler):
    size = value.shape[1] // LH
    rest = jnp.full((value.shape[0], 128 - size), filler, BF16)
    for head in range(LH):
        base = start + head * 128
        ref[rows, base : base + size] = value[:, head * size : (head + 1) * size]
        ref[rows, base + size : base + 128] = rest


def light_mask(tok_rows, length, bounds, step):
    lead, first, last = place(tok_rows, bounds)
    shape = (3 * WINDOW, WINDOW)
    query_place = lead + step * WINDOW + lax.broadcasted_iota(jnp.int32, shape, 1)
    key_place = lead + (step - 1) * WINDOW + lax.broadcasted_iota(jnp.int32, shape, 0)
    allowed = (key_place >= 0) & (key_place < length)
    allowed = allowed & (jnp.abs(query_place - key_place) <= WINDOW)
    return allowed & (segment(query_place, first, last) == segment(key_place, first, last))


def light_forward_kernel(
    length, bounds, query, keyval, low, above, below, gain, light_keyval,
    attended, peaks, span_low, span,
):
    tok_rows, width = low.shape
    size = width // LH
    values_start = LH * 128
    scale = size ** (-0.5) / math.log(2.0)
    own = slice(WINDOW, WINDOW + tok_rows)
    span_low[own] = low[...]
    span[own] = keyval[...]
    for rows, signal in ((slice(0, WINDOW), above), (slice(WINDOW + tok_rows, None), below)):
        span_low[rows] = normed(signal[...].astype(F32), gain[...]).astype(BF16)
        pair = dot(span_low[rows], light_keyval[...]).astype(BF16)
        widen(span, rows, 0, pair[:, :width], 0.0)
        widen(span, rows, values_start, pair[:, width:], 1.0)
    for step in range(tok_rows // WINDOW):
        rows = slice(step * WINDOW, (step + 1) * WINDOW)
        keys = slice(step * WINDOW, (step + 3) * WINDOW)
        allowed = light_mask(tok_rows, length, bounds, step)
        for head in range(LH):
            wide = slice(head * 128, (head + 1) * 128)
            values = slice(values_start + head * 128, values_start + (head + 1) * 128)
            scores = jnp.where(allowed, dot_right(span[keys, wide], query[rows, wide]), MASKED)
            peak = jnp.max(scores, 0, keepdims=True)
            exponent = jnp.exp2((scores - peak) * scale)
            total = jnp.sum(exponent, 0, keepdims=True)
            result = dot_left(exponent.astype(BF16), span[keys, values])
            result = result[:, :size] * (1.0 / result[:, size : size + 1])
            attended[rows, head * size : (head + 1) * size] = result.astype(BF16)
            peaks[head : head + 1, rows] = peak * scale + jnp.log2(total)


def light_half(
    half, length, bounds, query, span, peaks, grad, attended, grad_query, grad_keys, grad_values,
):
    tok_rows, width = grad.shape
    size = width // LH
    heads = LH // 2
    scale = size ** (-0.5) / math.log(2.0)
    lanes = slice(half * heads * size, (half + 1) * heads * size)
    product = grad[:, lanes].astype(F32) * attended[:, lanes].astype(F32)
    high = product.astype(BF16)
    rest = (product - high.astype(F32)).astype(BF16)
    shape = (8, heads * size)
    column = lax.broadcasted_iota(jnp.int32, shape, 1)
    row = lax.broadcasted_iota(jnp.int32, shape, 0)
    pickers = ((column >= row * size) & (column < (row + 1) * size)).astype(BF16)
    inners = dot_right(pickers, high) + dot_right(pickers, rest)
    grad_keys[...] = jnp.zeros_like(grad_keys)
    grad_values[...] = jnp.zeros_like(grad_values)
    for step in range(tok_rows // WINDOW):
        rows = slice(step * WINDOW, (step + 1) * WINDOW)
        keys = slice(step * WINDOW, (step + 3) * WINDOW)
        allowed = light_mask(tok_rows, length, bounds, step)
        for index in range(heads):
            head = half * heads + index
            wide = slice(head * 128, (head + 1) * 128)
            start = LH * 128 + head * 128
            here = slice(index * 128, (index + 1) * 128)
            columns = slice(head * size, (head + 1) * size)
            scores = dot_right(span[keys, wide], query[rows, wide]) * scale
            weights = jnp.exp2(
                jnp.where(allowed, scores, MASKED) - peaks[head : head + 1, rows]
            )
            given = grad[rows, columns]
            grad_weights = dot_right(span[keys, start : start + size], given)
            inner = inners[index : index + 1, rows]
            grad_scores = (weights * (grad_weights - inner)).astype(BF16)
            result = dot_left(grad_scores, span[keys, wide])[:, :size] * size ** (-0.5)
            grad_query[rows, index * size : (index + 1) * size] = result.astype(BF16)
            grad_keys[keys, here] += dot(grad_scores, query[rows, wide])
            grad_values[keys, index * 128 : index * 128 + size] += dot(weights.astype(BF16), given)


def narrow(grad_span, grad_keys, grad_values):
    half = grad_span.shape[1] // 2
    size = 2 * half // LH
    for head in range(LH // 2):
        here = slice(head * 128, head * 128 + size)
        columns = slice(head * size, (head + 1) * size)
        grad_span[:, columns] = (grad_keys[:, here] * size ** (-0.5)).astype(BF16)
        columns = slice(half + head * size, half + (head + 1) * size)
        grad_span[:, columns] = grad_values[:, here].astype(BF16)


def light_first_kernel(
    length, bounds, query, span, peaks, grad, attended, grad_query, grad_span, grad_keys, grad_values
):
    light_half(
        0, length, bounds, query, span, peaks, grad, attended, grad_query, grad_keys, grad_values
    )
    narrow(grad_span, grad_keys, grad_values)


def light_second_kernel(
    length, bounds, query, span, peaks, grad, attended, first_span,
    grad_query, grad_span, grad_above, grad_below, grad_keys, grad_values,
):
    light_half(
        1, length, bounds, query, span, peaks, grad, attended, grad_query, grad_keys, grad_values
    )
    narrow(grad_span, grad_keys, grad_values)
    half = grad_span.shape[1] // 2
    count = grad_span.shape[0]
    for ref, rows in ((grad_above, slice(0, WINDOW)), (grad_below, slice(count - WINDOW, count))):
        ref[:, :half] = first_span[rows, :half]
        ref[:, half : 2 * half] = grad_span[rows, :half]
        ref[:, 2 * half : 3 * half] = first_span[rows, half:]
        ref[:, 3 * half :] = grad_span[rows, half:]


def light_products_kernel(
    span_low, first_query, second_query, first_span, second_span, attended, grad_residual, kept, sent
):
    tok_rows, width = attended.shape
    quarter = width // 4
    half = width // 2
    core = lax.axis_index("dp") % 2
    own = slice(WINDOW, WINDOW + tok_rows)
    for part in range(4):
        grad_span = (first_span, second_span)[part % 2]
        columns = slice((part // 2) * half, (part // 2 + 1) * half)
        keyval_part = dot_left(span_low[...], grad_span[:, columns]).astype(BF16)
        grad_query = (first_query, second_query)[part // 2]
        columns = slice((part % 2) * quarter, (part % 2 + 1) * quarter)
        query_part = dot_left(span_low[own], grad_query[:, columns]).astype(BF16)
        columns = slice(part * quarter, (part + 1) * quarter)
        output_part = dot_left(attended[...], grad_residual[:, columns]).astype(BF16)
        for ref, chosen in ((kept, core == part % 2), (sent, core != part % 2)):

            @pl.when(chosen)
            def _(ref=ref, x=part // 2, parts=(keyval_part, query_part, output_part)):
                ref[x, :, : 2 * quarter] = parts[0]
                ref[x, :, 2 * quarter : 3 * quarter] = parts[1]
                ref[x, :, 3 * quarter :] = parts[2]


def heavy_forward_kernel(
    count, bounds, routes, gathered, query_heavy, score_query, gain, router, heavy_keyval,
    keyval, attended, scaled, peaks, own_values, score_keyval,
):
    width = query_heavy.shape[1]
    slots = query_heavy.shape[0]
    total_rows = gathered.shape[0]
    part = min(512, total_rows)
    for start in range(0, total_rows, part):
        rows = slice(start, start + part)
        signal = normed(gathered[rows, :width].astype(F32), gain[...])
        logit = jnp.sum(signal * router[1:2, :], -1, keepdims=True)
        score = sigmoid(logit)
        raw = dot(signal.astype(BF16), heavy_keyval[...])
        keyval[rows, :width] = raw[:, :width].astype(BF16)
        keyval[rows, width:] = (score * raw[:, width:]).astype(BF16)
        if start == 0:
            own_values[...] = raw[:slots, width:]
            score_keyval[...] = jnp.broadcast_to(score[:slots], score_keyval.shape)
    allowed = heavy_mask(count, bounds, routes, gathered, width)
    lanes = lax.broadcasted_iota(jnp.int32, (slots, 128), 1)
    kept = jnp.zeros((slots, 128), F32)
    for head in range(width // HHS):
        columns = slice(head * HHS, (head + 1) * HHS)
        values = slice(width + head * HHS, width + (head + 1) * HHS)
        scores = dot_right(query_heavy[:, columns], keyval[:, columns]) * HHS ** (-0.5)
        scores = jnp.where(allowed, scores, MASKED)
        peak = jnp.max(scores, -1, keepdims=True)
        exponent = jnp.where(allowed, jnp.exp(scores - peak), 0.0)
        total = jnp.sum(exponent, -1, keepdims=True)
        total = jnp.where(total > 0, total, 1.0)
        weights = (exponent * (1.0 / total)).astype(BF16)
        result = dot(weights, keyval[:, values])
        attended[:, columns] = result
        scaled[:, columns] = (score_query[:, :1] * result).astype(BF16)
        kept = jnp.where(lanes == head, peak + jnp.log(total), kept)
    peaks[...] = kept


def heavy_mask(count, bounds, routes, gathered, width):
    lead, first, last = place(count, bounds)
    pickers = (lax.broadcasted_iota(jnp.int32, (8, 128), 1) == 0).astype(BF16)
    key_segment = dot_right(pickers, gathered[:, width:])[:1]
    return own_segment(routes, lead, first, last) == key_segment


def own_segment(routes, lead, first, last):
    column = column_of(routes[0:1, :])
    spot = jnp.where(column >= 0, column.astype(jnp.int32) + lead, -1)
    return segment(spot, first, last)


def residual_kernel(
    routes, tokens, attended, light_output, scaled, heavy_output, gain, router, cotangent,
    residual, low, rows_feed, score_feed, cotangent_rows, grad_raw,
):
    count = tokens.shape[0]
    spread = tokens_by_slots(routes[0:1, :], count).astype(BF16)
    scattered = dot(spread, scaled[...]).astype(BF16)
    residual[...] = (
        tokens[...].astype(F32)
        + dot(attended[...], light_output[...])
        + dot(scattered, heavy_output[...])
    )
    signal = normed(residual[...], gain[...])
    low[...] = signal.astype(BF16)
    logit = jnp.sum(signal * router[2:3, :], -1, keepdims=True)
    chosen = slots_by_tokens(routes[2:3, :], count)
    logit = dot_exact(chosen, jnp.broadcast_to(logit, (count, 128)))
    score = sigmoid(logit)
    score_feed[...] = score
    chosen = chosen.astype(BF16)
    rows_feed[...] = dot(chosen, low[...]).astype(BF16)
    rows = dot(chosen, cotangent[...])
    cotangent_rows[...] = rows
    grad_raw[...] = (score[:, :1] * rows).astype(BF16)


def feed_step(rows_feed, grad_raw, gate_weight, up_weight, reduce_weight, raw, grad_rows):
    @pl.when(pl.program_id(0) == 0)
    def _():
        raw[...] = jnp.zeros_like(raw)
        grad_rows[...] = jnp.zeros_like(grad_rows)

    gate = dot(rows_feed[...], gate_weight[...])
    up = dot(rows_feed[...], up_weight[...])
    bent, rise = gelu_parts(gate)
    gated_low = (bent * up).astype(BF16)
    raw[...] += dot(gated_low, reduce_weight[...])
    grad_gated = dot_right(grad_raw[...], reduce_weight[...])
    gate_low = (grad_gated * up * rise).astype(BF16)
    up_low = (grad_gated * bent).astype(BF16)
    grad_rows[...] += dot_right(gate_low, gate_weight[...]) + dot_right(up_low, up_weight[...])
    return gated_low, gate_low, up_low


def heavy_feed_kernel(
    rows_feed, grad_raw, gate_weight, up_weight, reduce_weight,
    raw, grad_rows, gated, grad_gate, grad_up,
):
    gated_low, gate_low, up_low = feed_step(
        rows_feed, grad_raw, gate_weight, up_weight, reduce_weight, raw, grad_rows
    )
    gated[...] = gated_low
    grad_gate[...] = gate_low
    grad_up[...] = up_low


def heavy_feed_split_kernel(
    rows_feed, grad_raw, gate_weight, up_weight, reduce_weight,
    raw, grad_rows, kept, sent, own, first, second, third,
):
    gated_low, gate_low, up_low = feed_step(
        rows_feed, grad_raw, gate_weight, up_weight, reduce_weight, raw, grad_rows
    )
    step = pl.program_id(0)
    width, part = rows_feed.shape[1], gated_low.shape[1]
    half = kept.shape[1] // 2
    start = pl.multiple_of((step % 4) * part, part)
    mine = step // 4 == lax.axis_index("dp") % 2

    @pl.when(mine)
    def _():
        kept[:, pl.ds(start, part)] = gate_low
        kept[:, pl.ds(half + start, part)] = up_low

    @pl.when(jnp.logical_not(mine))
    def _():
        sent[:, pl.ds(width + start, part)] = gate_low
        sent[:, pl.ds(width + half + start, part)] = up_low

    slot = (step // 2 + 4 - lax.axis_index("seq") // 2) % 4
    spot = pl.multiple_of((step % 2) * part, part)
    for index, ref in enumerate((own, first, second, third)):

        @pl.when(slot == index)
        def _(ref=ref):
            ref[:, pl.ds(spot, part)] = gated_low

    @pl.when(step == 0)
    def _():
        sent[:, :width] = rows_feed[...]
        for ref in (first, second, third):
            ref[:, 2 * part :] = grad_raw[...]


def light_feed_kernel(
    low, cotangent, gate_weight, up_weight, reduce_weight, result, grad_low, kept, sent, turned
):
    step = pl.program_id(0)
    width = cotangent.shape[1]
    quarter = width // 4

    @pl.when(step == 0)
    def _():
        result[...] = jnp.zeros_like(result)
        grad_low[...] = jnp.zeros_like(grad_low)
        for part in range(4):
            turned[part] = cotangent[:, part * quarter : (part + 1) * quarter]

    gate = dot(low[...], gate_weight[...])
    up = dot(low[...], up_weight[...])
    bent, rise = gelu_parts(gate)
    gated_low = (bent * up).astype(BF16)
    result[...] += dot(gated_low, reduce_weight[...])
    grad_gated = dot_right(cotangent[...], reduce_weight[...])
    gate_low = (grad_gated * up * rise).astype(BF16)
    up_low = (grad_gated * bent).astype(BF16)
    grad_low[...] += dot_right(gate_low, gate_weight[...]) + dot_right(up_low, up_weight[...])
    hidden = gate_low.shape[1]
    seq, rows = kept.shape[1:3]
    core = lax.axis_index("dp") % 2
    products = [dot_left(low[...], grad).astype(BF16) for grad in (gate_low, up_low)]
    for ref, chosen in ((kept, core == step), (sent, core != step)):

        @pl.when(chosen)
        def _(ref=ref):
            for x in range(2):
                for i in range(seq):
                    ref[x, i, :, :hidden] = products[x][i * rows : (i + 1) * rows]

    more = rows // 3
    for part in range(4):
        product = dot_left(gated_low, turned[part]).astype(BF16)
        for ref, chosen in ((kept, core == part % 2), (sent, core != part % 2)):

            @pl.when(chosen)
            def _(ref=ref, x=part // 2, product=product):
                for i in range(seq // 2):
                    spot = step * (seq // 2) + i
                    start = i * (rows + more)
                    ref[x, spot, :, hidden : hidden + quarter] = product[start : start + rows]
                    rest = product[start + rows : start + rows + more]
                    for piece in range(3):
                        ref[x, spot, piece * more : (piece + 1) * more, hidden + quarter :] = rest[
                            :, piece * 64 : (piece + 1) * 64
                        ]


def turn_kernel(
    routes, residual, gain, result, grad_low, raw, grad_rows, score_feed, cotangent_rows, cotangent,
    router, light_output, heavy_output, heavy_attended, score_query,
    output, grad_residual, grad_residual_low, grad_attended, grad_heavy_rows, grad_heavy_attended,
    logit_query, small,
):
    count = residual.shape[0]
    spread = tokens_by_slots(routes[2:3, :], count)
    score = score_feed[:, :1]
    output[...] = (
        residual[...] + result[...] + dot_exact(spread, score * raw[...])
    ).astype(BF16)
    logit = score * (1.0 - score) * jnp.sum(cotangent_rows[...] * raw[...], -1, keepdims=True)
    grad = grad_low[...] + dot_exact(spread, grad_rows[...] + logit * router[2:3, :])
    back, gain_grad = norm_back(residual[...], gain[...], grad)
    token_logit = dot_exact(spread, jnp.broadcast_to(logit, (logit.shape[0], 128)))[:, :1]
    signal = normed(residual[...], gain[...])
    small[0:1] = gain_grad
    small[1:2] = jnp.sum(token_logit * signal, 0, keepdims=True)
    total = cotangent[...].astype(F32) + back
    grad_residual[...] = total
    grad_residual_low[...] = total.astype(BF16)
    grad_attended[...] = dot_right(grad_residual_low[...], light_output[...]).astype(BF16)
    chosen = slots_by_tokens(routes[0:1, :], count).astype(BF16)
    grad_heavy_rows[...] = dot(chosen, grad_residual_low[...]).astype(BF16)
    scaled = dot_right(grad_heavy_rows[...], heavy_output[...])
    score = score_query[:, :1]
    logit = score * (1.0 - score) * jnp.sum(scaled * heavy_attended[...], -1, keepdims=True)
    logit_query[...] = jnp.broadcast_to(logit, logit_query.shape)
    grad_heavy_attended[...] = (score * scaled).astype(BF16)


def heavy_query_kernel(
    count, bounds, routes, gathered, query_heavy, keyval, peaks, grad, grad_query, packet
):
    slots, width = query_heavy.shape
    heads = width // HHS
    allowed = heavy_mask(count, bounds, routes, gathered, width)
    lanes = lax.broadcasted_iota(jnp.int32, (slots, 128), 1)
    kept = peaks[...]
    lead, first, last = place(count, bounds)
    tag = jnp.where(lanes == 4 * heads, own_segment(routes, lead, first, last), 0.0)
    for head in range(heads):
        columns = slice(head * HHS, (head + 1) * HHS)
        values = slice(width + head * HHS, width + (head + 1) * HHS)
        scores = dot_right(query_heavy[:, columns], keyval[:, columns]) * HHS ** (-0.5)
        peak = jnp.sum(jnp.where(lanes == head, kept, 0.0), -1, keepdims=True)
        weights = jnp.where(allowed, jnp.exp(scores - peak), 0.0)
        grad_weights = dot_right(grad[:, columns], keyval[:, values])
        inner = jnp.sum(weights * grad_weights, -1, keepdims=True)
        grad_scores = (weights * (grad_weights - inner)).astype(BF16)
        grad_query[:, columns] = (dot(grad_scores, keyval[:, columns]) * HHS ** (-0.5)).astype(BF16)
        for lane, value in ((head, peak), (heads + head, inner)):
            high = value.astype(BF16).astype(F32)
            tag = jnp.where(lanes == lane, high, tag)
            tag = jnp.where(lanes == 2 * heads + lane, value - high, tag)
    packet[:, :width] = query_heavy[...]
    packet[:, width : 2 * width] = grad[...]
    packet[:, 2 * width :] = tag.astype(BF16)


def heavy_key_kernel(
    count, bounds, routes, packets, keyval, own_values, score_keyval, grad_raw, logit_keyval
):
    slots = own_values.shape[0]
    width = own_values.shape[1]
    heads = width // HHS
    lead, first, last = place(count, bounds)
    column = column_of(routes[1:2, :])
    key_segment = jnp.where(
        column >= 0, segment(column.astype(jnp.int32) + lead, first, last), -1.0
    )
    same = lax.broadcasted_iota(jnp.int32, (128, 128), 0) == lax.broadcasted_iota(
        jnp.int32, (128, 128), 1
    )
    tags = dot_right(same.astype(BF16), packets[:, 2 * width :])
    allowed = key_segment == tags[4 * heads : 4 * heads + 1]
    score = score_keyval[:, :1]
    logit = jnp.zeros((slots, 1), F32)
    for head in range(heads):
        columns = slice(head * HHS, (head + 1) * HHS)
        values = slice(width + head * HHS, width + (head + 1) * HHS)
        peak = tags[head : head + 1] + tags[2 * heads + head : 2 * heads + head + 1]
        inner = tags[heads + head : heads + head + 1] + tags[3 * heads + head : 3 * heads + head + 1]
        scores = dot_right(keyval[:slots, columns], packets[:, columns]) * HHS ** (-0.5)
        weights = jnp.where(allowed, jnp.exp(scores - peak), 0.0)
        grad_weights = dot_right(keyval[:slots, values], packets[:, values])
        grad_scores = (weights * (grad_weights - inner)).astype(BF16)
        key_grad = dot(grad_scores, packets[:, columns]) * HHS ** (-0.5)
        value_grad = dot(weights.astype(BF16), packets[:, values]).astype(BF16).astype(F32)
        logit += jnp.sum(value_grad * own_values[:, columns], -1, keepdims=True)
        grad_raw[:, columns] = key_grad.astype(BF16)
        grad_raw[:, values] = (score * value_grad).astype(BF16)
    logit_keyval[...] = jnp.broadcast_to(score * (1.0 - score) * logit, logit_keyval.shape)


def mixer_kernel(
    routes, tokens, gain, router, grad_residual, first_query, second_query, first_span, second_span,
    from_below, from_above, grad_heavy_query, grad_raw_keyval, logit_query, logit_keyval, light_query, light_keyval,
    heavy_query, heavy_keyval, feed_small, tokens_grad, small, total_keyval,
):
    count = tokens.shape[0]
    half = first_query.shape[1]
    own = slice(WINDOW, WINDOW + count)
    for i, (ref, base) in enumerate(
        ((first_span, 0), (second_span, 0), (first_span, half), (second_span, half))
    ):
        total_keyval[:, i * half : (i + 1) * half] = ref[own, base : base + half]
    for rows, more in (
        (slice(0, WINDOW), from_below),
        (slice(count - WINDOW, count), from_above),
    ):
        total_keyval[rows] = (total_keyval[rows].astype(F32) + more[...].astype(F32)).astype(BF16)
    spread_query = tokens_by_slots(routes[0:1, :], count)
    spread_keyval = tokens_by_slots(routes[1:2, :], count)
    query_rows = dot_right(grad_heavy_query[...], heavy_query[...])
    query_rows += logit_query[:, :1] * router[0:1, :]
    keyval_rows = dot_right(grad_raw_keyval[...], heavy_keyval[...])
    keyval_rows += logit_keyval[:, :1] * router[1:2, :]
    grad = (
        dot_right(first_query[...], light_query[:, :half])
        + dot_right(second_query[...], light_query[:, half:])
        + dot_right(total_keyval[...], light_keyval[...])
        + dot_exact(spread_query, query_rows)
        + dot_exact(spread_keyval, keyval_rows)
    )
    signal = tokens[...].astype(F32)
    back, gain_grad = norm_back(signal, gain[...], grad)
    tokens_grad[...] = (grad_residual[...] + back).astype(BF16)
    signal = normed(signal, gain[...])
    small[0:1] = gain_grad
    small[1:2] = feed_small[0:1]
    small[2:3] = jnp.sum(dot_exact(spread_query, logit_query[...])[:, :1] * signal, 0, keepdims=True)
    small[3:4] = jnp.sum(dot_exact(spread_keyval, logit_keyval[...])[:, :1] * signal, 0, keepdims=True)
    small[4:5] = feed_small[1:2]
    small[5:8] = jnp.zeros((3, small.shape[1]), F32)


def estimate(gflops, size):
    return pl.CostEstimate(flops=int(gflops * 2e10), bytes_accessed=20 * size, transcendentals=0)


def without(body, start, count):
    def inner(*refs):
        return body(*refs[:start], *refs[start + count :])

    return inner


def run(body, outs, ins, limit, gflops=0.0, scratch=(), smem=0, deps=()):
    vmem = pl.BlockSpec(memory_space=pltpu.VMEM)
    size = sum(v.size * v.dtype.itemsize for v in ins) + sum(
        math.prod(shape) * jnp.dtype(kind).itemsize for shape, kind in outs
    )
    return pl.pallas_call(
        without(body, len(ins), len(deps)),
        out_shape=[jax.ShapeDtypeStruct(shape, kind) for shape, kind in outs],
        in_specs=[pl.BlockSpec(memory_space=pltpu.SMEM)] * smem
        + [vmem] * (len(ins) - smem)
        + [pl.BlockSpec(memory_space=pl.ANY)] * len(deps),
        out_specs=[vmem] * len(outs),
        scratch_shapes=list(scratch),
        compiler_params=pltpu.CompilerParams(vmem_limit_bytes=int(limit * MIB)),
        cost_estimate=estimate(gflops, size),
    )(*ins, *deps)


def heavy_feed(rows_feed, grad_raw, heavy_expand, heavy_reduce, seq):
    slots, width = rows_feed.shape
    hidden = heavy_reduce.shape[0]
    steps = 8
    part = hidden // steps
    fixed = pl.BlockSpec((slots, width), lambda j: (0, 0))
    moving = pl.BlockSpec((slots, part), lambda j: (0, j))
    split = seq == 8
    if split:
        columns = [hidden, width + hidden, 2 * part] + [2 * part + width] * 3
        specs = [pl.BlockSpec((slots, c), lambda j: (0, 0)) for c in columns]
    else:
        columns, specs = [hidden] * 3, [moving] * 3
    return pl.pallas_call(
        heavy_feed_split_kernel if split else heavy_feed_kernel,
        grid=(steps,),
        out_shape=[jax.ShapeDtypeStruct((slots, width), F32)] * 2
        + [jax.ShapeDtypeStruct((slots, c), BF16) for c in columns],
        in_specs=[
            fixed,
            fixed,
            pl.BlockSpec((width, part), lambda j: (0, j)),
            pl.BlockSpec((width, part), lambda j: (0, steps + j)),
            pl.BlockSpec((part, width), lambda j: (j, 0)),
        ],
        out_specs=[fixed] * 2 + specs,
        compiler_params=pltpu.CompilerParams(vmem_limit_bytes=24 * MIB),
        cost_estimate=estimate(12e-9 * slots * width * hidden, 20 << 20),
    )(rows_feed, grad_raw, heavy_expand, heavy_expand, heavy_reduce)


def light_feed(low, cotangent, light_expand, light_reduce, seq, deps):
    count, width = low.shape
    hidden = light_reduce.shape[0]
    part = hidden // 2
    fixed = pl.BlockSpec((count, width), lambda j: (0, 0))
    packed = (2, seq, width // seq, part + width // 4 + 64)
    return pl.pallas_call(
        without(light_feed_kernel, 5, len(deps)),
        grid=(2,),
        out_shape=[
            jax.ShapeDtypeStruct((count, width), F32),
            jax.ShapeDtypeStruct((count, width), F32),
            jax.ShapeDtypeStruct(packed, BF16),
            jax.ShapeDtypeStruct(packed, BF16),
        ],
        in_specs=[
            fixed,
            fixed,
            pl.BlockSpec((width, part), lambda j: (0, j)),
            pl.BlockSpec((width, part), lambda j: (0, 2 + j)),
            pl.BlockSpec((part, width), lambda j: (j, 0)),
        ]
        + [pl.BlockSpec(memory_space=pl.ANY)] * len(deps),
        out_specs=[fixed, fixed] + [pl.BlockSpec(packed, lambda j: (0, 0, 0, 0))] * 2,
        scratch_shapes=[pltpu.VMEM((4, count, width // 4), BF16)],
        compiler_params=pltpu.CompilerParams(vmem_limit_bytes=48 * MIB),
        cost_estimate=estimate(18e-9 * count * width * hidden, 20 << 20),
    )(low, cotangent, light_expand, light_expand, light_reduce, *deps)


def products_kernel(formers, latters, small, products):
    width = formers.shape[1] // 3
    quarter = width // 4
    offsets = ((0, 0, quarter), (1, quarter, quarter), (2, 2 * quarter, 2 * quarter))
    for part, start, columns in offsets:
        products[:, start : start + columns] = dot_left(
            formers[:, part * width : (part + 1) * width], latters[:, start : start + columns]
        ).astype(BF16)
    products[:, width:] = turn_small(small[...])


def outer_kernel(former, latter, product):
    product[...] = dot_left(former[...], latter[...]).astype(BF16)


def fold_kernel(kept, got, left, sent):
    total = (kept[...].astype(F32) + got[...].astype(F32)).astype(BF16)
    half = total.shape[1] // 2
    x = lax.axis_index("dp") // 2
    left[...] = jnp.where(x == 0, total[:, :half], total[:, half:])
    sent[...] = jnp.where(x == 0, total[:, half:], total[:, :half])


def expand_x_kernel(former, kept, got, sent, left):
    slots, width = former.shape
    half = kept.shape[1] // 2
    x = lax.axis_index("dp") // 2
    sent[:slots, :width] = former[...]
    sent[slots:, :width] = got[:, :width]
    for rows, source, base in ((slice(0, slots), kept, 0), (slice(slots, None), got, width)):
        gate, up = source[:, base : base + half], source[:, base + half : base + 2 * half]
        left[rows] = jnp.where(x == 0, gate, up)
        sent[rows, width:] = jnp.where(x == 0, up, gate)


def feed_y_kernel(
    sent_x, left, got, own, grad_raw, first, second, third, sent, expand_former, reduce_former
):
    slots, width = grad_raw.shape
    rows = 2 * slots
    y = lax.axis_index("seq") % 2
    part = width // 8
    for start, source in ((0, sent_x), (rows, got)):
        here = slice(start, start + rows)
        for i in range(4):
            even = source[:, 2 * i * part : (2 * i + 1) * part]
            odd = source[:, (2 * i + 1) * part : (2 * i + 2) * part]
            columns = slice(i * part, (i + 1) * part)
            expand_former[here, columns] = jnp.where(y == 0, even, odd)
            sent[here, columns] = jnp.where(y == 0, odd, even)
    base = 4 * part
    wide = left.shape[1]
    sent[:rows, base : base + wide] = left[...]
    sent[rows:, base : base + wide] = got[:, width:]
    base += wide
    half = own.shape[1] // 2
    for i, source in enumerate((own, first, second, third)):
        here = slice(i * slots, (i + 1) * slots)
        even, odd = source[:, :half], source[:, half : 2 * half]
        reduce_former[here] = jnp.where(y == 0, even, odd)
        sent[here, base : base + half] = jnp.where(y == 0, odd, even)
        latter = grad_raw[...] if i == 0 else source[:, 2 * half :]
        sent[here, base + half :] = latter


def feed_product_kernel(
    sent, got, expand_former, reduce_former, own, first, second, third, kept, moved, slices, turned
):
    base = expand_former.shape[1]
    wide = own.shape[1]
    product = dot_left(expand_former[...], sent[:, base : base + wide])
    product += dot_left(got[:, :base], got[:, base : base + wide])
    part = own.shape[0]
    for i in range(4):
        slices[i] = product[i * part : (i + 1) * part].astype(BF16)
    z = lax.axis_index("seq") // 2
    for step, ref in enumerate((own, first, second, third)):
        ref[...] = slices[(z + step) % 4]
    base += wide
    half = reduce_former.shape[1]
    quarter = (sent.shape[1] - base - half) // 4
    for index, source in enumerate((sent, got)):
        for spot, i in enumerate((0, 2, 1, 3)):
            start = base + half + i * quarter
            turned[index, :, spot * quarter : (spot + 1) * quarter] = source[
                :, start : start + quarter
            ]
    product = dot_left(reduce_former[...], turned[0])
    product += dot_left(got[:, base : base + half], turned[1])
    core = lax.axis_index("dp") % 2
    low, high = product[:, : 2 * quarter], product[:, 2 * quarter :]
    kept[...] = jnp.where(core == 0, low, high).astype(BF16)
    moved[...] = jnp.where(core == 0, high, low).astype(BF16)


def heavy_core_kernel(
    rows_query, scaled, rows_keyval, grad_query, grad_rows, grad_keyval, sent, kept
):
    width = rows_query.shape[1]
    quarter = width // 4
    sent[:, :width] = rows_query[...]
    sent[:, width : 2 * width] = scaled[...]
    sent[:, 2 * width : 3 * width] = rows_keyval[...]
    core = lax.axis_index("dp") % 2
    for x in range(2):
        spot = x * width
        for source, columns in ((grad_query, quarter), (grad_rows, quarter), (grad_keyval, 2 * quarter)):
            even = source[:, 2 * x * columns : (2 * x + 1) * columns]
            odd = source[:, (2 * x + 1) * columns : (2 * x + 2) * columns]
            kept[:, spot : spot + columns] = jnp.where(core == 0, even, odd)
            sent[:, 3 * width + spot : 3 * width + spot + columns] = jnp.where(core == 0, odd, even)
            spot += columns


def heavy_x_kernel(sent_core, kept, got, sent, left):
    slots = kept.shape[0]
    width = kept.shape[1] // 2
    former = 3 * width
    x = lax.axis_index("dp") // 2
    sent[:slots, :former] = sent_core[:, :former]
    sent[slots:, :former] = got[:, :former]
    for rows, source, base in ((slice(0, slots), kept, 0), (slice(slots, None), got, former)):
        low, high = source[:, base : base + width], source[:, base + width : base + 2 * width]
        left[rows] = jnp.where(x == 0, low, high)
        sent[rows, former:] = jnp.where(x == 0, high, low)


def pair_x_kernel(kept, got, left, sent):
    x = lax.axis_index("dp") // 2
    left[...] = (kept[x].astype(F32) + got[x].astype(F32)).astype(BF16)
    sent[...] = (kept[1 - x].astype(F32) + got[1 - x].astype(F32)).astype(BF16)


def pair_y_kernel(left, got, kept, sent):
    y = lax.axis_index("seq") % 2
    for i in range(4):
        mine, other = 2 * i + y, 2 * i + 1 - y
        kept[i] = (left[mine].astype(F32) + got[mine].astype(F32)).astype(BF16)
        sent[i] = (left[other].astype(F32) + got[other].astype(F32)).astype(BF16)


def pair_z_kernel(kept, got, own, first, second, third):
    z = lax.axis_index("seq") // 2
    for step, ref in enumerate((own, first, second, third)):
        spot = (z + step) % 4
        ref[...] = (kept[spot].astype(F32) + got[spot].astype(F32)).astype(BF16)


def heavy_y_kernel(heavy_sent, heavy_left, heavy_got, small, kept, sent, total):
    width = heavy_left.shape[1]
    quarter = width // 4
    for part, start, columns in ((0, 0, quarter), (1, quarter, quarter), (2, 2 * quarter, 2 * quarter)):
        former = slice(part * width, (part + 1) * width)
        product = dot_left(heavy_sent[:, former], heavy_left[:, start : start + columns])
        product += dot_left(
            heavy_got[:, former], heavy_got[:, 3 * width + start : 3 * width + start + columns]
        )
        total[:, start : start + columns] = product.astype(BF16)
    total[:, width:] = turn_small(small[...])
    y = lax.axis_index("seq") % 2
    rows = width // 8
    for i in range(4):
        even = total[2 * i * rows : (2 * i + 1) * rows]
        odd = total[(2 * i + 1) * rows : (2 * i + 2) * rows]
        kept[i] = jnp.where(y == 0, even, odd)
        sent[i] = jnp.where(y == 0, odd, even)


def turn_small(small):
    high = small.astype(BF16)
    low = (small - high.astype(F32)).astype(BF16)
    same = (
        lax.broadcasted_iota(jnp.int32, (small.shape[0], 128), 0)
        == lax.broadcasted_iota(jnp.int32, (small.shape[0], 128), 1)
    ).astype(BF16)
    return (dot_left(high, same) + dot_left(low, same)).astype(BF16)


def total_of(blocks):
    total = blocks[0][...].astype(F32)
    for block in blocks[1:]:
        total = total + block[...].astype(F32)
    return total


def light_end_kernel(own, first, second, third, query, keyval, output):
    total = total_of((own, first, second, third))
    quarter = query.shape[1]
    keyval[...] = total[:, : 2 * quarter]
    query[...] = total[:, 2 * quarter : 3 * quarter]
    output[...] = total[:, 3 * quarter :]


def heavy_end_kernel(own, first, second, third, query, keyval, output, small):
    total = total_of((own, first, second, third))
    quarter = query.shape[1]
    query[...] = total[:, :quarter]
    output[...] = total[:, quarter : 2 * quarter]
    keyval[...] = total[:, 2 * quarter : 4 * quarter]
    same = (
        lax.broadcasted_iota(jnp.int32, (8, 128), 0)
        == lax.broadcasted_iota(jnp.int32, (8, 128), 1)
    ).astype(F32)
    small[...] = lax.dot_general(
        same,
        total[:, 4 * quarter :],
        (((1,), (1,)), ((), ())),
        preferred_element_type=F32,
        precision=HIGHEST,
    )


def feed_end_kernel(own, first, second, third, expand, reduce):
    total = total_of((own, first, second, third))
    hidden, quarter = expand.shape[1], reduce.shape[1]
    rows = total.shape[0]
    more = rows // 3
    expand[...] = total[:, :hidden]
    reduce[:rows] = total[:, hidden : hidden + quarter]
    for piece in range(3):
        reduce[rows:, piece * 64 : (piece + 1) * 64] = total[
            piece * more : (piece + 1) * more, hidden + quarter :
        ]


def stages(count):
    found, stride = [], 1
    while count > 1:
        size = 4 if count % 4 == 0 and count != 8 else 2
        found.append((size, stride))
        stride, count = stride * size, count // size
    return found


def shifted(block, axis, size, stride, step):
    route = []
    for i in range(lax.axis_size(axis)):
        member = (i // stride) % size
        route.append((i, i + ((member + step) % size - member) * stride))
    return lax.ppermute(block, axis, route)


def neighbours(block, distance):
    devices = range(lax.axis_size("seq"))
    return lax.ppermute(
        block, "seq", [(i - distance, i) for i in devices if i - distance in devices]
    )


def member_of(axis, size, stride):
    return (lax.axis_index(axis) // stride) % size


def pick(block, index, dim):
    return lax.dynamic_index_in_dim(block, index, dim, keepdims=False)


def reduce_stage(block, axis, size, stride, dim):
    me = member_of(axis, size, stride)
    total = pick(block, me, dim).astype(F32)
    for step in range(1, size):
        sent = pick(block, (me + step) % size, dim)
        total = total + shifted(sent, axis, size, stride, step).astype(F32)
    return total.astype(BF16)


def reduce_dp(block):
    block = reduce_stage(block, "dp", 2, 1, 0)
    half = block.shape[1] // 2
    first, second = block[:, :half], block[:, half:]
    x = member_of("dp", 2, 2)
    got = shifted(jnp.where(x == 0, second, first), "dp", 2, 2, 1)
    return (jnp.where(x == 0, first, second).astype(F32) + got.astype(F32)).astype(BF16)


def reduce_seq(block, skip=0):
    for size, stride in stages(lax.axis_size("seq"))[skip:]:
        count = lax.axis_size("seq") // stride
        block = block.reshape(count // size, size, block.shape[0] // count, block.shape[1])
        block = reduce_stage(block, "seq", size, stride, 1)
        block = block.reshape(-1, block.shape[-1])
    return block


def gather_part(block, size, stride):
    return jnp.concatenate(
        [block] + [shifted(block, "seq", size, stride, step) for step in range(1, size)], 0
    )


def gather_seq(block):
    for size, stride in stages(lax.axis_size("seq"))[::-1]:
        block = gather_part(block, size, stride)
    return block


def total_parts(parts):
    total = parts[0].astype(F32)
    for part in parts[1:]:
        total = total + part.astype(F32)
    return total


def reduce_pair(kept, sent):
    block = (kept.astype(F32) + shifted(sent, "dp", 2, 1, 1).astype(F32)).astype(BF16)
    return reduce_stage(block, "dp", 2, 2, 0).reshape(-1, block.shape[3])


def swap_rows(axis, stride, whole, mine, other):
    got = shifted(jnp.concatenate([whole, other], 1), axis, 2, stride, 1)
    width = whole.shape[1]
    return (
        jnp.concatenate([whole, got[:, :width]], 0),
        jnp.concatenate([mine, got[:, width:]], 0),
    )


def gather_dp(former, first, second):
    core, x = member_of("dp", 2, 1), member_of("dp", 2, 2)
    half = first.shape[1] // 2

    def both(low, high):
        return jnp.concatenate([low, high], 1)

    lows = both(first[:, :half], second[:, :half])
    highs = both(first[:, half:], second[:, half:])
    former, latter = swap_rows(
        "dp", 1, former, jnp.where(core == 0, lows, highs), jnp.where(core == 0, highs, lows)
    )
    low, high = latter[:, :half], latter[:, half:]
    return swap_rows(
        "dp", 2, former, jnp.where(x == 0, low, high), jnp.where(x == 0, high, low)
    )


def split_rows(former, latter, size, stride):
    rows, width = former.shape
    count = lax.axis_size("seq") // stride
    former = former.reshape(rows, count // size, size, width // count)
    me = member_of("seq", size, stride)
    formers, latters = [pick(former, me, 2).reshape(rows, width // size)], [latter]
    for step in range(1, size):
        other = pick(former, (me + step) % size, 2).reshape(rows, width // size)
        got = shifted(jnp.concatenate([other, latter], 1), "seq", size, stride, step)
        formers.append(got[:, : width // size])
        latters.append(got[:, width // size :])
    return jnp.concatenate(formers, 0), jnp.concatenate(latters, 0)


def outer(former, latter):
    rows, width = former.shape
    columns = latter.shape[1]
    return run(
        outer_kernel, [((width, columns), BF16)], [former, latter], 24, 2e-9 * rows * width * columns
    )[0]


def expand_gradient(former, gate, up):
    former, latter = gather_dp(former, gate, up)
    size, stride = stages(lax.axis_size("seq"))[0]
    former, latter = split_rows(former, latter, size, stride)
    return reduce_seq(outer(former, latter), 1)


def reduce_gradient(former, latter):
    for size, stride in stages(lax.axis_size("seq")):
        former, latter = split_rows(former, latter, size, stride)
    quarter = latter.shape[1] // 4
    parts = [latter[:, i * quarter : (i + 1) * quarter] for i in (0, 2, 1, 3)]
    product = outer(former, jnp.concatenate(parts, 1))
    half = product.shape[1] // 2
    return reduce_dp(jnp.stack([product[:, :half], product[:, half:]]))


def sum_dp(block):
    for stride in (1, 2):
        block = block + shifted(block, "dp", 2, stride, 1)
    return block


def pair_x(kept, sent, deps=()):
    got = shifted(sent, "dp", 2, 1, 1)
    left, sent = run(pair_x_kernel, [(kept.shape[1:], BF16)] * 2, [kept, got], 24, deps=deps)
    return left, sent, shifted(sent, "dp", 2, 2, 1)


def pair_y(left, got, deps=()):
    shape = (4,) + left.shape[1:]
    kept, sent = run(pair_y_kernel, [(shape, BF16)] * 2, [left, got], 16, deps=deps)
    return kept, sent, shifted(sent, "seq", 2, 1, 1)


def pair_z(kept, got, deps=()):
    own, *sent = run(pair_z_kernel, [(kept.shape[1:], BF16)] * 4, [kept, got], 16, deps=deps)
    return [own] + [shifted(block, "seq", 4, 2, 1 + i) for i, block in enumerate(sent)]


def send_feed(rows_feed, grad_raw, parts):
    kept, sent, own, *moved = parts
    slots, width = rows_feed.shape
    wide = kept.shape[1] // 2
    got = shifted(sent, "dp", 2, 1, 1)
    moved = [shifted(block, "seq", 4, 2, 1 + i) for i, block in enumerate(moved)]
    sent, left = run(
        expand_x_kernel,
        [((2 * slots, width + wide), BF16), ((2 * slots, wide), BF16)],
        [rows_feed, kept, got],
        16,
    )
    return sent, left, shifted(sent, "dp", 2, 2, 1), own, grad_raw, moved


def send_feed_y(sent, left, got, own, grad_raw, moved):
    slots, width = grad_raw.shape
    wide, half = left.shape[1], own.shape[1] // 2
    sent, expand_former, reduce_former = run(
        feed_y_kernel,
        [
            ((4 * slots, width // 2 + wide + half + width), BF16),
            ((4 * slots, width // 2), BF16),
            ((4 * slots, half), BF16),
        ],
        [sent, left, got, own, grad_raw] + moved,
        16,
    )
    return sent, expand_former, reduce_former, shifted(sent, "seq", 2, 1, 1)


def end_feed(sent, expand_former, reduce_former, got, deps):
    width = 2 * expand_former.shape[1]
    rows, half = width // 8, reduce_former.shape[1]
    wide = sent.shape[1] - half - width - width // 2
    *expand, kept, sent = run(
        feed_product_kernel,
        [((rows, wide), BF16)] * 4 + [((half, width // 2), BF16)] * 2,
        [sent, got, expand_former, reduce_former],
        32,
        1.2,
        [pltpu.VMEM((4, rows, wide), BF16), pltpu.VMEM((2,) + (sent.shape[0], width), BF16)],
        deps=deps,
    )
    parts = [expand[0]] + [shifted(expand[1 + i], "seq", 4, 2, 1 + i) for i in range(3)]
    return parts, kept, sent


def send_heavy(rows_query, scaled, rows_keyval, grad_query, grad_rows, grad_keyval):
    slots, width = rows_query.shape
    sent, kept = run(
        heavy_core_kernel,
        [((slots, 5 * width), BF16), ((slots, 2 * width), BF16)],
        [rows_query, scaled, rows_keyval, grad_query, grad_rows, grad_keyval],
        16,
    )
    got = shifted(sent, "dp", 2, 1, 1)
    sent, left = run(
        heavy_x_kernel,
        [((2 * slots, 4 * width), BF16), ((2 * slots, width), BF16)],
        [sent, kept, got],
        16,
    )
    return sent, left, shifted(sent, "dp", 2, 2, 1)


def on_device(
    tokens,
    cotangent,
    document_bounds,
    routes,
    attention_gain,
    feedforward_gain,
    router,
    light_query,
    light_keyval,
    light_output,
    heavy_query,
    heavy_keyval,
    heavy_output_weight,
    light_expand,
    light_reduce,
    heavy_expand,
    heavy_reduce,
):
    count, width = tokens.shape
    slots = routes.shape[1]
    seq = lax.axis_size("seq")
    length = count * seq
    gain, feed_gain = attention_gain[None], feedforward_gain[None]
    heavy_width = heavy_query.shape[1]

    above = neighbours(tokens[count - WINDOW :], 1)
    below = neighbours(tokens[:WINDOW], -1)
    (packet,) = run(
        select_kernel,
        [((slots, width + 128), BF16)],
        [document_bounds, routes, tokens],
        8,
        0.1,
        smem=1,
    )
    gathered = gather_seq(packet)
    wide = LH * 128
    low, query, keyval, rows_query, rows_keyval, query_heavy, score_query = run(
        project_kernel,
        [
            ((count, width), BF16),
            ((count, wide), BF16),
            ((count, 2 * wide), BF16),
            ((slots, width), BF16),
            ((slots, width), BF16),
            ((slots, heavy_width), BF16),
            ((slots, 128), F32),
        ],
        [routes, tokens, gain, router, light_query, light_keyval, heavy_query],
        24,
        2.5,
    )
    span_rows = count + 2 * WINDOW
    attended, peaks, span_low, span = run(
        functools.partial(light_forward_kernel, length),
        [
            ((count, width), BF16),
            ((8, count), F32),
            ((span_rows, width), BF16),
            ((span_rows, 2 * wide), BF16),
        ],
        [document_bounds, query, keyval, low, above, below, gain, light_keyval],
        24,
        3.0,
        smem=1,
    )
    keyval_heavy, heavy_attended, heavy_scaled, heavy_peaks, own_values, score_keyval = run(
        functools.partial(heavy_forward_kernel, count),
        [
            ((seq * slots, 2 * heavy_width), BF16),
            ((slots, heavy_width), F32),
            ((slots, heavy_width), BF16),
            ((slots, 128), F32),
            ((slots, heavy_width), F32),
            ((slots, 128), F32),
        ],
        [document_bounds, routes, gathered, query_heavy, score_query, gain, router, heavy_keyval],
        24 if seq <= 8 else 48,
        2.0,
        smem=1,
    )
    residual, feed_low, rows_feed, score_feed, cotangent_rows, grad_raw = run(
        residual_kernel,
        [
            ((count, width), F32),
            ((count, width), BF16),
            ((slots, width), BF16),
            ((slots, 128), F32),
            ((slots, width), F32),
            ((slots, width), BF16),
        ],
        [
            routes, tokens, attended, light_output, heavy_scaled, heavy_output_weight, feed_gain,
            router, cotangent,
        ],
        24,
        1.5,
    )
    feed = heavy_feed(rows_feed, grad_raw, heavy_expand, heavy_reduce, seq)
    raw_feed, grad_rows = feed[:2]
    fast = seq == 8
    rows = width // seq
    if fast:
        moves = send_feed(rows_feed, grad_raw, feed[2:])
    light_result, grad_low, feed_kept, feed_sent = light_feed(
        feed_low, cotangent, light_expand, light_reduce, seq, [moves[0]] if fast else []
    )
    deps = []
    if fast:
        moves = send_feed_y(*moves)
        feed_left, feed_sent, feed_got = pair_x(feed_kept, feed_sent, [moves[0]])
        deps = [feed_sent]
    (
        output,
        grad_residual,
        grad_residual_low,
        grad_attended,
        grad_heavy_rows,
        grad_heavy_attended,
        logit_query,
        feed_small,
    ) = run(
        turn_kernel,
        [
            ((count, width), BF16),
            ((count, width), F32),
            ((count, width), BF16),
            ((count, width), BF16),
            ((slots, width), BF16),
            ((slots, heavy_width), BF16),
            ((slots, 128), F32),
            ((2, width), F32),
        ],
        [
            routes, residual, feed_gain, light_result, grad_low, raw_feed, grad_rows, score_feed,
            cotangent_rows, cotangent, router, light_output, heavy_output_weight, heavy_attended,
            score_query,
        ],
        32,
        1.5,
        deps=deps,
    )
    grad_heavy_query, packet = run(
        functools.partial(heavy_query_kernel, count),
        [((slots, heavy_width), BF16), ((slots, 2 * heavy_width + 128), BF16)],
        [
            document_bounds, routes, gathered, query_heavy, keyval_heavy, heavy_peaks,
            grad_heavy_attended,
        ],
        16 if seq <= 8 else 48,
        0.3,
        smem=1,
    )
    sums = [pltpu.VMEM((span_rows, wide // 2), F32)] * 2
    light_ins = [document_bounds, query, span, peaks, grad_attended, attended]
    first_query, first_span = run(
        functools.partial(light_first_kernel, length),
        [((count, width // 2), BF16), ((span_rows, width), BF16)],
        light_ins,
        24,
        2.5,
        sums,
        smem=1,
        deps=[packet],
    )
    packets, deps = gather_seq(packet), []
    if fast:
        packets = gather_part(packet, 4, 2)
        deps = [packets]
        packets = gather_part(packets, 2, 1)
        feed_kept, feed_sent, feed_got = pair_y(feed_left, feed_got, [first_query])
        deps.append(feed_sent)
    second_query, second_span, grad_above, grad_below = run(
        functools.partial(light_second_kernel, length),
        [
            ((count, width // 2), BF16),
            ((span_rows, width), BF16),
            ((WINDOW, 2 * width), BF16),
            ((WINDOW, 2 * width), BF16),
        ],
        light_ins + [first_span],
        24,
        2.5,
        sums,
        smem=1,
        deps=deps,
    )
    from_above = neighbours(grad_above, -1)
    from_below = neighbours(grad_below, 1)
    deps = []
    if fast:
        expand_parts, reduce_kept, reduce_sent = end_feed(*moves, [second_query])
        feed_parts = pair_z(feed_kept, feed_got, [second_query])
        deps = [reduce_sent, feed_parts[0]]
    mixer_kept, mixer_sent = run(
        light_products_kernel,
        [((2, width, width), BF16)] * 2,
        [
            span_low, first_query, second_query, first_span, second_span, attended,
            grad_residual_low,
        ],
        24,
        4.0,
        deps=deps,
    )
    shape = (2, seq, rows, width)
    mixer_kept, mixer_sent = mixer_kept.reshape(shape), mixer_sent.reshape(shape)
    deps = []
    if fast:
        mixer_left, mixer_sent, mixer_got = pair_x(mixer_kept, mixer_sent)
        deps = [mixer_sent]
        half = reduce_kept.shape[1] // 2
        shape = (2, reduce_kept.shape[0], half)
        got = shifted(reduce_sent, "dp", 2, 1, 1)
        left, sent = run(fold_kernel, [(shape[1:], BF16)] * 2, [reduce_kept, got], 8)
        reduce_got = shifted(sent, "dp", 2, 2, 1)
        grad_heavy_reduce = left.astype(F32) + reduce_got.astype(F32)
    grad_raw_keyval, logit_keyval = run(
        functools.partial(heavy_key_kernel, count),
        [((slots, 2 * heavy_width), BF16), ((slots, 128), F32)],
        [document_bounds, routes, packets, keyval_heavy[:slots], own_values, score_keyval],
        16 if seq <= 8 else 48,
        0.3,
        smem=1,
        deps=deps,
    )
    deps = []
    if fast:
        heavy_sent, heavy_left, heavy_got = send_heavy(
            rows_query, heavy_scaled, rows_keyval, grad_heavy_query, grad_heavy_rows, grad_raw_keyval
        )
        deps = [heavy_sent]
    tokens_grad, small = run(
        mixer_kernel,
        [((count, width), BF16), ((8, width), F32)],
        [
            routes, tokens, gain, router, grad_residual, first_query, second_query, first_span,
            second_span, from_below, from_above, grad_heavy_query, grad_raw_keyval, logit_query,
            logit_keyval, light_query, light_keyval, heavy_query, heavy_keyval, feed_small,
        ],
        40,
        3.0,
        [pltpu.VMEM((count, 2 * width), BF16)],
        deps=deps,
    )
    small = sum_dp(small)
    quarter = width // 4
    hidden = light_reduce.shape[0] // 2
    if fast:
        kept, sent, got = pair_y(mixer_left, mixer_got)
        light_parts = pair_z(kept, got)
        kept, sent = run(
            heavy_y_kernel,
            [((4, rows, width + 128), BF16)] * 2,
            [heavy_sent, heavy_left, heavy_got, small],
            16,
            0.7,
            [pltpu.VMEM((width, width + 128), BF16)],
            deps=[light_parts[0]],
        )
        got = shifted(sent, "seq", 2, 1, 1)
        heavy_parts = pair_z(kept, got)
        grad_light_expand, grad_light_reduce = run(
            feed_end_kernel,
            [((rows, hidden), F32), ((light_reduce.shape[0] // seq, quarter), F32)],
            feed_parts,
            8,
        )
        grad_heavy_expand = total_parts(expand_parts)
        grad_light_query, grad_light_keyval, grad_light_output = run(
            light_end_kernel,
            [((rows, quarter), F32), ((rows, 2 * quarter), F32), ((rows, quarter), F32)],
            light_parts,
            8,
        )
        grad_heavy_query, grad_heavy_keyval, grad_heavy_output, small = run(
            heavy_end_kernel,
            [
                ((rows, quarter), F32),
                ((rows, 2 * quarter), F32),
                ((rows, quarter), F32),
                ((8, rows), F32),
            ],
            heavy_parts,
            8,
        )
        smalls = (small[0], small[1], small[2:5])
    else:
        gated_heavy, grad_gate, grad_up = feed[2:]
        grad_heavy_expand = expand_gradient(rows_feed, grad_gate, grad_up).astype(F32)
        grad_heavy_reduce = reduce_gradient(gated_heavy, grad_raw).astype(F32)
        formers = jnp.concatenate([rows_query, heavy_scaled, rows_keyval], 1)

        def mine(part):
            low_columns = slice(part * quarter, (part + 1) * quarter)
            high_columns = slice(2 * part * quarter, 2 * (part + 1) * quarter)
            return [
                grad_heavy_query[:, low_columns],
                grad_heavy_rows[:, low_columns],
                grad_raw_keyval[:, high_columns],
            ]

        first = jnp.concatenate(mine(0) + mine(1), 1)
        second = jnp.concatenate(mine(2) + mine(3), 1)
        formers, latters = gather_dp(formers, first, second)
        (heavy_products,) = run(
            products_kernel,
            [((width, width + 128), BF16)],
            [formers, latters, small],
            16,
            0.6,
        )
        heavy = reduce_seq(heavy_products).astype(F32)
        light = reduce_seq(reduce_pair(mixer_kept, mixer_sent)).astype(F32)
        packed = reduce_seq(reduce_pair(feed_kept, feed_sent)).astype(F32)
        grad_light_query = light[:, 2 * quarter : 3 * quarter]
        grad_light_keyval = light[:, : 2 * quarter]
        grad_light_output = light[:, 3 * quarter :]
        grad_light_expand = packed[:, :hidden]
        rest = packed[:, hidden + quarter :].reshape(3, rows // 3, 64)
        rest = rest.transpose(1, 0, 2).reshape(rows // 3, quarter)
        grad_light_reduce = jnp.concatenate([packed[:, hidden : hidden + quarter], rest], 0)
        grad_heavy_query = heavy[:, :quarter]
        grad_heavy_output = heavy[:, quarter : 2 * quarter]
        grad_heavy_keyval = heavy[:, 2 * quarter : 4 * quarter]
        smalls = (heavy[:, width], heavy[:, width + 1], heavy[:, width + 2 : width + 5].T)
    return (
        output,
        tokens_grad,
        *smalls,
        grad_light_query,
        grad_light_keyval,
        grad_light_output,
        grad_heavy_query,
        grad_heavy_keyval,
        grad_heavy_output,
        grad_light_expand,
        grad_light_reduce,
        grad_heavy_expand,
        grad_heavy_reduce,
    )


def solution(mesh):
    whole, rows = P(), P(("dp", "seq"), None)
    return jax.shard_map(
        on_device,
        mesh=mesh,
        in_specs=(rows, rows, whole, P(None, ("dp", "seq"))) + (whole,) * 13,
        out_specs=(rows, rows, P("seq"), P("seq"), P(None, "seq")) + (P("seq", "dp"),) * 10,
        check_vma=False,
    )
```

```python
import functools
import math

import jax
import jax.numpy as jnp
from jax import lax
from jax.experimental import pallas as pl
from jax.experimental.pallas import tpu as pltpu
from jax.sharding import PartitionSpec as P

LH = 8
HHS = 64
WINDOW = 128
EPSILON = 1e-06
MASKED = -1e30
HIGHEST = lax.Precision.HIGHEST
F32, BF16 = jnp.float32, jnp.bfloat16
MIB = 1 << 20
LONG = 60


def dot(former, latter):
    return jnp.dot(former, latter, preferred_element_type=F32)


def dot_left(former, latter):
    return lax.dot_general(former, latter, (((0,), (0,)), ((), ())), preferred_element_type=F32)


def dot_right(former, latter):
    return lax.dot_general(former, latter, (((1,), (1,)), ((), ())), preferred_element_type=F32)


def dot_exact(former, latter):
    return jnp.dot(former, latter, preferred_element_type=F32, precision=HIGHEST)


def column_of(row):
    count = row.shape[1]
    same = lax.broadcasted_iota(jnp.int32, (count, count), 0) == lax.broadcasted_iota(
        jnp.int32, (count, count), 1
    )
    return jnp.sum(jnp.where(same, row.astype(F32), 0.0), axis=1, keepdims=True)


def slots_by_tokens(route_row, tokens):
    column = column_of(route_row).astype(jnp.int32)
    lanes = lax.broadcasted_iota(jnp.int32, (route_row.shape[1], tokens), 1)
    return (column == lanes).astype(F32)


def tokens_by_slots(route_row, tokens):
    rows = lax.broadcasted_iota(jnp.int32, (tokens, route_row.shape[1]), 0)
    return (rows == route_row).astype(F32)


def normed(rows, gain):
    return rows * lax.rsqrt(jnp.mean(rows * rows, -1, keepdims=True) + EPSILON) * gain


def norm_back(rows, gain, grad):
    inverse = lax.rsqrt(jnp.mean(rows * rows, -1, keepdims=True) + EPSILON)
    plain = rows * inverse
    scaled = grad * gain
    inner = jnp.mean(scaled * plain, -1, keepdims=True)
    return inverse * (scaled - plain * inner), jnp.sum(grad * plain, 0, keepdims=True)


def sigmoid(value):
    return 1.0 / (1.0 + jnp.exp(-value))


def segment(place, first, last):
    return (place >= first).astype(F32) + (place >= last).astype(F32)


def gelu_parts(value):
    slope = math.sqrt(2.0 / math.pi)
    square = value * value
    bent = jnp.tanh(slope * value * (1.0 + 0.044715 * square))
    half = 0.5 * (1.0 + bent)
    rise = half + 0.5 * value * (1.0 - bent * bent) * slope * (1.0 + 3 * 0.044715 * square)
    return value * half, rise


def place(tok_rows, bounds):
    lead = lax.axis_index("seq") * tok_rows
    group = lax.axis_index("dp")
    return lead, bounds[group, 0], bounds[group, 1]


def select_kernel(bounds, routes, tokens, packet):
    count, width = tokens.shape
    lead, first, last = place(count, bounds)
    row = routes[1:2, :]
    chosen = slots_by_tokens(row, count).astype(BF16)
    packet[:, :width] = dot(chosen, tokens[...]).astype(BF16)
    column = column_of(row)
    tag = jnp.where(column >= 0, segment(column.astype(jnp.int32) + lead, first, last), -1.0)
    packet[:, width:] = jnp.broadcast_to(tag, (tag.shape[0], 128)).astype(BF16)


def project_kernel(
    routes, tokens, gain, router, light_query, light_keyval, heavy_query,
    low, query, keyval, rows_query, rows_keyval, query_heavy, score_query,
):
    count = tokens.shape[0]
    width = tokens.shape[1]
    low[...] = normed(tokens[...].astype(F32), gain[...]).astype(BF16)
    widen(query, slice(None), 0, dot(low[...], light_query[...]).astype(BF16), 0.0)
    pair = dot(low[...], light_keyval[...]).astype(BF16)
    widen(keyval, slice(None), 0, pair[:, :width], 0.0)
    widen(keyval, slice(None), LH * 128, pair[:, width:], 1.0)
    chosen = slots_by_tokens(routes[0:1, :], count).astype(BF16)
    raw = dot(chosen, tokens[...])
    rows = normed(raw, gain[...])
    logit = jnp.sum(rows * router[0:1, :], -1, keepdims=True)
    score_query[...] = jnp.broadcast_to(sigmoid(logit), score_query.shape)
    rows_query[...] = dot(chosen, low[...]).astype(BF16)
    query_heavy[...] = dot(rows_query[...], heavy_query[...]).astype(BF16)
    chosen = slots_by_tokens(routes[1:2, :], count).astype(BF16)
    rows_keyval[...] = dot(chosen, low[...]).astype(BF16)


def widen(ref, rows, start, value, filler):
    size = value.shape[1] // LH
    rest = jnp.full((value.shape[0], 128 - size), filler, BF16)
    for head in range(LH):
        base = start + head * 128
        ref[rows, base : base + size] = value[:, head * size : (head + 1) * size]
        ref[rows, base + size : base + 128] = rest


def light_mask(tok_rows, length, bounds, step):
    lead, first, last = place(tok_rows, bounds)
    shape = (3 * WINDOW, WINDOW)
    query_place = lead + step * WINDOW + lax.broadcasted_iota(jnp.int32, shape, 1)
    key_place = lead + (step - 1) * WINDOW + lax.broadcasted_iota(jnp.int32, shape, 0)
    allowed = (key_place >= 0) & (key_place < length)
    allowed = allowed & (jnp.abs(query_place - key_place) <= WINDOW)
    return allowed & (segment(query_place, first, last) == segment(key_place, first, last))


def light_forward_kernel(
    length, bounds, query, keyval, low, above, below, gain, light_keyval,
    attended, peaks, span_low, span,
):
    tok_rows, width = low.shape
    size = width // LH
    values_start = LH * 128
    scale = size ** (-0.5) / math.log(2.0)
    own = slice(WINDOW, WINDOW + tok_rows)
    span_low[own] = low[...]
    span[own] = keyval[...]
    for rows, signal in ((slice(0, WINDOW), above), (slice(WINDOW + tok_rows, None), below)):
        span_low[rows] = normed(signal[...].astype(F32), gain[...]).astype(BF16)
        pair = dot(span_low[rows], light_keyval[...]).astype(BF16)
        widen(span, rows, 0, pair[:, :width], 0.0)
        widen(span, rows, values_start, pair[:, width:], 1.0)
    for step in range(tok_rows // WINDOW):
        rows = slice(step * WINDOW, (step + 1) * WINDOW)
        keys = slice(step * WINDOW, (step + 3) * WINDOW)
        allowed = light_mask(tok_rows, length, bounds, step)
        for head in range(LH):
            wide = slice(head * 128, (head + 1) * 128)
            values = slice(values_start + head * 128, values_start + (head + 1) * 128)
            scores = jnp.where(allowed, dot_right(span[keys, wide], query[rows, wide]), MASKED)
            peak = jnp.max(scores, 0, keepdims=True)
            exponent = jnp.exp2((scores - peak) * scale)
            total = jnp.sum(exponent, 0, keepdims=True)
            result = dot_left(exponent.astype(BF16), span[keys, values])
            result = result[:, :size] * (1.0 / result[:, size : size + 1])
            attended[rows, head * size : (head + 1) * size] = result.astype(BF16)
            peaks[head : head + 1, rows] = peak * scale + jnp.log2(total)


def light_half(
    half, length, bounds, query, span, peaks, grad, attended, grad_query, grad_keys, grad_values,
):
    tok_rows, width = grad.shape
    size = width // LH
    heads = LH // 2
    scale = size ** (-0.5) / math.log(2.0)
    lanes = slice(half * heads * size, (half + 1) * heads * size)
    product = grad[:, lanes].astype(F32) * attended[:, lanes].astype(F32)
    high = product.astype(BF16)
    rest = (product - high.astype(F32)).astype(BF16)
    shape = (8, heads * size)
    column = lax.broadcasted_iota(jnp.int32, shape, 1)
    row = lax.broadcasted_iota(jnp.int32, shape, 0)
    pickers = ((column >= row * size) & (column < (row + 1) * size)).astype(BF16)
    inners = dot_right(pickers, high) + dot_right(pickers, rest)
    grad_keys[...] = jnp.zeros_like(grad_keys)
    grad_values[...] = jnp.zeros_like(grad_values)
    for step in range(tok_rows // WINDOW):
        rows = slice(step * WINDOW, (step + 1) * WINDOW)
        keys = slice(step * WINDOW, (step + 3) * WINDOW)
        allowed = light_mask(tok_rows, length, bounds, step)
        for index in range(heads):
            head = half * heads + index
            wide = slice(head * 128, (head + 1) * 128)
            start = LH * 128 + head * 128
            here = slice(index * 128, (index + 1) * 128)
            columns = slice(head * size, (head + 1) * size)
            scores = dot_right(span[keys, wide], query[rows, wide]) * scale
            weights = jnp.exp2(
                jnp.where(allowed, scores, MASKED) - peaks[head : head + 1, rows]
            )
            given = grad[rows, columns]
            grad_weights = dot_right(span[keys, start : start + size], given)
            inner = inners[index : index + 1, rows]
            grad_scores = (weights * (grad_weights - inner)).astype(BF16)
            result = dot_left(grad_scores, span[keys, wide])[:, :size] * size ** (-0.5)
            grad_query[rows, index * size : (index + 1) * size] = result.astype(BF16)
            grad_keys[keys, here] += dot(grad_scores, query[rows, wide])
            grad_values[keys, index * 128 : index * 128 + size] += dot(weights.astype(BF16), given)


def narrow(grad_span, grad_keys, grad_values):
    half = grad_span.shape[1] // 2
    size = 2 * half // LH
    for head in range(LH // 2):
        here = slice(head * 128, head * 128 + size)
        columns = slice(head * size, (head + 1) * size)
        grad_span[:, columns] = (grad_keys[:, here] * size ** (-0.5)).astype(BF16)
        columns = slice(half + head * size, half + (head + 1) * size)
        grad_span[:, columns] = grad_values[:, here].astype(BF16)


def light_first_kernel(
    length, bounds, query, span, peaks, grad, attended, grad_query, grad_span, grad_keys, grad_values
):
    light_half(
        0, length, bounds, query, span, peaks, grad, attended, grad_query, grad_keys, grad_values
    )
    narrow(grad_span, grad_keys, grad_values)


def light_second_kernel(
    length, bounds, query, span, peaks, grad, attended, first_span,
    grad_query, grad_span, grad_above, grad_below, grad_keys, grad_values,
):
    light_half(
        1, length, bounds, query, span, peaks, grad, attended, grad_query, grad_keys, grad_values
    )
    narrow(grad_span, grad_keys, grad_values)
    half = grad_span.shape[1] // 2
    count = grad_span.shape[0]
    for ref, rows in ((grad_above, slice(0, WINDOW)), (grad_below, slice(count - WINDOW, count))):
        ref[:, :half] = first_span[rows, :half]
        ref[:, half : 2 * half] = grad_span[rows, :half]
        ref[:, 2 * half : 3 * half] = first_span[rows, half:]
        ref[:, 3 * half :] = grad_span[rows, half:]


def light_products_kernel(
    span_low, first_query, second_query, first_span, second_span, attended, grad_residual, kept, sent
):
    tok_rows, width = attended.shape
    quarter = width // 4
    half = width // 2
    core = lax.axis_index("dp") % 2
    own = slice(WINDOW, WINDOW + tok_rows)
    for part in range(4):
        grad_span = (first_span, second_span)[part % 2]
        columns = slice((part // 2) * half, (part // 2 + 1) * half)
        keyval_part = dot_left(span_low[...], grad_span[:, columns]).astype(BF16)
        grad_query = (first_query, second_query)[part // 2]
        columns = slice((part % 2) * quarter, (part % 2 + 1) * quarter)
        query_part = dot_left(span_low[own], grad_query[:, columns]).astype(BF16)
        columns = slice(part * quarter, (part + 1) * quarter)
        output_part = dot_left(attended[...], grad_residual[:, columns]).astype(BF16)
        for ref, chosen in ((kept, core == part % 2), (sent, core != part % 2)):

            @pl.when(chosen)
            def _(ref=ref, x=part // 2, parts=(keyval_part, query_part, output_part)):
                ref[x, :, : 2 * quarter] = parts[0]
                ref[x, :, 2 * quarter : 3 * quarter] = parts[1]
                ref[x, :, 3 * quarter :] = parts[2]


def heavy_forward_kernel(
    count, bounds, routes, gathered, query_heavy, score_query, gain, router, heavy_keyval,
    keyval, attended, scaled, peaks, own_values, score_keyval,
):
    width = query_heavy.shape[1]
    slots = query_heavy.shape[0]
    total_rows = gathered.shape[0]
    part = min(512, total_rows)
    for start in range(0, total_rows, part):
        rows = slice(start, start + part)
        signal = normed(gathered[rows, :width].astype(F32), gain[...])
        logit = jnp.sum(signal * router[1:2, :], -1, keepdims=True)
        score = sigmoid(logit)
        raw = dot(signal.astype(BF16), heavy_keyval[...])
        keyval[rows, :width] = raw[:, :width].astype(BF16)
        keyval[rows, width:] = (score * raw[:, width:]).astype(BF16)
        if start == 0:
            own_values[...] = raw[:slots, width:]
            score_keyval[...] = jnp.broadcast_to(score[:slots], score_keyval.shape)
    allowed = heavy_mask(count, bounds, routes, gathered, width)
    lanes = lax.broadcasted_iota(jnp.int32, (slots, 128), 1)
    kept = jnp.zeros((slots, 128), F32)
    for head in range(width // HHS):
        columns = slice(head * HHS, (head + 1) * HHS)
        values = slice(width + head * HHS, width + (head + 1) * HHS)
        scores = dot_right(query_heavy[:, columns], keyval[:, columns]) * HHS ** (-0.5)
        scores = jnp.where(allowed, scores, MASKED)
        peak = jnp.max(scores, -1, keepdims=True)
        exponent = jnp.where(allowed, jnp.exp(scores - peak), 0.0)
        total = jnp.sum(exponent, -1, keepdims=True)
        total = jnp.where(total > 0, total, 1.0)
        weights = (exponent * (1.0 / total)).astype(BF16)
        result = dot(weights, keyval[:, values])
        attended[:, columns] = result
        scaled[:, columns] = (score_query[:, :1] * result).astype(BF16)
        kept = jnp.where(lanes == head, peak + jnp.log(total), kept)
    peaks[...] = kept


def heavy_mask(count, bounds, routes, gathered, width):
    lead, first, last = place(count, bounds)
    pickers = (lax.broadcasted_iota(jnp.int32, (8, 128), 1) == 0).astype(BF16)
    key_segment = dot_right(pickers, gathered[:, width:])[:1]
    return own_segment(routes, lead, first, last) == key_segment


def own_segment(routes, lead, first, last):
    column = column_of(routes[0:1, :])
    spot = jnp.where(column >= 0, column.astype(jnp.int32) + lead, -1)
    return segment(spot, first, last)


def residual_kernel(
    routes, tokens, attended, light_output, scaled, heavy_output, gain, router, cotangent,
    residual, low, rows_feed, score_feed, cotangent_rows, grad_raw,
):
    count = tokens.shape[0]
    spread = tokens_by_slots(routes[0:1, :], count).astype(BF16)
    scattered = dot(spread, scaled[...]).astype(BF16)
    residual[...] = (
        tokens[...].astype(F32)
        + dot(attended[...], light_output[...])
        + dot(scattered, heavy_output[...])
    )
    signal = normed(residual[...], gain[...])
    low[...] = signal.astype(BF16)
    logit = jnp.sum(signal * router[2:3, :], -1, keepdims=True)
    chosen = slots_by_tokens(routes[2:3, :], count)
    logit = dot_exact(chosen, jnp.broadcast_to(logit, (count, 128)))
    score = sigmoid(logit)
    score_feed[...] = score
    chosen = chosen.astype(BF16)
    rows_feed[...] = dot(chosen, low[...]).astype(BF16)
    rows = dot(chosen, cotangent[...])
    cotangent_rows[...] = rows
    grad_raw[...] = (score[:, :1] * rows).astype(BF16)


def feed_step(rows_feed, grad_raw, gate_weight, up_weight, reduce_weight, raw, grad_rows):
    @pl.when(pl.program_id(0) == 0)
    def _():
        raw[...] = jnp.zeros_like(raw)
        grad_rows[...] = jnp.zeros_like(grad_rows)

    gate = dot(rows_feed[...], gate_weight[...])
    up = dot(rows_feed[...], up_weight[...])
    bent, rise = gelu_parts(gate)
    gated_low = (bent * up).astype(BF16)
    raw[...] += dot(gated_low, reduce_weight[...])
    grad_gated = dot_right(grad_raw[...], reduce_weight[...])
    gate_low = (grad_gated * up * rise).astype(BF16)
    up_low = (grad_gated * bent).astype(BF16)
    grad_rows[...] += dot_right(gate_low, gate_weight[...]) + dot_right(up_low, up_weight[...])
    return gated_low, gate_low, up_low


def heavy_feed_kernel(
    rows_feed, grad_raw, gate_weight, up_weight, reduce_weight,
    raw, grad_rows, gated, grad_gate, grad_up,
):
    gated_low, gate_low, up_low = feed_step(
        rows_feed, grad_raw, gate_weight, up_weight, reduce_weight, raw, grad_rows
    )
    gated[...] = gated_low
    grad_gate[...] = gate_low
    grad_up[...] = up_low


def heavy_feed_split_kernel(
    rows_feed, grad_raw, gate_weight, up_weight, reduce_weight,
    raw, grad_rows, kept, sent, own, first, second, third,
):
    gated_low, gate_low, up_low = feed_step(
        rows_feed, grad_raw, gate_weight, up_weight, reduce_weight, raw, grad_rows
    )
    step = pl.program_id(0)
    width, part = rows_feed.shape[1], gated_low.shape[1]
    half = kept.shape[1] // 2
    start = pl.multiple_of((step % 4) * part, part)
    mine = step // 4 == lax.axis_index("dp") % 2

    @pl.when(mine)
    def _():
        kept[:, pl.ds(start, part)] = gate_low
        kept[:, pl.ds(half + start, part)] = up_low

    @pl.when(jnp.logical_not(mine))
    def _():
        sent[:, pl.ds(width + start, part)] = gate_low
        sent[:, pl.ds(width + half + start, part)] = up_low

    slot = (step // 2 + 4 - lax.axis_index("seq") // 2) % 4
    spot = pl.multiple_of((step % 2) * part, part)
    for index, ref in enumerate((own, first, second, third)):

        @pl.when(slot == index)
        def _(ref=ref):
            ref[:, pl.ds(spot, part)] = gated_low

    @pl.when(step == 0)
    def _():
        sent[:, :width] = rows_feed[...]
        for ref in (first, second, third):
            ref[:, 2 * part :] = grad_raw[...]


def light_feed_kernel(
    low, cotangent, gate_weight, up_weight, reduce_weight, result, grad_low, kept, sent, turned
):
    step = pl.program_id(0)
    width = cotangent.shape[1]
    quarter = width // 4

    @pl.when(step == 0)
    def _():
        result[...] = jnp.zeros_like(result)
        grad_low[...] = jnp.zeros_like(grad_low)
        for part in range(4):
            turned[part] = cotangent[:, part * quarter : (part + 1) * quarter]

    gate = dot(low[...], gate_weight[...])
    up = dot(low[...], up_weight[...])
    bent, rise = gelu_parts(gate)
    gated_low = (bent * up).astype(BF16)
    result[...] += dot(gated_low, reduce_weight[...])
    grad_gated = dot_right(cotangent[...], reduce_weight[...])
    gate_low = (grad_gated * up * rise).astype(BF16)
    up_low = (grad_gated * bent).astype(BF16)
    grad_low[...] += dot_right(gate_low, gate_weight[...]) + dot_right(up_low, up_weight[...])
    hidden = gate_low.shape[1]
    seq, rows = kept.shape[1:3]
    core = lax.axis_index("dp") % 2
    products = [dot_left(low[...], grad).astype(BF16) for grad in (gate_low, up_low)]
    for ref, chosen in ((kept, core == step), (sent, core != step)):

        @pl.when(chosen)
        def _(ref=ref):
            for x in range(2):
                for i in range(seq):
                    ref[x, i, :, :hidden] = products[x][i * rows : (i + 1) * rows]

    more = rows // 3
    for part in range(4):
        product = dot_left(gated_low, turned[part]).astype(BF16)
        for ref, chosen in ((kept, core == part % 2), (sent, core != part % 2)):

            @pl.when(chosen)
            def _(ref=ref, x=part // 2, product=product):
                for i in range(seq // 2):
                    spot = step * (seq // 2) + i
                    start = i * (rows + more)
                    ref[x, spot, :, hidden : hidden + quarter] = product[start : start + rows]
                    rest = product[start + rows : start + rows + more]
                    for piece in range(3):
                        ref[x, spot, piece * more : (piece + 1) * more, hidden + quarter :] = rest[
                            :, piece * 64 : (piece + 1) * 64
                        ]


def turn_kernel(
    routes, residual, gain, result, grad_low, raw, grad_rows, score_feed, cotangent_rows, cotangent,
    router, light_output, heavy_output, heavy_attended, score_query,
    output, grad_residual, grad_residual_low, grad_attended, grad_heavy_rows, grad_heavy_attended,
    logit_query, small,
):
    count = residual.shape[0]
    spread = tokens_by_slots(routes[2:3, :], count)
    score = score_feed[:, :1]
    output[...] = (
        residual[...] + result[...] + dot_exact(spread, score * raw[...])
    ).astype(BF16)
    logit = score * (1.0 - score) * jnp.sum(cotangent_rows[...] * raw[...], -1, keepdims=True)
    grad = grad_low[...] + dot_exact(spread, grad_rows[...] + logit * router[2:3, :])
    back, gain_grad = norm_back(residual[...], gain[...], grad)
    token_logit = dot_exact(spread, jnp.broadcast_to(logit, (logit.shape[0], 128)))[:, :1]
    signal = normed(residual[...], gain[...])
    small[0:1] = gain_grad
    small[1:2] = jnp.sum(token_logit * signal, 0, keepdims=True)
    total = cotangent[...].astype(F32) + back
    grad_residual[...] = total
    grad_residual_low[...] = total.astype(BF16)
    grad_attended[...] = dot_right(grad_residual_low[...], light_output[...]).astype(BF16)
    chosen = slots_by_tokens(routes[0:1, :], count).astype(BF16)
    grad_heavy_rows[...] = dot(chosen, grad_residual_low[...]).astype(BF16)
    scaled = dot_right(grad_heavy_rows[...], heavy_output[...])
    score = score_query[:, :1]
    logit = score * (1.0 - score) * jnp.sum(scaled * heavy_attended[...], -1, keepdims=True)
    logit_query[...] = jnp.broadcast_to(logit, logit_query.shape)
    grad_heavy_attended[...] = (score * scaled).astype(BF16)


def heavy_query_kernel(
    count, bounds, routes, gathered, query_heavy, keyval, peaks, grad, grad_query, packet
):
    slots, width = query_heavy.shape
    heads = width // HHS
    allowed = heavy_mask(count, bounds, routes, gathered, width)
    lanes = lax.broadcasted_iota(jnp.int32, (slots, 128), 1)
    kept = peaks[...]
    lead, first, last = place(count, bounds)
    tag = jnp.where(lanes == 4 * heads, own_segment(routes, lead, first, last), 0.0)
    for head in range(heads):
        columns = slice(head * HHS, (head + 1) * HHS)
        values = slice(width + head * HHS, width + (head + 1) * HHS)
        scores = dot_right(query_heavy[:, columns], keyval[:, columns]) * HHS ** (-0.5)
        peak = jnp.sum(jnp.where(lanes == head, kept, 0.0), -1, keepdims=True)
        weights = jnp.where(allowed, jnp.exp(scores - peak), 0.0)
        grad_weights = dot_right(grad[:, columns], keyval[:, values])
        inner = jnp.sum(weights * grad_weights, -1, keepdims=True)
        grad_scores = (weights * (grad_weights - inner)).astype(BF16)
        grad_query[:, columns] = (dot(grad_scores, keyval[:, columns]) * HHS ** (-0.5)).astype(BF16)
        for lane, value in ((head, peak), (heads + head, inner)):
            high = value.astype(BF16).astype(F32)
            tag = jnp.where(lanes == lane, high, tag)
            tag = jnp.where(lanes == 2 * heads + lane, value - high, tag)
    packet[:, :width] = query_heavy[...]
    packet[:, width : 2 * width] = grad[...]
    packet[:, 2 * width :] = tag.astype(BF16)


def heavy_key_kernel(
    count, bounds, routes, first, second, keyval, own_values, score_keyval, grad_raw, logit_keyval, packets
):
    half = first.shape[0]
    packets[:half] = first[...]
    packets[half:] = second[...]
    slots = own_values.shape[0]
    width = own_values.shape[1]
    heads = width // HHS
    lead, first, last = place(count, bounds)
    column = column_of(routes[1:2, :])
    key_segment = jnp.where(
        column >= 0, segment(column.astype(jnp.int32) + lead, first, last), -1.0
    )
    same = lax.broadcasted_iota(jnp.int32, (128, 128), 0) == lax.broadcasted_iota(
        jnp.int32, (128, 128), 1
    )
    tags = dot_right(same.astype(BF16), packets[:, 2 * width :])
    allowed = key_segment == tags[4 * heads : 4 * heads + 1]
    score = score_keyval[:, :1]
    logit = jnp.zeros((slots, 1), F32)
    for head in range(heads):
        columns = slice(head * HHS, (head + 1) * HHS)
        values = slice(width + head * HHS, width + (head + 1) * HHS)
        peak = tags[head : head + 1] + tags[2 * heads + head : 2 * heads + head + 1]
        inner = tags[heads + head : heads + head + 1] + tags[3 * heads + head : 3 * heads + head + 1]
        scores = dot_right(keyval[:slots, columns], packets[:, columns]) * HHS ** (-0.5)
        weights = jnp.where(allowed, jnp.exp(scores - peak), 0.0)
        grad_weights = dot_right(keyval[:slots, values], packets[:, values])
        grad_scores = (weights * (grad_weights - inner)).astype(BF16)
        key_grad = dot(grad_scores, packets[:, columns]) * HHS ** (-0.5)
        value_grad = dot(weights.astype(BF16), packets[:, values]).astype(BF16).astype(F32)
        logit += jnp.sum(value_grad * own_values[:, columns], -1, keepdims=True)
        grad_raw[:, columns] = key_grad.astype(BF16)
        grad_raw[:, values] = (score * value_grad).astype(BF16)
    logit_keyval[...] = jnp.broadcast_to(score * (1.0 - score) * logit, logit_keyval.shape)


def mixer_light_kernel(
    first_query, second_query, first_span, second_span, from_below, from_above, light_query,
    light_keyval, grad, total_keyval,
):
    count, half = first_query.shape
    own = slice(WINDOW, WINDOW + count)
    for i, (ref, base) in enumerate(
        ((first_span, 0), (second_span, 0), (first_span, half), (second_span, half))
    ):
        total_keyval[:, i * half : (i + 1) * half] = ref[own, base : base + half]
    for rows, more in (
        (slice(0, WINDOW), from_below),
        (slice(count - WINDOW, count), from_above),
    ):
        total_keyval[rows] = (total_keyval[rows].astype(F32) + more[...].astype(F32)).astype(BF16)
    grad[...] = (
        dot_right(first_query[...], light_query[:, :half])
        + dot_right(second_query[...], light_query[:, half:])
        + dot_right(total_keyval[...], light_keyval[...])
    )


def mixer_kernel(
    routes, tokens, gain, router, grad_residual, grad_light, grad_heavy_query, grad_raw_keyval,
    logit_query, logit_keyval, heavy_query, heavy_keyval, feed_small, tokens_grad, small,
):
    count = tokens.shape[0]
    spread_query = tokens_by_slots(routes[0:1, :], count)
    spread_keyval = tokens_by_slots(routes[1:2, :], count)
    query_rows = dot_right(grad_heavy_query[...], heavy_query[...])
    query_rows += logit_query[:, :1] * router[0:1, :]
    keyval_rows = dot_right(grad_raw_keyval[...], heavy_keyval[...])
    keyval_rows += logit_keyval[:, :1] * router[1:2, :]
    grad = (
        grad_light[...]
        + dot_exact(spread_query, query_rows)
        + dot_exact(spread_keyval, keyval_rows)
    )
    signal = tokens[...].astype(F32)
    back, gain_grad = norm_back(signal, gain[...], grad)
    tokens_grad[...] = (grad_residual[...] + back).astype(BF16)
    signal = normed(signal, gain[...])
    small[0:1] = gain_grad
    small[1:2] = feed_small[0:1]
    small[2:3] = jnp.sum(dot_exact(spread_query, logit_query[...])[:, :1] * signal, 0, keepdims=True)
    small[3:4] = jnp.sum(dot_exact(spread_keyval, logit_keyval[...])[:, :1] * signal, 0, keepdims=True)
    small[4:5] = feed_small[1:2]
    small[5:8] = jnp.zeros((3, small.shape[1]), F32)


def estimate(weight, size):
    return pl.CostEstimate(
        flops=int(weight * 1e9), bytes_accessed=20 * size, transcendentals=0
    )


def without(body, start, count):
    def inner(*refs):
        return body(*refs[:start], *refs[start + count :])

    return inner


def run(body, outs, ins, limit, weight=0, scratch=(), smem=0, deps=()):
    vmem = pl.BlockSpec(memory_space=pltpu.VMEM)
    size = sum(v.size * v.dtype.itemsize for v in ins) + sum(
        math.prod(shape) * jnp.dtype(kind).itemsize for shape, kind in outs
    )
    return pl.pallas_call(
        without(body, len(ins), len(deps)),
        out_shape=[jax.ShapeDtypeStruct(shape, kind) for shape, kind in outs],
        in_specs=[pl.BlockSpec(memory_space=pltpu.SMEM)] * smem
        + [vmem] * (len(ins) - smem)
        + [pl.BlockSpec(memory_space=pl.ANY)] * len(deps),
        out_specs=[vmem] * len(outs),
        scratch_shapes=list(scratch),
        compiler_params=pltpu.CompilerParams(vmem_limit_bytes=int(limit * MIB)),
        cost_estimate=estimate(weight, size),
    )(*ins, *deps)


def heavy_feed(rows_feed, grad_raw, heavy_expand, heavy_reduce, seq, deps):
    slots, width = rows_feed.shape
    hidden = heavy_reduce.shape[0]
    steps = 8
    part = hidden // steps
    fixed = pl.BlockSpec((slots, width), lambda j: (0, 0))
    moving = pl.BlockSpec((slots, part), lambda j: (0, j))
    split = seq == 8
    if split:
        columns = [hidden, width + hidden, 2 * part] + [2 * part + width] * 3
        specs = [pl.BlockSpec((slots, c), lambda j: (0, 0)) for c in columns]
    else:
        columns, specs = [hidden] * 3, [moving] * 3
    return pl.pallas_call(
        without(heavy_feed_split_kernel if split else heavy_feed_kernel, 5, len(deps)),
        grid=(steps,),
        out_shape=[jax.ShapeDtypeStruct((slots, width), F32)] * 2
        + [jax.ShapeDtypeStruct((slots, c), BF16) for c in columns],
        in_specs=[
            fixed,
            fixed,
            pl.BlockSpec((width, part), lambda j: (0, j)),
            pl.BlockSpec((width, part), lambda j: (0, steps + j)),
            pl.BlockSpec((part, width), lambda j: (j, 0)),
        ]
        + [pl.BlockSpec(memory_space=pl.ANY)] * len(deps),
        out_specs=[fixed] * 2 + specs,
        compiler_params=pltpu.CompilerParams(vmem_limit_bytes=24 * MIB),
        cost_estimate=estimate(75, 20 << 20),
    )(rows_feed, grad_raw, heavy_expand, heavy_expand, heavy_reduce, *deps)


def light_feed(low, cotangent, light_expand, light_reduce, seq, deps):
    count, width = low.shape
    hidden = light_reduce.shape[0]
    part = hidden // 2
    fixed = pl.BlockSpec((count, width), lambda j: (0, 0))
    packed = (2, seq, width // seq, part + width // 4 + 64)
    return pl.pallas_call(
        without(light_feed_kernel, 5, len(deps)),
        grid=(2,),
        out_shape=[
            jax.ShapeDtypeStruct((count, width), F32),
            jax.ShapeDtypeStruct((count, width), F32),
            jax.ShapeDtypeStruct(packed, BF16),
            jax.ShapeDtypeStruct(packed, BF16),
        ],
        in_specs=[
            fixed,
            fixed,
            pl.BlockSpec((width, part), lambda j: (0, j)),
            pl.BlockSpec((width, part), lambda j: (0, 2 + j)),
            pl.BlockSpec((part, width), lambda j: (j, 0)),
        ]
        + [pl.BlockSpec(memory_space=pl.ANY)] * len(deps),
        out_specs=[fixed, fixed] + [pl.BlockSpec(packed, lambda j: (0, 0, 0, 0))] * 2,
        scratch_shapes=[pltpu.VMEM((4, count, width // 4), BF16)],
        compiler_params=pltpu.CompilerParams(vmem_limit_bytes=48 * MIB),
        cost_estimate=estimate(LONG, 8 << 20),
    )(low, cotangent, light_expand, light_expand, light_reduce, *deps)


def products_kernel(formers, latters, small, products):
    width = formers.shape[1] // 3
    quarter = width // 4
    offsets = ((0, 0, quarter), (1, quarter, quarter), (2, 2 * quarter, 2 * quarter))
    for part, start, columns in offsets:
        products[:, start : start + columns] = dot_left(
            formers[:, part * width : (part + 1) * width], latters[:, start : start + columns]
        ).astype(BF16)
    products[:, width:] = turn_small(small[...])


def outer_kernel(former, latter, product):
    product[...] = dot_left(former[...], latter[...]).astype(BF16)


def fold_kernel(kept, got, left, sent):
    total = (kept[...].astype(F32) + got[...].astype(F32)).astype(BF16)
    half = total.shape[1] // 2
    x = lax.axis_index("dp") // 2
    left[...] = jnp.where(x == 0, total[:, :half], total[:, half:])
    sent[...] = jnp.where(x == 0, total[:, half:], total[:, :half])


def expand_x_kernel(former, kept, got, sent, left):
    slots, width = former.shape
    half = kept.shape[1] // 2
    x = lax.axis_index("dp") // 2
    sent[:slots, :width] = former[...]
    sent[slots:, :width] = got[:, :width]
    for rows, source, base in ((slice(0, slots), kept, 0), (slice(slots, None), got, width)):
        gate, up = source[:, base : base + half], source[:, base + half : base + 2 * half]
        left[rows] = jnp.where(x == 0, gate, up)
        sent[rows, width:] = jnp.where(x == 0, up, gate)


def expand_y_kernel(sent_x, left, got, sent, former):
    rows, wide = left.shape
    part = former.shape[1] // 4
    y = lax.axis_index("seq") % 2
    for start, source in ((0, sent_x), (rows, got)):
        here = slice(start, start + rows)
        for i in range(4):
            even = source[:, 2 * i * part : (2 * i + 1) * part]
            odd = source[:, (2 * i + 1) * part : (2 * i + 2) * part]
            columns = slice(i * part, (i + 1) * part)
            former[here, columns] = jnp.where(y == 0, even, odd)
            sent[here, columns] = jnp.where(y == 0, odd, even)
    sent[:rows, 4 * part :] = left[...]
    sent[rows:, 4 * part :] = got[:, 8 * part :]


def reduce_y_kernel(own, grad_raw, first, second, third, sent, former):
    slots = own.shape[0]
    half = own.shape[1] // 2
    y = lax.axis_index("seq") % 2
    for i, source in enumerate((own, first, second, third)):
        here = slice(i * slots, (i + 1) * slots)
        even, odd = source[:, :half], source[:, half : 2 * half]
        former[here] = jnp.where(y == 0, even, odd)
        sent[here, :half] = jnp.where(y == 0, odd, even)
        latter = grad_raw[...] if i == 0 else source[:, 2 * half :]
        sent[here, half:] = latter


def expand_product_kernel(sent, got, former, own, first, second, third, slices):
    base = former.shape[1]
    product = dot_left(former[...], sent[:, base:])
    product += dot_left(got[:, :base], got[:, base:])
    part = own.shape[0]
    for i in range(4):
        slices[i] = product[i * part : (i + 1) * part].astype(BF16)
    z = lax.axis_index("seq") // 2
    for step, ref in enumerate((own, first, second, third)):
        ref[...] = slices[(z + step) % 4]


def reduce_product_kernel(sent, got, former, kept, moved, turned):
    half = former.shape[1]
    quarter = (sent.shape[1] - half) // 4
    for index, source in enumerate((sent, got)):
        for spot, i in enumerate((0, 2, 1, 3)):
            start = half + i * quarter
            turned[index, :, spot * quarter : (spot + 1) * quarter] = source[
                :, start : start + quarter
            ]
    product = dot_left(former[...], turned[0]) + dot_left(got[:, :half], turned[1])
    core = lax.axis_index("dp") % 2
    low, high = product[:, : 2 * quarter], product[:, 2 * quarter :]
    kept[...] = jnp.where(core == 0, low, high).astype(BF16)
    moved[...] = jnp.where(core == 0, high, low).astype(BF16)


def stack_kernel(own, first, second, third, stacked):
    rows = own.shape[0]
    for i, ref in enumerate((own, first, second, third)):
        stacked[i * rows : (i + 1) * rows] = ref[...]


def rows_kernel(rows_query, scaled, rows_keyval, joined):
    width = rows_query.shape[1]
    for i, ref in enumerate((rows_query, scaled, rows_keyval)):
        joined[:, i * width : (i + 1) * width] = ref[...]


def stack_two_kernel(first, second, stacked):
    rows = first.shape[0]
    stacked[:rows] = first[...]
    stacked[rows:] = second[...]


def heavy_core_kernel(grad_query, grad_rows, grad_keyval, sent, kept):
    width = grad_query.shape[1]
    quarter = width // 4
    core = lax.axis_index("dp") % 2
    for x in range(2):
        spot = x * width
        for source, columns in ((grad_query, quarter), (grad_rows, quarter), (grad_keyval, 2 * quarter)):
            even = source[:, 2 * x * columns : (2 * x + 1) * columns]
            odd = source[:, (2 * x + 1) * columns : (2 * x + 2) * columns]
            kept[:, spot : spot + columns] = jnp.where(core == 0, even, odd)
            sent[:, spot : spot + columns] = jnp.where(core == 0, odd, even)
            spot += columns


def heavy_x_kernel(kept, got, sent, left):
    slots = kept.shape[0]
    width = kept.shape[1] // 2
    x = lax.axis_index("dp") // 2
    for rows, source in ((slice(0, slots), kept), (slice(slots, None), got)):
        low, high = source[:, :width], source[:, width:]
        left[rows] = jnp.where(x == 0, low, high)
        sent[rows] = jnp.where(x == 0, high, low)


def pair_x_kernel(kept, got, left, sent):
    x = lax.axis_index("dp") // 2
    left[...] = (kept[x].astype(F32) + got[x].astype(F32)).astype(BF16)
    sent[...] = (kept[1 - x].astype(F32) + got[1 - x].astype(F32)).astype(BF16)


def pair_y_kernel(left, got, kept, sent):
    y = lax.axis_index("seq") % 2
    for i in range(4):
        mine, other = 2 * i + y, 2 * i + 1 - y
        kept[i] = (left[mine].astype(F32) + got[mine].astype(F32)).astype(BF16)
        sent[i] = (left[other].astype(F32) + got[other].astype(F32)).astype(BF16)


def pair_z_kernel(kept, got, own, first, second, third):
    z = lax.axis_index("seq") // 2
    for step, ref in enumerate((own, first, second, third)):
        spot = (z + step) % 4
        ref[...] = (kept[spot].astype(F32) + got[spot].astype(F32)).astype(BF16)


def heavy_y_kernel(own_rows, got_rows, left, got, small, kept, sent, total):
    width = left.shape[1]
    quarter = width // 4
    for part, start, columns in ((0, 0, quarter), (1, quarter, quarter), (2, 2 * quarter, 2 * quarter)):
        former = slice(part * width, (part + 1) * width)
        here = slice(start, start + columns)
        product = dot_left(own_rows[:, former], left[:, here])
        product += dot_left(got_rows[:, former], got[:, here])
        total[:, here] = product.astype(BF16)
    total[:, width:] = turn_small(small[...])
    y = lax.axis_index("seq") % 2
    rows = width // 8
    for i in range(4):
        even = total[2 * i * rows : (2 * i + 1) * rows]
        odd = total[(2 * i + 1) * rows : (2 * i + 2) * rows]
        kept[i] = jnp.where(y == 0, even, odd)
        sent[i] = jnp.where(y == 0, odd, even)


def turn_small(small):
    high = small.astype(BF16)
    low = (small - high.astype(F32)).astype(BF16)
    same = (
        lax.broadcasted_iota(jnp.int32, (small.shape[0], 128), 0)
        == lax.broadcasted_iota(jnp.int32, (small.shape[0], 128), 1)
    ).astype(BF16)
    return (dot_left(high, same) + dot_left(low, same)).astype(BF16)


def total_of(blocks):
    total = blocks[0][...].astype(F32)
    for block in blocks[1:]:
        total = total + block[...].astype(F32)
    return total


def light_end_kernel(own, first, second, third, query, keyval, output):
    total = total_of((own, first, second, third))
    quarter = query.shape[1]
    keyval[...] = total[:, : 2 * quarter]
    query[...] = total[:, 2 * quarter : 3 * quarter]
    output[...] = total[:, 3 * quarter :]


def heavy_end_kernel(own, first, second, third, query, keyval, output, small):
    total = total_of((own, first, second, third))
    quarter = query.shape[1]
    query[...] = total[:, :quarter]
    output[...] = total[:, quarter : 2 * quarter]
    keyval[...] = total[:, 2 * quarter : 4 * quarter]
    same = (
        lax.broadcasted_iota(jnp.int32, (8, 128), 0)
        == lax.broadcasted_iota(jnp.int32, (8, 128), 1)
    ).astype(F32)
    small[...] = lax.dot_general(
        same,
        total[:, 4 * quarter :],
        (((1,), (1,)), ((), ())),
        preferred_element_type=F32,
        precision=HIGHEST,
    )


def feed_end_kernel(own, first, second, third, expand, reduce):
    total = total_of((own, first, second, third))
    hidden, quarter = expand.shape[1], reduce.shape[1]
    rows = total.shape[0]
    more = rows // 3
    expand[...] = total[:, :hidden]
    reduce[:rows] = total[:, hidden : hidden + quarter]
    for piece in range(3):
        reduce[rows:, piece * 64 : (piece + 1) * 64] = total[
            piece * more : (piece + 1) * more, hidden + quarter :
        ]


def stages(count):
    found, stride = [], 1
    while count > 1:
        size = 4 if count % 4 == 0 and count != 8 else 2
        found.append((size, stride))
        stride, count = stride * size, count // size
    return found


def shifted(block, axis, size, stride, step):
    route = []
    for i in range(lax.axis_size(axis)):
        member = (i // stride) % size
        route.append((i, i + ((member + step) % size - member) * stride))
    return lax.ppermute(block, axis, route)


def neighbours(block, distance):
    devices = range(lax.axis_size("seq"))
    return lax.ppermute(
        block, "seq", [(i - distance, i) for i in devices if i - distance in devices]
    )


def member_of(axis, size, stride):
    return (lax.axis_index(axis) // stride) % size


def pick(block, index, dim):
    return lax.dynamic_index_in_dim(block, index, dim, keepdims=False)


def reduce_stage(block, axis, size, stride, dim):
    me = member_of(axis, size, stride)
    total = pick(block, me, dim).astype(F32)
    for step in range(1, size):
        sent = pick(block, (me + step) % size, dim)
        total = total + shifted(sent, axis, size, stride, step).astype(F32)
    return total.astype(BF16)


def reduce_dp(block):
    block = reduce_stage(block, "dp", 2, 1, 0)
    half = block.shape[1] // 2
    first, second = block[:, :half], block[:, half:]
    x = member_of("dp", 2, 2)
    got = shifted(jnp.where(x == 0, second, first), "dp", 2, 2, 1)
    return (jnp.where(x == 0, first, second).astype(F32) + got.astype(F32)).astype(BF16)


def reduce_seq(block, skip=0):
    for size, stride in stages(lax.axis_size("seq"))[skip:]:
        count = lax.axis_size("seq") // stride
        block = block.reshape(count // size, size, block.shape[0] // count, block.shape[1])
        block = reduce_stage(block, "seq", size, stride, 1)
        block = block.reshape(-1, block.shape[-1])
    return block


def gather_part(block, size, stride):
    return jnp.concatenate(
        [block] + [shifted(block, "seq", size, stride, step) for step in range(1, size)], 0
    )


def gather_seq(block):
    for size, stride in stages(lax.axis_size("seq"))[::-1]:
        block = gather_part(block, size, stride)
    return block


def total_parts(parts):
    total = parts[0].astype(F32)
    for part in parts[1:]:
        total = total + part.astype(F32)
    return total


def reduce_pair(kept, sent):
    block = (kept.astype(F32) + shifted(sent, "dp", 2, 1, 1).astype(F32)).astype(BF16)
    return reduce_stage(block, "dp", 2, 2, 0).reshape(-1, block.shape[3])


def swap_rows(axis, stride, whole, mine, other):
    got = shifted(jnp.concatenate([whole, other], 1), axis, 2, stride, 1)
    width = whole.shape[1]
    return (
        jnp.concatenate([whole, got[:, :width]], 0),
        jnp.concatenate([mine, got[:, width:]], 0),
    )


def gather_dp(former, first, second):
    core, x = member_of("dp", 2, 1), member_of("dp", 2, 2)
    half = first.shape[1] // 2

    def both(low, high):
        return jnp.concatenate([low, high], 1)

    lows = both(first[:, :half], second[:, :half])
    highs = both(first[:, half:], second[:, half:])
    former, latter = swap_rows(
        "dp", 1, former, jnp.where(core == 0, lows, highs), jnp.where(core == 0, highs, lows)
    )
    low, high = latter[:, :half], latter[:, half:]
    return swap_rows(
        "dp", 2, former, jnp.where(x == 0, low, high), jnp.where(x == 0, high, low)
    )


def split_rows(former, latter, size, stride):
    rows, width = former.shape
    count = lax.axis_size("seq") // stride
    former = former.reshape(rows, count // size, size, width // count)
    me = member_of("seq", size, stride)
    formers, latters = [pick(former, me, 2).reshape(rows, width // size)], [latter]
    for step in range(1, size):
        other = pick(former, (me + step) % size, 2).reshape(rows, width // size)
        got = shifted(jnp.concatenate([other, latter], 1), "seq", size, stride, step)
        formers.append(got[:, : width // size])
        latters.append(got[:, width // size :])
    return jnp.concatenate(formers, 0), jnp.concatenate(latters, 0)


def outer(former, latter):
    rows, width = former.shape
    columns = latter.shape[1]
    return run(
        outer_kernel, [((width, columns), BF16)], [former, latter], 24, 2e-9 * rows * width * columns
    )[0]


def expand_gradient(former, gate, up):
    former, latter = gather_dp(former, gate, up)
    size, stride = stages(lax.axis_size("seq"))[0]
    former, latter = split_rows(former, latter, size, stride)
    return reduce_seq(outer(former, latter), 1)


def reduce_gradient(former, latter):
    for size, stride in stages(lax.axis_size("seq")):
        former, latter = split_rows(former, latter, size, stride)
    quarter = latter.shape[1] // 4
    parts = [latter[:, i * quarter : (i + 1) * quarter] for i in (0, 2, 1, 3)]
    product = outer(former, jnp.concatenate(parts, 1))
    half = product.shape[1] // 2
    return reduce_dp(jnp.stack([product[:, :half], product[:, half:]]))


def sum_dp(block):
    for stride in (1, 2):
        block = block + shifted(block, "dp", 2, stride, 1)
    return block


def pair_x(kept, sent, deps=(), weight=0):
    got = shifted(sent, "dp", 2, 1, 1)
    left, sent = run(
        pair_x_kernel, [(kept.shape[1:], BF16)] * 2, [kept, got], 24, weight, deps=deps
    )
    return left, sent, shifted(sent, "dp", 2, 2, 1)


def pair_y(left, got, deps=(), weight=0):
    shape = (4,) + left.shape[1:]
    kept, sent = run(pair_y_kernel, [(shape, BF16)] * 2, [left, got], 16, weight, deps=deps)
    return kept, sent, shifted(sent, "seq", 2, 1, 1)


def pair_z(kept, got, deps=(), weight=0):
    own, *sent = run(
        pair_z_kernel, [(kept.shape[1:], BF16)] * 4, [kept, got], 16, weight, deps=deps
    )
    return [own] + [shifted(block, "seq", 4, 2, 1 + i) for i, block in enumerate(sent)]


def send_expand(rows_feed, kept, sent, deps):
    slots, width = rows_feed.shape
    wide = kept.shape[1] // 2
    got = shifted(sent, "dp", 2, 1, 1)
    sent, left = run(
        expand_x_kernel,
        [((2 * slots, width + wide), BF16), ((2 * slots, wide), BF16)],
        [rows_feed, kept, got],
        16,
        deps=deps,
    )
    return sent, left, shifted(sent, "dp", 2, 2, 1)


def send_expand_y(sent, left, got, deps=()):
    rows, wide = left.shape
    half = (sent.shape[1] - wide) // 2
    sent, former = run(
        expand_y_kernel,
        [((2 * rows, half + wide), BF16), ((2 * rows, half), BF16)],
        [sent, left, got],
        16,
        deps=deps,
    )
    return sent, shifted(sent, "seq", 2, 1, 1), former


def send_expand_z(sent, got, former, deps=()):
    wide = sent.shape[1] - former.shape[1]
    rows = former.shape[1] // 4
    own, *sent = run(
        expand_product_kernel,
        [((rows, wide), BF16)] * 4,
        [sent, got, former],
        24,
        0,
        [pltpu.VMEM((4, rows, wide), BF16)],
        deps=deps,
    )
    return [own] + [shifted(block, "seq", 4, 2, 1 + i) for i, block in enumerate(sent)]


def send_reduce_y(own, grad_raw, moved, deps=()):
    slots, width = grad_raw.shape
    half = own.shape[1] // 2
    sent, former = run(
        reduce_y_kernel,
        [((4 * slots, half + width), BF16), ((4 * slots, half), BF16)],
        [own, grad_raw] + moved,
        16,
        deps=deps,
    )
    return sent, shifted(sent, "seq", 2, 1, 1), former


def send_reduce_core(sent, got, former, deps=()):
    rows, half = former.shape
    width = sent.shape[1] - half
    kept, sent = run(
        reduce_product_kernel,
        [((half, width // 2), BF16)] * 2,
        [sent, got, former],
        16,
        0,
        [pltpu.VMEM((2, rows, width), BF16)],
        deps=deps,
    )
    return kept, sent, shifted(sent, "dp", 2, 1, 1)


def send_reduce_x(kept, got, deps=()):
    shape = (kept.shape[0], kept.shape[1] // 2)
    left, sent = run(fold_kernel, [(shape, BF16)] * 2, [kept, got], 8, deps=deps)
    return left, shifted(sent, "dp", 2, 2, 1)


def send_rows(rows_query, scaled, rows_keyval):
    slots, width = rows_query.shape
    (joined,) = run(
        rows_kernel, [((slots, 3 * width), BF16)], [rows_query, scaled, rows_keyval], 8
    )
    got = shifted(joined, "dp", 2, 1, 1)
    (joined,) = run(stack_two_kernel, [((2 * slots, 3 * width), BF16)], [joined, got], 8)
    return joined, shifted(joined, "dp", 2, 2, 1)


def on_device(
    tokens,
    cotangent,
    document_bounds,
    routes,
    attention_gain,
    feedforward_gain,
    router,
    light_query,
    light_keyval,
    light_output,
    heavy_query,
    heavy_keyval,
    heavy_output_weight,
    light_expand,
    light_reduce,
    heavy_expand,
    heavy_reduce,
):
    count, width = tokens.shape
    slots = routes.shape[1]
    seq = lax.axis_size("seq")
    length = count * seq
    gain, feed_gain = attention_gain[None], feedforward_gain[None]
    heavy_width = heavy_query.shape[1]

    above = neighbours(tokens[count - WINDOW :], 1)
    below = neighbours(tokens[:WINDOW], -1)
    (packet,) = run(
        select_kernel,
        [((slots, width + 128), BF16)],
        [document_bounds, routes, tokens],
        8,
        0,
        smem=1,
    )
    gathered = gather_seq(packet)
    wide = LH * 128
    low, query, keyval, rows_query, rows_keyval, query_heavy, score_query = run(
        project_kernel,
        [
            ((count, width), BF16),
            ((count, wide), BF16),
            ((count, 2 * wide), BF16),
            ((slots, width), BF16),
            ((slots, width), BF16),
            ((slots, heavy_width), BF16),
            ((slots, 128), F32),
        ],
        [routes, tokens, gain, router, light_query, light_keyval, heavy_query],
        24,
        50,
    )
    span_rows = count + 2 * WINDOW
    attended, peaks, span_low, span = run(
        functools.partial(light_forward_kernel, length),
        [
            ((count, width), BF16),
            ((8, count), F32),
            ((span_rows, width), BF16),
            ((span_rows, 2 * wide), BF16),
        ],
        [document_bounds, query, keyval, low, above, below, gain, light_keyval],
        24,
        60,
        smem=1,
    )
    keyval_heavy, heavy_attended, heavy_scaled, heavy_peaks, own_values, score_keyval = run(
        functools.partial(heavy_forward_kernel, count),
        [
            ((seq * slots, 2 * heavy_width), BF16),
            ((slots, heavy_width), F32),
            ((slots, heavy_width), BF16),
            ((slots, 128), F32),
            ((slots, heavy_width), F32),
            ((slots, 128), F32),
        ],
        [document_bounds, routes, gathered, query_heavy, score_query, gain, router, heavy_keyval],
        24 if seq <= 8 else 48,
        40,
        smem=1,
    )
    residual, feed_low, rows_feed, score_feed, cotangent_rows, grad_raw = run(
        residual_kernel,
        [
            ((count, width), F32),
            ((count, width), BF16),
            ((slots, width), BF16),
            ((slots, 128), F32),
            ((slots, width), F32),
            ((slots, width), BF16),
        ],
        [
            routes, tokens, attended, light_output, heavy_scaled, heavy_output_weight, feed_gain,
            router, cotangent,
        ],
        24,
        30,
    )
    fast = seq == 8
    deps = []
    if fast:
        heavy_rows = send_rows(rows_query, heavy_scaled, rows_keyval)
        deps = [heavy_rows[0]]
    feed = heavy_feed(rows_feed, grad_raw, heavy_expand, heavy_reduce, seq, deps)
    raw_feed, grad_rows = feed[:2]
    rows = width // seq
    if fast:
        expand_kept, expand_sent, reduce_own, *reduce_sent = feed[2:]
        moved = [shifted(block, "seq", 4, 2, 1 + i) for i, block in enumerate(reduce_sent)]
        expand_moves = send_expand(rows_feed, expand_kept, expand_sent, heavy_rows[:1])
    light_result, grad_low, feed_kept, feed_sent = light_feed(
        feed_low, cotangent, light_expand, light_reduce, seq, [expand_moves[0]] if fast else []
    )
    deps = []
    if fast:
        expand_moves = send_expand_y(*expand_moves, moved)
        deps = [expand_moves[0]]
    (
        output,
        grad_residual,
        grad_residual_low,
        grad_attended,
        grad_heavy_rows,
        grad_heavy_attended,
        logit_query,
        feed_small,
    ) = run(
        turn_kernel,
        [
            ((count, width), BF16),
            ((count, width), F32),
            ((count, width), BF16),
            ((count, width), BF16),
            ((slots, width), BF16),
            ((slots, heavy_width), BF16),
            ((slots, 128), F32),
            ((2, width), F32),
        ],
        [
            routes, residual, feed_gain, light_result, grad_low, raw_feed, grad_rows, score_feed,
            cotangent_rows, cotangent, router, light_output, heavy_output_weight, heavy_attended,
            score_query,
        ],
        32,
        LONG,
        deps=deps,
    )
    deps = []
    if fast:
        feed_left, feed_sent, feed_got = pair_x(feed_kept, feed_sent, [feed_small, heavy_rows[1]])
        deps = [feed_sent]
    grad_heavy_query, packet = run(
        functools.partial(heavy_query_kernel, count),
        [((slots, heavy_width), BF16), ((slots, 2 * heavy_width + 128), BF16)],
        [
            document_bounds, routes, gathered, query_heavy, keyval_heavy, heavy_peaks,
            grad_heavy_attended,
        ],
        16 if seq <= 8 else 48,
        LONG,
        smem=1,
        deps=deps,
    )
    sums = [pltpu.VMEM((span_rows, wide // 2), F32)] * 2
    light_ins = [document_bounds, query, span, peaks, grad_attended, attended]
    first_query, first_span = run(
        functools.partial(light_first_kernel, length),
        [((count, width // 2), BF16), ((span_rows, width), BF16)],
        light_ins,
        24,
        0,
        sums,
        smem=1,
        deps=[packet],
    )
    second_query, second_span, grad_above, grad_below = run(
        functools.partial(light_second_kernel, length),
        [
            ((count, width // 2), BF16),
            ((span_rows, width), BF16),
            ((WINDOW, 2 * width), BF16),
            ((WINDOW, 2 * width), BF16),
        ],
        light_ins + [first_span],
        24,
        0,
        sums,
        smem=1,
    )
    from_above = neighbours(grad_above, -1)
    from_below = neighbours(grad_below, 1)
    mixer_kept, mixer_sent = run(
        light_products_kernel,
        [((2, width, width), BF16)] * 2,
        [
            span_low, first_query, second_query, first_span, second_span, attended,
            grad_residual_low,
        ],
        24,
        0,
    )
    shape = (2, seq, rows, width)
    mixer_kept, mixer_sent = mixer_kept.reshape(shape), mixer_sent.reshape(shape)
    deps = []
    if fast:
        moved_packets = [shifted(packet, "seq", 4, 2, 1 + i) for i in range(3)]
        (stacked,) = run(
            stack_kernel,
            [((4 * slots, packet.shape[1]), BF16)],
            [packet] + moved_packets,
            8,
            LONG,
            deps=[mixer_sent, expand_moves[1], feed_got],
        )
        packets = (stacked, shifted(stacked, "seq", 2, 1, 1))
        expand_parts = send_expand_z(*expand_moves, [stacked])
        mixer_left, mixer_sent, mixer_got = pair_x(
            mixer_kept, mixer_sent, expand_parts[:1], LONG
        )
        reduce_moves = send_reduce_y(reduce_own, grad_raw, moved, [mixer_sent])
        deps = reduce_moves[:1] + tuple(expand_parts[1:])
    else:
        packets = gather_seq(packet)
        packets = (packets[: packets.shape[0] // 2], packets[packets.shape[0] // 2 :])
    grad_raw_keyval, logit_keyval = run(
        functools.partial(heavy_key_kernel, count),
        [((slots, 2 * heavy_width), BF16), ((slots, 128), F32)],
        [document_bounds, routes, *packets, keyval_heavy[:slots], own_values, score_keyval],
        16 if seq <= 8 else 56,
        0,
        [pltpu.VMEM((seq * slots, 2 * heavy_width + 128), BF16)],
        smem=1,
        deps=deps,
    )
    deps = []
    if fast:
        heavy_sent, heavy_kept = run(
            heavy_core_kernel,
            [((slots, 2 * width), BF16)] * 2,
            [grad_heavy_query, grad_heavy_rows, grad_raw_keyval],
            8,
        )
        feed_kept, feed_sent, feed_got = pair_y(feed_left, feed_got, [heavy_sent])
        got = shifted(heavy_sent, "dp", 2, 1, 1)
        heavy_sent, heavy_left = run(
            heavy_x_kernel,
            [((2 * slots, width), BF16)] * 2,
            [heavy_kept, got],
            8,
            deps=[feed_sent],
        )
        heavy_got = shifted(heavy_sent, "dp", 2, 2, 1)
        deps = [heavy_sent]
    (grad_light,) = run(
        mixer_light_kernel,
        [((count, width), F32)],
        [
            first_query, second_query, first_span, second_span, from_below, from_above,
            light_query, light_keyval,
        ],
        24,
        5,
        [pltpu.VMEM((count, 2 * width), BF16)],
        deps=deps,
    )
    deps = [mixer_got, reduce_moves[1]] if fast else []
    tokens_grad, small = run(
        mixer_kernel,
        [((count, width), BF16), ((8, width), F32)],
        [
            routes, tokens, gain, router, grad_residual, grad_light, grad_heavy_query,
            grad_raw_keyval, logit_query, logit_keyval, heavy_query, heavy_keyval, feed_small,
        ],
        32,
        LONG,
        deps=deps,
    )
    quarter = width // 4
    hidden = light_reduce.shape[0] // 2
    if fast:
        light_kept, light_sent, light_got = pair_y(mixer_left, mixer_got, [tokens_grad])
        small = small + shifted(small, "dp", 2, 1, 1)
        feed_parts = pair_z(feed_kept, feed_got, [light_sent, small], LONG)
        small = small + shifted(small, "dp", 2, 2, 1)
        kept, sent = run(
            heavy_y_kernel,
            [((4, rows, width + 128), BF16)] * 2,
            [*heavy_rows, heavy_left, heavy_got, small],
            16,
            0,
            [pltpu.VMEM((width, width + 128), BF16)],
            deps=[feed_parts[0]],
        )
        reduce_moves = send_reduce_core(*reduce_moves, [sent])
        got = shifted(sent, "seq", 2, 1, 1)
        reduce_left, reduce_got = send_reduce_x(reduce_moves[0], reduce_moves[2])
        grad_heavy_reduce = reduce_left.astype(F32) + reduce_got.astype(F32)
        light_parts = pair_z(light_kept, light_got, [reduce_left])
        heavy_parts = pair_z(kept, got)
        grad_light_expand, grad_light_reduce = run(
            feed_end_kernel,
            [((rows, hidden), F32), ((light_reduce.shape[0] // seq, quarter), F32)],
            feed_parts,
            8,
        )
        grad_heavy_expand = total_parts(expand_parts)
        grad_light_query, grad_light_keyval, grad_light_output = run(
            light_end_kernel,
            [((rows, quarter), F32), ((rows, 2 * quarter), F32), ((rows, quarter), F32)],
            light_parts,
            8,
        )
        grad_heavy_query, grad_heavy_keyval, grad_heavy_output, small = run(
            heavy_end_kernel,
            [
                ((rows, quarter), F32),
                ((rows, 2 * quarter), F32),
                ((rows, quarter), F32),
                ((8, rows), F32),
            ],
            heavy_parts,
            8,
        )
        smalls = (small[0], small[1], small[2:5])
    else:
        small = sum_dp(small)
        gated_heavy, grad_gate, grad_up = feed[2:]
        grad_heavy_expand = expand_gradient(rows_feed, grad_gate, grad_up).astype(F32)
        grad_heavy_reduce = reduce_gradient(gated_heavy, grad_raw).astype(F32)
        formers = jnp.concatenate([rows_query, heavy_scaled, rows_keyval], 1)

        def mine(part):
            low_columns = slice(part * quarter, (part + 1) * quarter)
            high_columns = slice(2 * part * quarter, 2 * (part + 1) * quarter)
            return [
                grad_heavy_query[:, low_columns],
                grad_heavy_rows[:, low_columns],
                grad_raw_keyval[:, high_columns],
            ]

        first = jnp.concatenate(mine(0) + mine(1), 1)
        second = jnp.concatenate(mine(2) + mine(3), 1)
        formers, latters = gather_dp(formers, first, second)
        (heavy_products,) = run(
            products_kernel,
            [((width, width + 128), BF16)],
            [formers, latters, small],
            16,
            0.6,
        )
        heavy = reduce_seq(heavy_products).astype(F32)
        light = reduce_seq(reduce_pair(mixer_kept, mixer_sent)).astype(F32)
        packed = reduce_seq(reduce_pair(feed_kept, feed_sent)).astype(F32)
        grad_light_query = light[:, 2 * quarter : 3 * quarter]
        grad_light_keyval = light[:, : 2 * quarter]
        grad_light_output = light[:, 3 * quarter :]
        grad_light_expand = packed[:, :hidden]
        rest = packed[:, hidden + quarter :].reshape(3, rows // 3, 64)
        rest = rest.transpose(1, 0, 2).reshape(rows // 3, quarter)
        grad_light_reduce = jnp.concatenate([packed[:, hidden : hidden + quarter], rest], 0)
        grad_heavy_query = heavy[:, :quarter]
        grad_heavy_output = heavy[:, quarter : 2 * quarter]
        grad_heavy_keyval = heavy[:, 2 * quarter : 4 * quarter]
        smalls = (heavy[:, width], heavy[:, width + 1], heavy[:, width + 2 : width + 5].T)
    return (
        output,
        tokens_grad,
        *smalls,
        grad_light_query,
        grad_light_keyval,
        grad_light_output,
        grad_heavy_query,
        grad_heavy_keyval,
        grad_heavy_output,
        grad_light_expand,
        grad_light_reduce,
        grad_heavy_expand,
        grad_heavy_reduce,
    )


def solution(mesh):
    whole, rows = P(), P(("dp", "seq"), None)
    return jax.shard_map(
        on_device,
        mesh=mesh,
        in_specs=(rows, rows, whole, P(None, ("dp", "seq"))) + (whole,) * 13,
        out_specs=(rows, rows, P("seq"), P("seq"), P(None, "seq")) + (P("seq", "dp"),) * 10,
        check_vma=False,
    )
```

```python
import functools
import math

import jax
import jax.numpy as jnp
from jax import lax
from jax.experimental import pallas as pl
from jax.experimental.pallas import tpu as pltpu
from jax.sharding import PartitionSpec as P

LH = 8
HHS = 64
WINDOW = 128
EPSILON = 1e-06
MASKED = -1e30
HIGHEST = lax.Precision.HIGHEST
F32, BF16 = jnp.float32, jnp.bfloat16
MIB = 1 << 20
LONG = 60


def dot(former, latter):
    return jnp.dot(former, latter, preferred_element_type=F32)


def dot_left(former, latter):
    return lax.dot_general(former, latter, (((0,), (0,)), ((), ())), preferred_element_type=F32)


def dot_right(former, latter):
    return lax.dot_general(former, latter, (((1,), (1,)), ((), ())), preferred_element_type=F32)


def dot_exact(former, latter):
    return jnp.dot(former, latter, preferred_element_type=F32, precision=HIGHEST)


def column_of(row):
    count = row.shape[1]
    same = lax.broadcasted_iota(jnp.int32, (count, count), 0) == lax.broadcasted_iota(
        jnp.int32, (count, count), 1
    )
    return jnp.sum(jnp.where(same, row.astype(F32), 0.0), axis=1, keepdims=True)


def slots_by_tokens(route_row, tokens):
    column = column_of(route_row).astype(jnp.int32)
    lanes = lax.broadcasted_iota(jnp.int32, (route_row.shape[1], tokens), 1)
    return (column == lanes).astype(F32)


def tokens_by_slots(route_row, tokens):
    rows = lax.broadcasted_iota(jnp.int32, (tokens, route_row.shape[1]), 0)
    return (rows == route_row).astype(F32)


def normed(rows, gain):
    return rows * lax.rsqrt(jnp.mean(rows * rows, -1, keepdims=True) + EPSILON) * gain


def norm_back(rows, gain, grad):
    inverse = lax.rsqrt(jnp.mean(rows * rows, -1, keepdims=True) + EPSILON)
    plain = rows * inverse
    scaled = grad * gain
    inner = jnp.mean(scaled * plain, -1, keepdims=True)
    return inverse * (scaled - plain * inner), jnp.sum(grad * plain, 0, keepdims=True)


def sigmoid(value):
    return 1.0 / (1.0 + jnp.exp(-value))


def segment(place, first, last):
    return (place >= first).astype(F32) + (place >= last).astype(F32)


def gelu_parts(value):
    slope = math.sqrt(2.0 / math.pi)
    square = value * value
    bent = jnp.tanh(slope * value * (1.0 + 0.044715 * square))
    half = 0.5 * (1.0 + bent)
    rise = half + 0.5 * value * (1.0 - bent * bent) * slope * (1.0 + 3 * 0.044715 * square)
    return value * half, rise


def place(tok_rows, bounds):
    lead = lax.axis_index("seq") * tok_rows
    group = lax.axis_index("dp")
    return lead, bounds[group, 0], bounds[group, 1]


def select_kernel(bounds, routes, tokens, packet):
    count, width = tokens.shape
    lead, first, last = place(count, bounds)
    row = routes[1:2, :]
    chosen = slots_by_tokens(row, count).astype(BF16)
    packet[:, :width] = dot(chosen, tokens[...]).astype(BF16)
    column = column_of(row)
    tag = jnp.where(column >= 0, segment(column.astype(jnp.int32) + lead, first, last), -1.0)
    packet[:, width:] = jnp.broadcast_to(tag, (tag.shape[0], 128)).astype(BF16)


def project_kernel(
    routes, tokens, gain, router, light_query, light_keyval, heavy_query,
    low, query, keyval, rows_query, rows_keyval, query_heavy, score_query,
):
    count = tokens.shape[0]
    width = tokens.shape[1]
    low[...] = normed(tokens[...].astype(F32), gain[...]).astype(BF16)
    widen(query, slice(None), 0, dot(low[...], light_query[...]).astype(BF16), 0.0)
    pair = dot(low[...], light_keyval[...]).astype(BF16)
    widen(keyval, slice(None), 0, pair[:, :width], 0.0)
    widen(keyval, slice(None), LH * 128, pair[:, width:], 1.0)
    chosen = slots_by_tokens(routes[0:1, :], count).astype(BF16)
    raw = dot(chosen, tokens[...])
    rows = normed(raw, gain[...])
    logit = jnp.sum(rows * router[0:1, :], -1, keepdims=True)
    score_query[...] = jnp.broadcast_to(sigmoid(logit), score_query.shape)
    rows_query[...] = dot(chosen, low[...]).astype(BF16)
    query_heavy[...] = dot(rows_query[...], heavy_query[...]).astype(BF16)
    chosen = slots_by_tokens(routes[1:2, :], count).astype(BF16)
    rows_keyval[...] = dot(chosen, low[...]).astype(BF16)


def widen(ref, rows, start, value, filler):
    size = value.shape[1] // LH
    rest = jnp.full((value.shape[0], 128 - size), filler, BF16)
    for head in range(LH):
        base = start + head * 128
        ref[rows, base : base + size] = value[:, head * size : (head + 1) * size]
        ref[rows, base + size : base + 128] = rest


def light_mask(tok_rows, length, bounds, step):
    lead, first, last = place(tok_rows, bounds)
    shape = (3 * WINDOW, WINDOW)
    query_place = lead + step * WINDOW + lax.broadcasted_iota(jnp.int32, shape, 1)
    key_place = lead + (step - 1) * WINDOW + lax.broadcasted_iota(jnp.int32, shape, 0)
    allowed = (key_place >= 0) & (key_place < length)
    allowed = allowed & (jnp.abs(query_place - key_place) <= WINDOW)
    return allowed & (segment(query_place, first, last) == segment(key_place, first, last))


def light_forward_kernel(
    length, bounds, query, keyval, low, above, below, gain, light_keyval,
    attended, peaks, span_low, span,
):
    tok_rows, width = low.shape
    size = width // LH
    values_start = LH * 128
    scale = size ** (-0.5) / math.log(2.0)
    own = slice(WINDOW, WINDOW + tok_rows)
    span_low[own] = low[...]
    span[own] = keyval[...]
    for rows, signal in ((slice(0, WINDOW), above), (slice(WINDOW + tok_rows, None), below)):
        span_low[rows] = normed(signal[...].astype(F32), gain[...]).astype(BF16)
        pair = dot(span_low[rows], light_keyval[...]).astype(BF16)
        widen(span, rows, 0, pair[:, :width], 0.0)
        widen(span, rows, values_start, pair[:, width:], 1.0)
    for step in range(tok_rows // WINDOW):
        rows = slice(step * WINDOW, (step + 1) * WINDOW)
        keys = slice(step * WINDOW, (step + 3) * WINDOW)
        allowed = light_mask(tok_rows, length, bounds, step)
        for head in range(LH):
            wide = slice(head * 128, (head + 1) * 128)
            values = slice(values_start + head * 128, values_start + (head + 1) * 128)
            scores = jnp.where(allowed, dot_right(span[keys, wide], query[rows, wide]), MASKED)
            peak = jnp.max(scores, 0, keepdims=True)
            exponent = jnp.exp2((scores - peak) * scale)
            total = jnp.sum(exponent, 0, keepdims=True)
            result = dot_left(exponent.astype(BF16), span[keys, values])
            result = result[:, :size] * (1.0 / result[:, size : size + 1])
            attended[rows, head * size : (head + 1) * size] = result.astype(BF16)
            peaks[head : head + 1, rows] = peak * scale + jnp.log2(total)


def light_half(
    half, length, bounds, query, span, peaks, grad, attended, grad_query, grad_keys, grad_values,
):
    tok_rows, width = grad.shape
    size = width // LH
    heads = LH // 2
    scale = size ** (-0.5) / math.log(2.0)
    lanes = slice(half * heads * size, (half + 1) * heads * size)
    product = grad[:, lanes].astype(F32) * attended[:, lanes].astype(F32)
    high = product.astype(BF16)
    rest = (product - high.astype(F32)).astype(BF16)
    shape = (8, heads * size)
    column = lax.broadcasted_iota(jnp.int32, shape, 1)
    row = lax.broadcasted_iota(jnp.int32, shape, 0)
    pickers = ((column >= row * size) & (column < (row + 1) * size)).astype(BF16)
    inners = dot_right(pickers, high) + dot_right(pickers, rest)
    grad_keys[...] = jnp.zeros_like(grad_keys)
    grad_values[...] = jnp.zeros_like(grad_values)
    for step in range(tok_rows // WINDOW):
        rows = slice(step * WINDOW, (step + 1) * WINDOW)
        keys = slice(step * WINDOW, (step + 3) * WINDOW)
        allowed = light_mask(tok_rows, length, bounds, step)
        for index in range(heads):
            head = half * heads + index
            wide = slice(head * 128, (head + 1) * 128)
            start = LH * 128 + head * 128
            here = slice(index * 128, (index + 1) * 128)
            columns = slice(head * size, (head + 1) * size)
            scores = dot_right(span[keys, wide], query[rows, wide]) * scale
            weights = jnp.exp2(
                jnp.where(allowed, scores, MASKED) - peaks[head : head + 1, rows]
            )
            given = grad[rows, columns]
            grad_weights = dot_right(span[keys, start : start + size], given)
            inner = inners[index : index + 1, rows]
            grad_scores = (weights * (grad_weights - inner)).astype(BF16)
            result = dot_left(grad_scores, span[keys, wide])[:, :size] * size ** (-0.5)
            grad_query[rows, index * size : (index + 1) * size] = result.astype(BF16)
            grad_keys[keys, here] += dot(grad_scores, query[rows, wide])
            grad_values[keys, index * 128 : index * 128 + size] += dot(weights.astype(BF16), given)


def narrow(grad_span, grad_keys, grad_values):
    half = grad_span.shape[1] // 2
    size = 2 * half // LH
    for head in range(LH // 2):
        here = slice(head * 128, head * 128 + size)
        columns = slice(head * size, (head + 1) * size)
        grad_span[:, columns] = (grad_keys[:, here] * size ** (-0.5)).astype(BF16)
        columns = slice(half + head * size, half + (head + 1) * size)
        grad_span[:, columns] = grad_values[:, here].astype(BF16)


def light_first_kernel(
    length, bounds, query, span, peaks, grad, attended, grad_query, grad_span, grad_keys, grad_values
):
    light_half(
        0, length, bounds, query, span, peaks, grad, attended, grad_query, grad_keys, grad_values
    )
    narrow(grad_span, grad_keys, grad_values)


def light_second_kernel(
    length, bounds, query, span, peaks, grad, attended, first_span,
    grad_query, grad_span, grad_above, grad_below, grad_keys, grad_values,
):
    light_half(
        1, length, bounds, query, span, peaks, grad, attended, grad_query, grad_keys, grad_values
    )
    narrow(grad_span, grad_keys, grad_values)
    half = grad_span.shape[1] // 2
    count = grad_span.shape[0]
    for ref, rows in ((grad_above, slice(0, WINDOW)), (grad_below, slice(count - WINDOW, count))):
        ref[:, :half] = first_span[rows, :half]
        ref[:, half : 2 * half] = grad_span[rows, :half]
        ref[:, 2 * half : 3 * half] = first_span[rows, half:]
        ref[:, 3 * half :] = grad_span[rows, half:]


def light_products_kernel(
    span_low, first_query, second_query, first_span, second_span, attended, grad_residual, kept, sent
):
    tok_rows, width = attended.shape
    quarter = width // 4
    half = width // 2
    core = lax.axis_index("dp") % 2
    own = slice(WINDOW, WINDOW + tok_rows)
    for part in range(4):
        grad_span = (first_span, second_span)[part % 2]
        columns = slice((part // 2) * half, (part // 2 + 1) * half)
        keyval_part = dot_left(span_low[...], grad_span[:, columns]).astype(BF16)
        grad_query = (first_query, second_query)[part // 2]
        columns = slice((part % 2) * quarter, (part % 2 + 1) * quarter)
        query_part = dot_left(span_low[own], grad_query[:, columns]).astype(BF16)
        columns = slice(part * quarter, (part + 1) * quarter)
        output_part = dot_left(attended[...], grad_residual[:, columns]).astype(BF16)
        for ref, chosen in ((kept, core == part % 2), (sent, core != part % 2)):

            @pl.when(chosen)
            def _(ref=ref, x=part // 2, parts=(keyval_part, query_part, output_part)):
                ref[x, :, : 2 * quarter] = parts[0]
                ref[x, :, 2 * quarter : 3 * quarter] = parts[1]
                ref[x, :, 3 * quarter :] = parts[2]


def heavy_forward_kernel(
    count, bounds, routes, gathered, query_heavy, score_query, gain, router, heavy_keyval,
    keyval, attended, scaled, peaks, own_values, score_keyval,
):
    width = query_heavy.shape[1]
    slots = query_heavy.shape[0]
    total_rows = gathered.shape[0]
    part = min(512, total_rows)
    for start in range(0, total_rows, part):
        rows = slice(start, start + part)
        signal = normed(gathered[rows, :width].astype(F32), gain[...])
        logit = jnp.sum(signal * router[1:2, :], -1, keepdims=True)
        score = sigmoid(logit)
        raw = dot(signal.astype(BF16), heavy_keyval[...])
        keyval[rows, :width] = raw[:, :width].astype(BF16)
        keyval[rows, width:] = (score * raw[:, width:]).astype(BF16)
        if start == 0:
            own_values[...] = raw[:slots, width:]
            score_keyval[...] = jnp.broadcast_to(score[:slots], score_keyval.shape)
    allowed = heavy_mask(count, bounds, routes, gathered, width)
    lanes = lax.broadcasted_iota(jnp.int32, (slots, 128), 1)
    kept = jnp.zeros((slots, 128), F32)
    for head in range(width // HHS):
        columns = slice(head * HHS, (head + 1) * HHS)
        values = slice(width + head * HHS, width + (head + 1) * HHS)
        scores = dot_right(query_heavy[:, columns], keyval[:, columns]) * HHS ** (-0.5)
        scores = jnp.where(allowed, scores, MASKED)
        peak = jnp.max(scores, -1, keepdims=True)
        exponent = jnp.where(allowed, jnp.exp(scores - peak), 0.0)
        total = jnp.sum(exponent, -1, keepdims=True)
        total = jnp.where(total > 0, total, 1.0)
        weights = (exponent * (1.0 / total)).astype(BF16)
        result = dot(weights, keyval[:, values])
        attended[:, columns] = result
        scaled[:, columns] = (score_query[:, :1] * result).astype(BF16)
        kept = jnp.where(lanes == head, peak + jnp.log(total), kept)
    peaks[...] = kept


def heavy_mask(count, bounds, routes, gathered, width):
    lead, first, last = place(count, bounds)
    pickers = (lax.broadcasted_iota(jnp.int32, (8, 128), 1) == 0).astype(BF16)
    key_segment = dot_right(pickers, gathered[:, width:])[:1]
    return own_segment(routes, lead, first, last) == key_segment


def own_segment(routes, lead, first, last):
    column = column_of(routes[0:1, :])
    spot = jnp.where(column >= 0, column.astype(jnp.int32) + lead, -1)
    return segment(spot, first, last)


def residual_kernel(
    routes, tokens, attended, light_output, scaled, heavy_output, gain, router, cotangent,
    residual, low, rows_feed, score_feed, cotangent_rows, grad_raw,
):
    count = tokens.shape[0]
    spread = tokens_by_slots(routes[0:1, :], count).astype(BF16)
    scattered = dot(spread, scaled[...]).astype(BF16)
    residual[...] = (
        tokens[...].astype(F32)
        + dot(attended[...], light_output[...])
        + dot(scattered, heavy_output[...])
    )
    signal = normed(residual[...], gain[...])
    low[...] = signal.astype(BF16)
    logit = jnp.sum(signal * router[2:3, :], -1, keepdims=True)
    chosen = slots_by_tokens(routes[2:3, :], count)
    logit = dot_exact(chosen, jnp.broadcast_to(logit, (count, 128)))
    score = sigmoid(logit)
    score_feed[...] = score
    chosen = chosen.astype(BF16)
    rows_feed[...] = dot(chosen, low[...]).astype(BF16)
    rows = dot(chosen, cotangent[...])
    cotangent_rows[...] = rows
    grad_raw[...] = (score[:, :1] * rows).astype(BF16)


def feed_step(rows_feed, grad_raw, gate_weight, up_weight, reduce_weight, raw, grad_rows):
    @pl.when(pl.program_id(0) == 0)
    def _():
        raw[...] = jnp.zeros_like(raw)
        grad_rows[...] = jnp.zeros_like(grad_rows)

    gate = dot(rows_feed[...], gate_weight[...])
    up = dot(rows_feed[...], up_weight[...])
    bent, rise = gelu_parts(gate)
    gated_low = (bent * up).astype(BF16)
    raw[...] += dot(gated_low, reduce_weight[...])
    grad_gated = dot_right(grad_raw[...], reduce_weight[...])
    gate_low = (grad_gated * up * rise).astype(BF16)
    up_low = (grad_gated * bent).astype(BF16)
    grad_rows[...] += dot_right(gate_weight[...], gate_low) + dot_right(up_weight[...], up_low)
    return gated_low, gate_low, up_low


def heavy_feed_kernel(
    rows_feed, grad_raw, gate_weight, up_weight, reduce_weight,
    raw, grad_rows, gated, grad_gate, grad_up,
):
    gated_low, gate_low, up_low = feed_step(
        rows_feed, grad_raw, gate_weight, up_weight, reduce_weight, raw, grad_rows
    )
    gated[...] = gated_low
    grad_gate[...] = gate_low
    grad_up[...] = up_low


def heavy_feed_split_kernel(
    rows_feed, grad_raw, gate_weight, up_weight, reduce_weight,
    raw, grad_rows, kept, sent, own, moved,
):
    gated_low, gate_low, up_low = feed_step(
        rows_feed, grad_raw, gate_weight, up_weight, reduce_weight, raw, grad_rows
    )
    step = pl.program_id(0)
    width, part = rows_feed.shape[1], gated_low.shape[1]
    half = kept.shape[1] // 2
    start = pl.multiple_of((step % 2) * part, part)
    mine = step // 2 == lax.axis_index("dp") % 2

    @pl.when(mine)
    def _():
        kept[:, pl.ds(start, part)] = gate_low
        kept[:, pl.ds(half + start, part)] = up_low

    @pl.when(jnp.logical_not(mine))
    def _():
        sent[:, pl.ds(width + start, part)] = gate_low
        sent[:, pl.ds(width + half + start, part)] = up_low

    y = lax.axis_index("seq") % 2
    spot = pl.multiple_of(step * (part // 2), part // 2)
    even, odd = gated_low[:, : part // 2], gated_low[:, part // 2 :]
    own[:, pl.ds(spot, part // 2)] = jnp.where(y == 0, even, odd)
    moved[:, pl.ds(spot, part // 2)] = jnp.where(y == 0, odd, even)

    @pl.when(step == 0)
    def _():
        sent[:, :width] = rows_feed[...]
        moved[:, 2 * part :] = grad_raw[...]


def light_feed_kernel(
    low, cotangent, gate_weight, up_weight, reduce_weight, result, grad_low, gated, grad_gate, grad_up
):
    @pl.when(pl.program_id(0) == 0)
    def _():
        result[...] = jnp.zeros_like(result)
        grad_low[...] = jnp.zeros_like(grad_low)

    gate = dot(low[...], gate_weight[...])
    up = dot(low[...], up_weight[...])
    bent, rise = gelu_parts(gate)
    gated_low = (bent * up).astype(BF16)
    gated[...] = gated_low
    result[...] += dot(gated_low, reduce_weight[...])
    grad_gated = dot_right(cotangent[...], reduce_weight[...])
    gate_low = (grad_gated * up * rise).astype(BF16)
    up_low = (grad_gated * bent).astype(BF16)
    grad_gate[...] = gate_low
    grad_up[...] = up_low
    grad_low[...] += dot_right(gate_low, gate_weight[...]) + dot_right(up_low, up_weight[...])


def feed_products_kernel(low, cotangent, gated, grad_gate, grad_up, kept, sent, turned):
    width = cotangent.shape[1]
    quarter = width // 4
    hidden = gated.shape[1] // 2
    seq, rows = kept.shape[1:3]
    more = rows // 3
    core = lax.axis_index("dp") % 2
    for part in range(4):
        turned[:, part * 256 : part * 256 + quarter] = cotangent[
            :, part * quarter : (part + 1) * quarter
        ]
        turned[:, part * 256 + quarter : (part + 1) * 256] = jnp.zeros(
            (cotangent.shape[0], 256 - quarter), BF16
        )
    for part in range(4):
        grad = (grad_gate, grad_up)[part // 2]
        columns = slice((part % 2) * hidden, (part % 2 + 1) * hidden)
        product = dot_left(low[...], grad[:, columns]).astype(BF16)
        for ref, chosen in ((kept, core == part % 2), (sent, core != part % 2)):

            @pl.when(chosen)
            def _(ref=ref, x=part // 2, product=product):
                for i in range(seq):
                    ref[x, i, :, :hidden] = product[i * rows : (i + 1) * rows]

    for half in range(2):
        columns = slice(half * hidden, (half + 1) * hidden)
        every = dot_left(gated[:, columns], turned[...]).astype(BF16)
        for part in range(4):
            product = every[:, part * 256 : part * 256 + quarter]
            for ref, chosen in ((kept, core == part % 2), (sent, core != part % 2)):

                @pl.when(chosen)
                def _(ref=ref, x=part // 2, product=product, half=half):
                    for i in range(seq // 2):
                        spot = half * (seq // 2) + i
                        start = i * (rows + more)
                        ref[x, spot, :, hidden : hidden + quarter] = product[start : start + rows]
                        rest = product[start + rows : start + rows + more]
                        for piece in range(3):
                            ref[
                                x, spot, piece * more : (piece + 1) * more, hidden + quarter :
                            ] = rest[:, piece * 64 : (piece + 1) * 64]


def turn_kernel(
    routes, residual, gain, result, grad_low, raw, grad_rows, score_feed, cotangent_rows, cotangent,
    router, light_output, heavy_output, heavy_attended, score_query,
    output, grad_residual, grad_residual_low, grad_attended, grad_heavy_rows, grad_heavy_attended,
    logit_query, small,
):
    count = residual.shape[0]
    spread = tokens_by_slots(routes[2:3, :], count)
    score = score_feed[:, :1]
    output[...] = (
        residual[...] + result[...] + dot_exact(spread, score * raw[...])
    ).astype(BF16)
    logit = score * (1.0 - score) * jnp.sum(cotangent_rows[...] * raw[...], -1, keepdims=True)
    grad = grad_low[...] + dot_exact(spread, grad_rows[...].T + logit * router[2:3, :])
    back, gain_grad = norm_back(residual[...], gain[...], grad)
    token_logit = dot_exact(spread, jnp.broadcast_to(logit, (logit.shape[0], 128)))[:, :1]
    signal = normed(residual[...], gain[...])
    small[0:1] = gain_grad
    small[1:2] = jnp.sum(token_logit * signal, 0, keepdims=True)
    total = cotangent[...].astype(F32) + back
    grad_residual[...] = total
    grad_residual_low[...] = total.astype(BF16)
    grad_attended[...] = dot_right(grad_residual_low[...], light_output[...]).astype(BF16)
    chosen = slots_by_tokens(routes[0:1, :], count).astype(BF16)
    grad_heavy_rows[...] = dot(chosen, grad_residual_low[...]).astype(BF16)
    scaled = dot_right(grad_heavy_rows[...], heavy_output[...])
    score = score_query[:, :1]
    logit = score * (1.0 - score) * jnp.sum(scaled * heavy_attended[...], -1, keepdims=True)
    logit_query[...] = jnp.broadcast_to(logit, logit_query.shape)
    grad_heavy_attended[...] = (score * scaled).astype(BF16)


def heavy_query_kernel(
    count, bounds, routes, gathered, query_heavy, keyval, peaks, grad, grad_query, packet
):
    slots, width = query_heavy.shape
    heads = width // HHS
    allowed = heavy_mask(count, bounds, routes, gathered, width)
    lanes = lax.broadcasted_iota(jnp.int32, (slots, 128), 1)
    kept = peaks[...]
    lead, first, last = place(count, bounds)
    tag = jnp.where(lanes == 4 * heads, own_segment(routes, lead, first, last), 0.0)
    for head in range(heads):
        columns = slice(head * HHS, (head + 1) * HHS)
        values = slice(width + head * HHS, width + (head + 1) * HHS)
        scores = dot_right(query_heavy[:, columns], keyval[:, columns]) * HHS ** (-0.5)
        peak = jnp.sum(jnp.where(lanes == head, kept, 0.0), -1, keepdims=True)
        weights = jnp.where(allowed, jnp.exp(scores - peak), 0.0)
        grad_weights = dot_right(grad[:, columns], keyval[:, values])
        inner = jnp.sum(weights * grad_weights, -1, keepdims=True)
        grad_scores = (weights * (grad_weights - inner)).astype(BF16)
        grad_query[:, columns] = (dot(grad_scores, keyval[:, columns]) * HHS ** (-0.5)).astype(BF16)
        for lane, value in ((head, peak), (heads + head, inner)):
            high = value.astype(BF16).astype(F32)
            tag = jnp.where(lanes == lane, high, tag)
            tag = jnp.where(lanes == 2 * heads + lane, value - high, tag)
    packet[:, :width] = query_heavy[...]
    packet[:, width : 2 * width] = grad[...]
    packet[:, 2 * width :] = tag.astype(BF16)


def heavy_key_kernel(
    count, bounds, routes, first, second, keyval, own_values, score_keyval, grad_raw, logit_keyval, packets
):
    half = first.shape[0]
    packets[:half] = first[...]
    packets[half:] = second[...]
    slots = own_values.shape[0]
    width = own_values.shape[1]
    heads = width // HHS
    lead, first, last = place(count, bounds)
    column = column_of(routes[1:2, :])
    key_segment = jnp.where(
        column >= 0, segment(column.astype(jnp.int32) + lead, first, last), -1.0
    )
    same = lax.broadcasted_iota(jnp.int32, (128, 128), 0) == lax.broadcasted_iota(
        jnp.int32, (128, 128), 1
    )
    tags = dot_right(same.astype(BF16), packets[:, 2 * width :])
    allowed = key_segment == tags[4 * heads : 4 * heads + 1]
    score = score_keyval[:, :1]
    logit = jnp.zeros((slots, 1), F32)
    for head in range(heads):
        columns = slice(head * HHS, (head + 1) * HHS)
        values = slice(width + head * HHS, width + (head + 1) * HHS)
        peak = tags[head : head + 1] + tags[2 * heads + head : 2 * heads + head + 1]
        inner = tags[heads + head : heads + head + 1] + tags[3 * heads + head : 3 * heads + head + 1]
        scores = dot_right(keyval[:slots, columns], packets[:, columns]) * HHS ** (-0.5)
        weights = jnp.where(allowed, jnp.exp(scores - peak), 0.0)
        grad_weights = dot_right(keyval[:slots, values], packets[:, values])
        grad_scores = (weights * (grad_weights - inner)).astype(BF16)
        key_grad = dot(grad_scores, packets[:, columns]) * HHS ** (-0.5)
        value_grad = dot(weights.astype(BF16), packets[:, values]).astype(BF16).astype(F32)
        logit += jnp.sum(value_grad * own_values[:, columns], -1, keepdims=True)
        grad_raw[:, columns] = key_grad.astype(BF16)
        grad_raw[:, values] = (score * value_grad).astype(BF16)
    logit_keyval[...] = jnp.broadcast_to(score * (1.0 - score) * logit, logit_keyval.shape)


def mixer_light_kernel(
    first_query, second_query, first_span, second_span, from_below, from_above, light_query,
    light_keyval, grad, total_keyval,
):
    count, half = first_query.shape
    own = slice(WINDOW, WINDOW + count)
    for i, (ref, base) in enumerate(
        ((first_span, 0), (second_span, 0), (first_span, half), (second_span, half))
    ):
        total_keyval[:, i * half : (i + 1) * half] = ref[own, base : base + half]
    for rows, more in (
        (slice(0, WINDOW), from_below),
        (slice(count - WINDOW, count), from_above),
    ):
        total_keyval[rows] = (total_keyval[rows].astype(F32) + more[...].astype(F32)).astype(BF16)
    grad[...] = (
        dot_right(first_query[...], light_query[:, :half])
        + dot_right(second_query[...], light_query[:, half:])
        + dot_right(total_keyval[...], light_keyval[...])
    )


def mixer_kernel(
    routes, tokens, gain, router, grad_residual, grad_light, grad_heavy_query, grad_raw_keyval,
    logit_query, logit_keyval, heavy_query, heavy_keyval, feed_small, tokens_grad, small,
):
    count = tokens.shape[0]
    spread_query = tokens_by_slots(routes[0:1, :], count)
    spread_keyval = tokens_by_slots(routes[1:2, :], count)
    query_rows = dot_right(grad_heavy_query[...], heavy_query[...])
    query_rows += logit_query[:, :1] * router[0:1, :]
    keyval_rows = dot_right(grad_raw_keyval[...], heavy_keyval[...])
    keyval_rows += logit_keyval[:, :1] * router[1:2, :]
    grad = (
        grad_light[...]
        + dot_exact(spread_query, query_rows)
        + dot_exact(spread_keyval, keyval_rows)
    )
    signal = tokens[...].astype(F32)
    back, gain_grad = norm_back(signal, gain[...], grad)
    tokens_grad[...] = (grad_residual[...] + back).astype(BF16)
    signal = normed(signal, gain[...])
    small[0:1] = gain_grad
    small[1:2] = feed_small[0:1]
    small[2:3] = jnp.sum(dot_exact(spread_query, logit_query[...])[:, :1] * signal, 0, keepdims=True)
    small[3:4] = jnp.sum(dot_exact(spread_keyval, logit_keyval[...])[:, :1] * signal, 0, keepdims=True)
    small[4:5] = feed_small[1:2]
    small[5:8] = jnp.zeros((3, small.shape[1]), F32)


def estimate(weight, size):
    return pl.CostEstimate(
        flops=int(weight * 1e9), bytes_accessed=20 * size, transcendentals=0
    )


def without(body, start, count):
    def inner(*refs):
        return body(*refs[:start], *refs[start + count :])

    return inner


def run(body, outs, ins, limit, weight=0, scratch=(), smem=0, deps=()):
    vmem = pl.BlockSpec(memory_space=pltpu.VMEM)
    size = sum(v.size * v.dtype.itemsize for v in ins) + sum(
        math.prod(shape) * jnp.dtype(kind).itemsize for shape, kind in outs
    )
    return pl.pallas_call(
        without(body, len(ins), len(deps)),
        out_shape=[jax.ShapeDtypeStruct(shape, kind) for shape, kind in outs],
        in_specs=[pl.BlockSpec(memory_space=pltpu.SMEM)] * smem
        + [vmem] * (len(ins) - smem)
        + [pl.BlockSpec(memory_space=pl.ANY)] * len(deps),
        out_specs=[vmem] * len(outs),
        scratch_shapes=list(scratch),
        compiler_params=pltpu.CompilerParams(vmem_limit_bytes=int(limit * MIB)),
        cost_estimate=estimate(weight, size),
    )(*ins, *deps)


def heavy_feed(rows_feed, grad_raw, heavy_expand, heavy_reduce, seq, deps):
    slots, width = rows_feed.shape
    hidden = heavy_reduce.shape[0]
    steps = 4
    part = hidden // steps
    fixed = pl.BlockSpec((slots, width), lambda j: (0, 0))
    moving = pl.BlockSpec((slots, part), lambda j: (0, j))
    split = seq == 8
    if split:
        columns = [hidden, width + hidden, 2 * part, 2 * part + width]
        specs = [pl.BlockSpec((slots, c), lambda j: (0, 0)) for c in columns]
    else:
        columns, specs = [hidden] * 3, [moving] * 3
    return pl.pallas_call(
        without(heavy_feed_split_kernel if split else heavy_feed_kernel, 5, len(deps)),
        grid=(steps,),
        out_shape=[
            jax.ShapeDtypeStruct((slots, width), F32),
            jax.ShapeDtypeStruct((width, slots), F32),
        ]
        + [jax.ShapeDtypeStruct((slots, c), BF16) for c in columns],
        in_specs=[
            fixed,
            fixed,
            pl.BlockSpec((width, part), lambda j: (0, j)),
            pl.BlockSpec((width, part), lambda j: (0, steps + j)),
            pl.BlockSpec((part, width), lambda j: (j, 0)),
        ]
        + [pl.BlockSpec(memory_space=pl.ANY)] * len(deps),
        out_specs=[fixed, pl.BlockSpec((width, slots), lambda j: (0, 0))] + specs,
        compiler_params=pltpu.CompilerParams(vmem_limit_bytes=32 * MIB),
        cost_estimate=estimate(75, 20 << 20),
    )(rows_feed, grad_raw, heavy_expand, heavy_expand, heavy_reduce, *deps)


def light_feed(low, cotangent, light_expand, light_reduce, deps):
    count, width = low.shape
    hidden = light_reduce.shape[0]
    part = hidden // 2
    fixed = pl.BlockSpec((count, width), lambda j: (0, 0))
    moving = pl.BlockSpec((count, part), lambda j: (0, j))
    return pl.pallas_call(
        without(light_feed_kernel, 5, len(deps)),
        grid=(2,),
        out_shape=[jax.ShapeDtypeStruct((count, width), F32)] * 2
        + [jax.ShapeDtypeStruct((count, hidden), BF16)] * 3,
        in_specs=[
            fixed,
            fixed,
            pl.BlockSpec((width, part), lambda j: (0, j)),
            pl.BlockSpec((width, part), lambda j: (0, 2 + j)),
            pl.BlockSpec((part, width), lambda j: (j, 0)),
        ]
        + [pl.BlockSpec(memory_space=pl.ANY)] * len(deps),
        out_specs=[fixed] * 2 + [moving] * 3,
        compiler_params=pltpu.CompilerParams(vmem_limit_bytes=32 * MIB),
        cost_estimate=estimate(LONG, 8 << 20),
    )(low, cotangent, light_expand, light_expand, light_reduce, *deps)


def products_kernel(formers, latters, small, products):
    width = formers.shape[1] // 3
    quarter = width // 4
    offsets = ((0, 0, quarter), (1, quarter, quarter), (2, 2 * quarter, 2 * quarter))
    for part, start, columns in offsets:
        products[:, start : start + columns] = dot_left(
            formers[:, part * width : (part + 1) * width], latters[:, start : start + columns]
        ).astype(BF16)
    products[:, width:] = turn_small(small[...])


def outer_kernel(former, latter, product):
    product[...] = dot_left(former[...], latter[...]).astype(BF16)


def fold_kernel(kept, got, left, sent):
    total = (kept[...].astype(F32) + got[...].astype(F32)).astype(BF16)
    half = total.shape[1] // 2
    x = lax.axis_index("dp") // 2
    left[...] = jnp.where(x == 0, total[:, :half], total[:, half:])
    sent[...] = jnp.where(x == 0, total[:, half:], total[:, :half])


def expand_x_kernel(former, kept, got, sent, left):
    slots, width = former.shape
    half = kept.shape[1] // 2
    x = lax.axis_index("dp") // 2
    sent[:slots, :width] = former[...]
    sent[slots:, :width] = got[:, :width]
    for rows, source, base in ((slice(0, slots), kept, 0), (slice(slots, None), got, width)):
        gate, up = source[:, base : base + half], source[:, base + half : base + 2 * half]
        left[rows] = jnp.where(x == 0, gate, up)
        sent[rows, width:] = jnp.where(x == 0, up, gate)


def expand_y_kernel(sent_x, left, got, sent, former):
    rows, wide = left.shape
    part = former.shape[1] // 4
    y = lax.axis_index("seq") % 2
    for start, source in ((0, sent_x), (rows, got)):
        here = slice(start, start + rows)
        for i in range(4):
            even = source[:, 2 * i * part : (2 * i + 1) * part]
            odd = source[:, (2 * i + 1) * part : (2 * i + 2) * part]
            columns = slice(i * part, (i + 1) * part)
            former[here, columns] = jnp.where(y == 0, even, odd)
            sent[here, columns] = jnp.where(y == 0, odd, even)
    sent[:rows, 4 * part :] = left[...]
    sent[rows:, 4 * part :] = got[:, 8 * part :]


def reduce_z_kernel(own, grad_raw, got, kept, first, second, third):
    slots, wide = own.shape
    part = wide // 4
    z = lax.axis_index("seq") // 2
    for step, ref in enumerate((kept, first, second, third)):
        spot = pl.multiple_of(((z + step) % 4) * part, part)
        ref[:slots, :part] = own[:, pl.ds(spot, part)]
        ref[slots:, :part] = got[:, pl.ds(spot, part)]
        ref[:slots, part:] = grad_raw[...]
        ref[slots:, part:] = got[:, wide:]


def expand_product_kernel(sent, got, former, own, first, second, third, slices):
    base = former.shape[1]
    product = dot_left(former[...], sent[:, base:])
    product += dot_left(got[:, :base], got[:, base:])
    part = own.shape[0]
    for i in range(4):
        slices[i] = product[i * part : (i + 1) * part].astype(BF16)
    z = lax.axis_index("seq") // 2
    for step, ref in enumerate((own, first, second, third)):
        ref[...] = slices[(z + step) % 4]


def reduce_product_kernel(own, first, second, third, kept, moved, turned):
    half = kept.shape[0]
    quarter = (own.shape[1] - half) // 4
    product = None
    for source in (own, first, second, third):
        for spot, i in enumerate((0, 2, 1, 3)):
            start = half + i * quarter
            turned[:, spot * quarter : (spot + 1) * quarter] = source[:, start : start + quarter]
        term = dot_left(source[:, :half], turned[...])
        product = term if product is None else product + term
    core = lax.axis_index("dp") % 2
    low, high = product[:, : 2 * quarter], product[:, 2 * quarter :]
    kept[...] = jnp.where(core == 0, low, high).astype(BF16)
    moved[...] = jnp.where(core == 0, high, low).astype(BF16)


def stack_kernel(own, first, second, third, stacked):
    rows = own.shape[0]
    for i, ref in enumerate((own, first, second, third)):
        stacked[i * rows : (i + 1) * rows] = ref[...]


def rows_kernel(rows_query, scaled, rows_keyval, joined):
    width = rows_query.shape[1]
    for i, ref in enumerate((rows_query, scaled, rows_keyval)):
        joined[:, i * width : (i + 1) * width] = ref[...]


def stack_two_kernel(first, second, stacked):
    rows = first.shape[0]
    stacked[:rows] = first[...]
    stacked[rows:] = second[...]


def heavy_core_kernel(grad_query, grad_rows, grad_keyval, sent, kept):
    width = grad_query.shape[1]
    quarter = width // 4
    core = lax.axis_index("dp") % 2
    for x in range(2):
        spot = x * width
        for source, columns in ((grad_query, quarter), (grad_rows, quarter), (grad_keyval, 2 * quarter)):
            even = source[:, 2 * x * columns : (2 * x + 1) * columns]
            odd = source[:, (2 * x + 1) * columns : (2 * x + 2) * columns]
            kept[:, spot : spot + columns] = jnp.where(core == 0, even, odd)
            sent[:, spot : spot + columns] = jnp.where(core == 0, odd, even)
            spot += columns


def heavy_x_kernel(kept, got, sent, left):
    slots = kept.shape[0]
    width = kept.shape[1] // 2
    x = lax.axis_index("dp") // 2
    for rows, source in ((slice(0, slots), kept), (slice(slots, None), got)):
        low, high = source[:, :width], source[:, width:]
        left[rows] = jnp.where(x == 0, low, high)
        sent[rows] = jnp.where(x == 0, high, low)


def pair_x_kernel(kept, got, left, sent):
    x = lax.axis_index("dp") // 2
    left[...] = (kept[x].astype(F32) + got[x].astype(F32)).astype(BF16)
    sent[...] = (kept[1 - x].astype(F32) + got[1 - x].astype(F32)).astype(BF16)


def pair_y_kernel(left, got, kept, sent):
    y = lax.axis_index("seq") % 2
    for i in range(4):
        mine, other = 2 * i + y, 2 * i + 1 - y
        kept[i] = (left[mine].astype(F32) + got[mine].astype(F32)).astype(BF16)
        sent[i] = (left[other].astype(F32) + got[other].astype(F32)).astype(BF16)


def pair_z_kernel(kept, got, own, first, second, third):
    z = lax.axis_index("seq") // 2
    for step, ref in enumerate((own, first, second, third)):
        spot = (z + step) % 4
        ref[...] = (kept[spot].astype(F32) + got[spot].astype(F32)).astype(BF16)


def heavy_y_kernel(own_rows, got_rows, left, got, small, kept, sent, total):
    width = left.shape[1]
    quarter = width // 4
    for part, start, columns in ((0, 0, quarter), (1, quarter, quarter), (2, 2 * quarter, 2 * quarter)):
        former = slice(part * width, (part + 1) * width)
        here = slice(start, start + columns)
        product = dot_left(own_rows[:, former], left[:, here])
        product += dot_left(got_rows[:, former], got[:, here])
        total[:, here] = product.astype(BF16)
    total[:, width:] = turn_small(small[...])
    y = lax.axis_index("seq") % 2
    rows = width // 8
    for i in range(4):
        even = total[2 * i * rows : (2 * i + 1) * rows]
        odd = total[(2 * i + 1) * rows : (2 * i + 2) * rows]
        kept[i] = jnp.where(y == 0, even, odd)
        sent[i] = jnp.where(y == 0, odd, even)


def turn_small(small):
    high = small.astype(BF16)
    low = (small - high.astype(F32)).astype(BF16)
    same = (
        lax.broadcasted_iota(jnp.int32, (small.shape[0], 128), 0)
        == lax.broadcasted_iota(jnp.int32, (small.shape[0], 128), 1)
    ).astype(BF16)
    return (dot_left(high, same) + dot_left(low, same)).astype(BF16)


def total_of(blocks):
    total = blocks[0][...].astype(F32)
    for block in blocks[1:]:
        total = total + block[...].astype(F32)
    return total


def light_end_kernel(own, first, second, third, query, keyval, output):
    total = total_of((own, first, second, third))
    quarter = query.shape[1]
    keyval[...] = total[:, : 2 * quarter]
    query[...] = total[:, 2 * quarter : 3 * quarter]
    output[...] = total[:, 3 * quarter :]


def heavy_end_kernel(own, first, second, third, query, keyval, output, small):
    total = total_of((own, first, second, third))
    quarter = query.shape[1]
    query[...] = total[:, :quarter]
    output[...] = total[:, quarter : 2 * quarter]
    keyval[...] = total[:, 2 * quarter : 4 * quarter]
    same = (
        lax.broadcasted_iota(jnp.int32, (8, 128), 0)
        == lax.broadcasted_iota(jnp.int32, (8, 128), 1)
    ).astype(F32)
    small[...] = lax.dot_general(
        same,
        total[:, 4 * quarter :],
        (((1,), (1,)), ((), ())),
        preferred_element_type=F32,
        precision=HIGHEST,
    )


def feed_end_kernel(own, first, second, third, expand, reduce):
    total = total_of((own, first, second, third))
    hidden, quarter = expand.shape[1], reduce.shape[1]
    rows = total.shape[0]
    more = rows // 3
    expand[...] = total[:, :hidden]
    reduce[:rows] = total[:, hidden : hidden + quarter]
    for piece in range(3):
        reduce[rows:, piece * 64 : (piece + 1) * 64] = total[
            piece * more : (piece + 1) * more, hidden + quarter :
        ]


def stages(count):
    found, stride = [], 1
    while count > 1:
        size = 4 if count % 4 == 0 and count != 8 else 2
        found.append((size, stride))
        stride, count = stride * size, count // size
    return found


def shifted(block, axis, size, stride, step):
    route = []
    for i in range(lax.axis_size(axis)):
        member = (i // stride) % size
        route.append((i, i + ((member + step) % size - member) * stride))
    return lax.ppermute(block, axis, route)


def neighbours(block, distance):
    devices = range(lax.axis_size("seq"))
    return lax.ppermute(
        block, "seq", [(i - distance, i) for i in devices if i - distance in devices]
    )


def member_of(axis, size, stride):
    return (lax.axis_index(axis) // stride) % size


def pick(block, index, dim):
    return lax.dynamic_index_in_dim(block, index, dim, keepdims=False)


def reduce_stage(block, axis, size, stride, dim):
    me = member_of(axis, size, stride)
    total = pick(block, me, dim).astype(F32)
    for step in range(1, size):
        sent = pick(block, (me + step) % size, dim)
        total = total + shifted(sent, axis, size, stride, step).astype(F32)
    return total.astype(BF16)


def reduce_dp(block):
    block = reduce_stage(block, "dp", 2, 1, 0)
    half = block.shape[1] // 2
    first, second = block[:, :half], block[:, half:]
    x = member_of("dp", 2, 2)
    got = shifted(jnp.where(x == 0, second, first), "dp", 2, 2, 1)
    return (jnp.where(x == 0, first, second).astype(F32) + got.astype(F32)).astype(BF16)


def reduce_seq(block, skip=0):
    for size, stride in stages(lax.axis_size("seq"))[skip:]:
        count = lax.axis_size("seq") // stride
        block = block.reshape(count // size, size, block.shape[0] // count, block.shape[1])
        block = reduce_stage(block, "seq", size, stride, 1)
        block = block.reshape(-1, block.shape[-1])
    return block


def gather_part(block, size, stride):
    return jnp.concatenate(
        [block] + [shifted(block, "seq", size, stride, step) for step in range(1, size)], 0
    )


def gather_seq(block):
    for size, stride in stages(lax.axis_size("seq"))[::-1]:
        block = gather_part(block, size, stride)
    return block


def total_parts(parts):
    total = parts[0].astype(F32)
    for part in parts[1:]:
        total = total + part.astype(F32)
    return total


def reduce_pair(kept, sent):
    block = (kept.astype(F32) + shifted(sent, "dp", 2, 1, 1).astype(F32)).astype(BF16)
    return reduce_stage(block, "dp", 2, 2, 0).reshape(-1, block.shape[3])


def swap_rows(axis, stride, whole, mine, other):
    got = shifted(jnp.concatenate([whole, other], 1), axis, 2, stride, 1)
    width = whole.shape[1]
    return (
        jnp.concatenate([whole, got[:, :width]], 0),
        jnp.concatenate([mine, got[:, width:]], 0),
    )


def gather_dp(former, first, second):
    core, x = member_of("dp", 2, 1), member_of("dp", 2, 2)
    half = first.shape[1] // 2

    def both(low, high):
        return jnp.concatenate([low, high], 1)

    lows = both(first[:, :half], second[:, :half])
    highs = both(first[:, half:], second[:, half:])
    former, latter = swap_rows(
        "dp", 1, former, jnp.where(core == 0, lows, highs), jnp.where(core == 0, highs, lows)
    )
    low, high = latter[:, :half], latter[:, half:]
    return swap_rows(
        "dp", 2, former, jnp.where(x == 0, low, high), jnp.where(x == 0, high, low)
    )


def split_rows(former, latter, size, stride):
    rows, width = former.shape
    count = lax.axis_size("seq") // stride
    former = former.reshape(rows, count // size, size, width // count)
    me = member_of("seq", size, stride)
    formers, latters = [pick(former, me, 2).reshape(rows, width // size)], [latter]
    for step in range(1, size):
        other = pick(former, (me + step) % size, 2).reshape(rows, width // size)
        got = shifted(jnp.concatenate([other, latter], 1), "seq", size, stride, step)
        formers.append(got[:, : width // size])
        latters.append(got[:, width // size :])
    return jnp.concatenate(formers, 0), jnp.concatenate(latters, 0)


def outer(former, latter):
    rows, width = former.shape
    columns = latter.shape[1]
    return run(
        outer_kernel, [((width, columns), BF16)], [former, latter], 24, 2e-9 * rows * width * columns
    )[0]


def expand_gradient(former, gate, up):
    former, latter = gather_dp(former, gate, up)
    size, stride = stages(lax.axis_size("seq"))[0]
    former, latter = split_rows(former, latter, size, stride)
    return reduce_seq(outer(former, latter), 1)


def reduce_gradient(former, latter):
    for size, stride in stages(lax.axis_size("seq")):
        former, latter = split_rows(former, latter, size, stride)
    quarter = latter.shape[1] // 4
    parts = [latter[:, i * quarter : (i + 1) * quarter] for i in (0, 2, 1, 3)]
    product = outer(former, jnp.concatenate(parts, 1))
    half = product.shape[1] // 2
    return reduce_dp(jnp.stack([product[:, :half], product[:, half:]]))


def sum_dp(block):
    for stride in (1, 2):
        block = block + shifted(block, "dp", 2, stride, 1)
    return block


def pair_x(kept, sent, deps=(), weight=0):
    got = shifted(sent, "dp", 2, 1, 1)
    left, sent = run(
        pair_x_kernel, [(kept.shape[1:], BF16)] * 2, [kept, got], 24, weight, deps=deps
    )
    return left, sent, shifted(sent, "dp", 2, 2, 1)


def pair_y(left, got, deps=(), weight=0):
    shape = (4,) + left.shape[1:]
    kept, sent = run(pair_y_kernel, [(shape, BF16)] * 2, [left, got], 16, weight, deps=deps)
    return kept, sent, shifted(sent, "seq", 2, 1, 1)


def pair_z(kept, got, deps=(), weight=0):
    own, *sent = run(
        pair_z_kernel, [(kept.shape[1:], BF16)] * 4, [kept, got], 16, weight, deps=deps
    )
    return [own] + [shifted(block, "seq", 4, 2, 1 + i) for i, block in enumerate(sent)]


def send_expand(rows_feed, kept, sent, deps):
    slots, width = rows_feed.shape
    wide = kept.shape[1] // 2
    got = shifted(sent, "dp", 2, 1, 1)
    sent, left = run(
        expand_x_kernel,
        [((2 * slots, width + wide), BF16), ((2 * slots, wide), BF16)],
        [rows_feed, kept, got],
        16,
        deps=deps,
    )
    return sent, left, shifted(sent, "dp", 2, 2, 1)


def send_expand_y(sent, left, got, deps=()):
    rows, wide = left.shape
    half = (sent.shape[1] - wide) // 2
    sent, former = run(
        expand_y_kernel,
        [((2 * rows, half + wide), BF16), ((2 * rows, half), BF16)],
        [sent, left, got],
        16,
        deps=deps,
    )
    return sent, shifted(sent, "seq", 2, 1, 1), former


def send_expand_z(sent, got, former, deps=()):
    wide = sent.shape[1] - former.shape[1]
    rows = former.shape[1] // 4
    own, *sent = run(
        expand_product_kernel,
        [((rows, wide), BF16)] * 4,
        [sent, got, former],
        24,
        0,
        [pltpu.VMEM((4, rows, wide), BF16)],
        deps=deps,
    )
    return [own] + [shifted(block, "seq", 4, 2, 1 + i) for i, block in enumerate(sent)]


def send_reduce_z(own, grad_raw, got, deps=()):
    slots, width = grad_raw.shape
    part = own.shape[1] // 4
    own, *sent = run(
        reduce_z_kernel,
        [((2 * slots, part + width), BF16)] * 4,
        [own, grad_raw, got],
        8,
        deps=deps,
    )
    return [own] + [shifted(block, "seq", 4, 2, 1 + i) for i, block in enumerate(sent)]


def send_reduce_core(parts, width, deps=()):
    rows, wide = parts[0].shape
    half = wide - width
    kept, sent = run(
        reduce_product_kernel,
        [((half, width // 2), BF16)] * 2,
        list(parts),
        12,
        0,
        [pltpu.VMEM((rows, width), BF16)],
        deps=deps,
    )
    return kept, sent, shifted(sent, "dp", 2, 1, 1)


def send_reduce_x(kept, got, deps=()):
    shape = (kept.shape[0], kept.shape[1] // 2)
    left, sent = run(fold_kernel, [(shape, BF16)] * 2, [kept, got], 8, deps=deps)
    return left, shifted(sent, "dp", 2, 2, 1)


def send_rows(rows_query, scaled, rows_keyval):
    slots, width = rows_query.shape
    (joined,) = run(
        rows_kernel, [((slots, 3 * width), BF16)], [rows_query, scaled, rows_keyval], 8
    )
    return joined, shifted(joined, "dp", 2, 1, 1)


def send_rows_x(own, got, deps):
    rows, width = own.shape
    (joined,) = run(stack_two_kernel, [((2 * rows, width), BF16)], [own, got], 8, deps=deps)
    return joined, shifted(joined, "dp", 2, 2, 1)


def on_device(
    tokens,
    cotangent,
    document_bounds,
    routes,
    attention_gain,
    feedforward_gain,
    router,
    light_query,
    light_keyval,
    light_output,
    heavy_query,
    heavy_keyval,
    heavy_output_weight,
    light_expand,
    light_reduce,
    heavy_expand,
    heavy_reduce,
):
    count, width = tokens.shape
    slots = routes.shape[1]
    seq = lax.axis_size("seq")
    length = count * seq
    gain, feed_gain = attention_gain[None], feedforward_gain[None]
    heavy_width = heavy_query.shape[1]

    above = neighbours(tokens[count - WINDOW :], 1)
    below = neighbours(tokens[:WINDOW], -1)
    (packet,) = run(
        select_kernel,
        [((slots, width + 128), BF16)],
        [document_bounds, routes, tokens],
        8,
        0,
        smem=1,
    )
    gathered = gather_seq(packet)
    wide = LH * 128
    low, query, keyval, rows_query, rows_keyval, query_heavy, score_query = run(
        project_kernel,
        [
            ((count, width), BF16),
            ((count, wide), BF16),
            ((count, 2 * wide), BF16),
            ((slots, width), BF16),
            ((slots, width), BF16),
            ((slots, heavy_width), BF16),
            ((slots, 128), F32),
        ],
        [routes, tokens, gain, router, light_query, light_keyval, heavy_query],
        20,
        50,
    )
    span_rows = count + 2 * WINDOW
    attended, peaks, span_low, span = run(
        functools.partial(light_forward_kernel, length),
        [
            ((count, width), BF16),
            ((8, count), F32),
            ((span_rows, width), BF16),
            ((span_rows, 2 * wide), BF16),
        ],
        [document_bounds, query, keyval, low, above, below, gain, light_keyval],
        18,
        60,
        smem=1,
    )
    keyval_heavy, heavy_attended, heavy_scaled, heavy_peaks, own_values, score_keyval = run(
        functools.partial(heavy_forward_kernel, count),
        [
            ((seq * slots, 2 * heavy_width), BF16),
            ((slots, heavy_width), F32),
            ((slots, heavy_width), BF16),
            ((slots, 128), F32),
            ((slots, heavy_width), F32),
            ((slots, 128), F32),
        ],
        [document_bounds, routes, gathered, query_heavy, score_query, gain, router, heavy_keyval],
        16 if seq <= 8 else 48,
        40,
        smem=1,
    )
    residual, feed_low, rows_feed, score_feed, cotangent_rows, grad_raw = run(
        residual_kernel,
        [
            ((count, width), F32),
            ((count, width), BF16),
            ((slots, width), BF16),
            ((slots, 128), F32),
            ((slots, width), F32),
            ((slots, width), BF16),
        ],
        [
            routes, tokens, attended, light_output, heavy_scaled, heavy_output_weight, feed_gain,
            router, cotangent,
        ],
        20,
        30,
    )
    fast = seq == 8
    deps = []
    if fast:
        heavy_rows = send_rows(rows_query, heavy_scaled, rows_keyval)
        deps = [heavy_rows[1]]
    feed = heavy_feed(rows_feed, grad_raw, heavy_expand, heavy_reduce, seq, deps)
    raw_feed, grad_rows = feed[:2]
    rows = width // seq
    if fast:
        expand_kept, expand_sent, reduce_own, reduce_sent = feed[2:]
        reduce_got = shifted(reduce_sent, "seq", 2, 1, 1)
        expand_moves = send_expand(rows_feed, expand_kept, expand_sent, ())
    light_result, grad_low, *feed_grads = light_feed(
        feed_low, cotangent, light_expand, light_reduce, [expand_moves[0]] if fast else []
    )
    deps = []
    if fast:
        reduce_parts = send_reduce_z(reduce_own, grad_raw, reduce_got, [light_result])
        expand_moves = send_expand_y(*expand_moves, reduce_parts[:1])
        heavy_rows = send_rows_x(*heavy_rows, [expand_moves[0]])
        deps = [heavy_rows[0]]
    half = light_reduce.shape[0] // 2
    feed_kept, feed_sent = run(
        feed_products_kernel,
        [((2, seq, rows, half + width // 4 + 64), BF16)] * 2,
        [feed_low, cotangent] + feed_grads,
        18,
        0,
        [pltpu.VMEM((count, 1024), BF16)],
        deps=deps,
    )
    (
        output,
        grad_residual,
        grad_residual_low,
        grad_attended,
        grad_heavy_rows,
        grad_heavy_attended,
        logit_query,
        feed_small,
    ) = run(
        turn_kernel,
        [
            ((count, width), BF16),
            ((count, width), F32),
            ((count, width), BF16),
            ((count, width), BF16),
            ((slots, width), BF16),
            ((slots, heavy_width), BF16),
            ((slots, 128), F32),
            ((2, width), F32),
        ],
        [
            routes, residual, feed_gain, light_result, grad_low, raw_feed, grad_rows, score_feed,
            cotangent_rows, cotangent, router, light_output, heavy_output_weight, heavy_attended,
            score_query,
        ],
        26,
        LONG,
        deps=[feed_sent],
    )
    deps = []
    if fast:
        deps = [heavy_rows[1]]
    deps = []
    if fast:
        feed_left, feed_moved, feed_got = pair_x(feed_kept, feed_sent, [feed_small])
        deps = [feed_moved]
    grad_heavy_query, packet = run(
        functools.partial(heavy_query_kernel, count),
        [((slots, heavy_width), BF16), ((slots, 2 * heavy_width + 128), BF16)],
        [
            document_bounds, routes, gathered, query_heavy, keyval_heavy, heavy_peaks,
            grad_heavy_attended,
        ],
        10 if seq <= 8 else 48,
        LONG,
        smem=1,
        deps=deps,
    )
    sums = [pltpu.VMEM((span_rows, wide // 2), F32)] * 2
    light_ins = [document_bounds, query, span, peaks, grad_attended, attended]
    first_query, first_span = run(
        functools.partial(light_first_kernel, length),
        [((count, width // 2), BF16), ((span_rows, width), BF16)],
        light_ins,
        18,
        0,
        sums,
        smem=1,
        deps=[packet] + ([heavy_rows[1]] if fast else []),
    )
    second_query, second_span, grad_above, grad_below = run(
        functools.partial(light_second_kernel, length),
        [
            ((count, width // 2), BF16),
            ((span_rows, width), BF16),
            ((WINDOW, 2 * width), BF16),
            ((WINDOW, 2 * width), BF16),
        ],
        light_ins + [first_span],
        18,
        0,
        sums,
        smem=1,
    )
    from_above = neighbours(grad_above, -1)
    from_below = neighbours(grad_below, 1)
    mixer_kept, mixer_sent = run(
        light_products_kernel,
        [((2, width, width), BF16)] * 2,
        [
            span_low, first_query, second_query, first_span, second_span, attended,
            grad_residual_low,
        ],
        20,
        0,
    )
    shape = (2, seq, rows, width)
    mixer_kept, mixer_sent = mixer_kept.reshape(shape), mixer_sent.reshape(shape)
    deps = []
    if fast:
        moved_packets = [shifted(packet, "seq", 4, 2, 1 + i) for i in range(3)]
        (stacked,) = run(
            stack_kernel,
            [((4 * slots, packet.shape[1]), BF16)],
            [packet] + moved_packets,
            8,
            LONG,
            deps=[mixer_sent, expand_moves[1], feed_got] + reduce_parts[1:],
        )
        packets = (stacked, shifted(stacked, "seq", 2, 1, 1))
        expand_parts = send_expand_z(*expand_moves, [stacked])
        mixer_left, mixer_sent, mixer_got = pair_x(
            mixer_kept, mixer_sent, expand_parts[:1], LONG
        )
        reduce_moves = send_reduce_core(reduce_parts, width, [mixer_sent])
        deps = list(reduce_moves[:1])
    else:
        packets = gather_seq(packet)
        packets = (packets[: packets.shape[0] // 2], packets[packets.shape[0] // 2 :])
    grad_raw_keyval, logit_keyval = run(
        functools.partial(heavy_key_kernel, count),
        [((slots, 2 * heavy_width), BF16), ((slots, 128), F32)],
        [document_bounds, routes, *packets, keyval_heavy[:slots], own_values, score_keyval],
        16 if seq <= 8 else 56,
        0,
        [pltpu.VMEM((seq * slots, 2 * heavy_width + 128), BF16)],
        smem=1,
        deps=deps,
    )
    deps = []
    if fast:
        heavy_sent, heavy_kept = run(
            heavy_core_kernel,
            [((slots, 2 * width), BF16)] * 2,
            [grad_heavy_query, grad_heavy_rows, grad_raw_keyval],
            8,
        )
        feed_kept, feed_sent, feed_got = pair_y(
            feed_left,
            feed_got,
            [heavy_sent, mixer_got] + expand_parts[1:],
            LONG,
        )
        got = shifted(heavy_sent, "dp", 2, 1, 1)
        heavy_sent, heavy_left = run(
            heavy_x_kernel,
            [((2 * slots, width), BF16)] * 2,
            [heavy_kept, got],
            8,
            deps=[feed_sent],
        )
        heavy_got = shifted(heavy_sent, "dp", 2, 2, 1)
        deps = [heavy_sent]
    (grad_light,) = run(
        mixer_light_kernel,
        [((count, width), F32)],
        [
            first_query, second_query, first_span, second_span, from_below, from_above,
            light_query, light_keyval,
        ],
        16,
        5,
        [pltpu.VMEM((count, 2 * width), BF16)],
        deps=deps,
    )
    deps = []
    if fast:
        light_kept, light_sent, light_got = pair_y(mixer_left, mixer_got, [heavy_sent])
        feed_parts = pair_z(feed_kept, feed_got, [light_sent])
        deps = [heavy_got, feed_parts[0]]
    tokens_grad, small = run(
        mixer_kernel,
        [((count, width), BF16), ((8, width), F32)],
        [
            routes, tokens, gain, router, grad_residual, grad_light, grad_heavy_query,
            grad_raw_keyval, logit_query, logit_keyval, heavy_query, heavy_keyval, feed_small,
        ],
        20,
        LONG,
        deps=deps,
    )
    quarter = width // 4
    hidden = light_reduce.shape[0] // 2
    if fast:
        small = small + shifted(small, "dp", 2, 1, 1)
        light_parts = pair_z(light_kept, light_got, [small] + feed_parts[1:], LONG)
        small = small + shifted(small, "dp", 2, 2, 1)
        kept, sent = run(
            heavy_y_kernel,
            [((4, rows, width + 128), BF16)] * 2,
            [*heavy_rows, heavy_left, heavy_got, small],
            16,
            0,
            [pltpu.VMEM((width, width + 128), BF16)],
            deps=[light_parts[0]],
        )
        got = shifted(sent, "seq", 2, 1, 1)
        reduce_left, reduce_got = send_reduce_x(reduce_moves[0], reduce_moves[2], [heavy_sent])
        grad_heavy_reduce = reduce_left.astype(F32) + reduce_got.astype(F32)
        heavy_parts = pair_z(kept, got, light_parts[1:])
        grad_light_expand, grad_light_reduce = run(
            feed_end_kernel,
            [((rows, hidden), F32), ((light_reduce.shape[0] // seq, quarter), F32)],
            feed_parts,
            8,
        )
        grad_heavy_expand = total_parts(expand_parts)
        grad_light_query, grad_light_keyval, grad_light_output = run(
            light_end_kernel,
            [((rows, quarter), F32), ((rows, 2 * quarter), F32), ((rows, quarter), F32)],
            light_parts,
            8,
        )
        grad_heavy_query, grad_heavy_keyval, grad_heavy_output, small = run(
            heavy_end_kernel,
            [
                ((rows, quarter), F32),
                ((rows, 2 * quarter), F32),
                ((rows, quarter), F32),
                ((8, rows), F32),
            ],
            heavy_parts,
            8,
        )
        smalls = (small[0], small[1], small[2:5])
    else:
        small = sum_dp(small)
        gated_heavy, grad_gate, grad_up = feed[2:]
        grad_heavy_expand = expand_gradient(rows_feed, grad_gate, grad_up).astype(F32)
        grad_heavy_reduce = reduce_gradient(gated_heavy, grad_raw).astype(F32)
        formers = jnp.concatenate([rows_query, heavy_scaled, rows_keyval], 1)

        def mine(part):
            low_columns = slice(part * quarter, (part + 1) * quarter)
            high_columns = slice(2 * part * quarter, 2 * (part + 1) * quarter)
            return [
                grad_heavy_query[:, low_columns],
                grad_heavy_rows[:, low_columns],
                grad_raw_keyval[:, high_columns],
            ]

        first = jnp.concatenate(mine(0) + mine(1), 1)
        second = jnp.concatenate(mine(2) + mine(3), 1)
        formers, latters = gather_dp(formers, first, second)
        (heavy_products,) = run(
            products_kernel,
            [((width, width + 128), BF16)],
            [formers, latters, small],
            16,
            0.6,
        )
        heavy = reduce_seq(heavy_products).astype(F32)
        light = reduce_seq(reduce_pair(mixer_kept, mixer_sent)).astype(F32)
        packed = reduce_seq(reduce_pair(feed_kept, feed_sent)).astype(F32)
        grad_light_query = light[:, 2 * quarter : 3 * quarter]
        grad_light_keyval = light[:, : 2 * quarter]
        grad_light_output = light[:, 3 * quarter :]
        grad_light_expand = packed[:, :hidden]
        rest = packed[:, hidden + quarter :].reshape(3, rows // 3, 64)
        rest = rest.transpose(1, 0, 2).reshape(rows // 3, quarter)
        grad_light_reduce = jnp.concatenate([packed[:, hidden : hidden + quarter], rest], 0)
        grad_heavy_query = heavy[:, :quarter]
        grad_heavy_output = heavy[:, quarter : 2 * quarter]
        grad_heavy_keyval = heavy[:, 2 * quarter : 4 * quarter]
        smalls = (heavy[:, width], heavy[:, width + 1], heavy[:, width + 2 : width + 5].T)
    return (
        output,
        tokens_grad,
        *smalls,
        grad_light_query,
        grad_light_keyval,
        grad_light_output,
        grad_heavy_query,
        grad_heavy_keyval,
        grad_heavy_output,
        grad_light_expand,
        grad_light_reduce,
        grad_heavy_expand,
        grad_heavy_reduce,
    )


def solution(mesh):
    whole, rows = P(), P(("dp", "seq"), None)
    return jax.shard_map(
        on_device,
        mesh=mesh,
        in_specs=(rows, rows, whole, P(None, ("dp", "seq"))) + (whole,) * 13,
        out_specs=(rows, rows, P("seq"), P("seq"), P(None, "seq")) + (P("seq", "dp"),) * 10,
        check_vma=False,
    )
```

```python
import functools
import math

import jax
import jax.numpy as jnp
from jax import lax
from jax.experimental import pallas as pl
from jax.experimental.pallas import tpu as pltpu
from jax.sharding import PartitionSpec as P

LH = 8
HHS = 64
WINDOW = 128
EPSILON = 1e-06
MASKED = -1e30
HIGHEST = lax.Precision.HIGHEST
F32, BF16 = jnp.float32, jnp.bfloat16
HEAVY_SCALE = HHS ** (-0.5) / math.log(2.0)
MIB = 1 << 20
LONG = 60


def dot(former, latter):
    return jnp.dot(former, latter, preferred_element_type=F32)


def dot_left(former, latter):
    return lax.dot_general(former, latter, (((0,), (0,)), ((), ())), preferred_element_type=F32)


def dot_right(former, latter):
    return lax.dot_general(former, latter, (((1,), (1,)), ((), ())), preferred_element_type=F32)


def dot_exact(former, latter):
    return jnp.dot(former, latter, preferred_element_type=F32, precision=HIGHEST)


def column_of(row):
    count = row.shape[1]
    same = lax.broadcasted_iota(jnp.int32, (count, count), 0) == lax.broadcasted_iota(
        jnp.int32, (count, count), 1
    )
    return jnp.sum(jnp.where(same, row.astype(F32), 0.0), axis=1, keepdims=True)


def slots_by_tokens(route_row, tokens):
    column = column_of(route_row).astype(jnp.int32)
    lanes = lax.broadcasted_iota(jnp.int32, (route_row.shape[1], tokens), 1)
    return (column == lanes).astype(F32)


def tokens_by_slots(route_row, tokens):
    rows = lax.broadcasted_iota(jnp.int32, (tokens, route_row.shape[1]), 0)
    return (rows == route_row).astype(F32)


def normed(rows, gain):
    return rows * lax.rsqrt(jnp.mean(rows * rows, -1, keepdims=True) + EPSILON) * gain


def norm_back(rows, gain, grad):
    inverse = lax.rsqrt(jnp.mean(rows * rows, -1, keepdims=True) + EPSILON)
    plain = rows * inverse
    scaled = grad * gain
    inner = jnp.mean(scaled * plain, -1, keepdims=True)
    return inverse * (scaled - plain * inner), jnp.sum(grad * plain, 0, keepdims=True)


def sigmoid(value):
    return 1.0 / (1.0 + jnp.exp(-value))


def segment(place, first, last):
    return (place >= first).astype(F32) + (place >= last).astype(F32)


def gelu_parts(value):
    slope = math.sqrt(2.0 / math.pi)
    square = value * value
    bent = jnp.tanh(slope * value * (1.0 + 0.044715 * square))
    half = 0.5 * (1.0 + bent)
    rise = half + 0.5 * value * (1.0 - bent * bent) * slope * (1.0 + 3 * 0.044715 * square)
    return value * half, rise


def place(tok_rows, bounds):
    lead = lax.axis_index("seq") * tok_rows
    group = lax.axis_index("dp")
    return lead, bounds[group, 0], bounds[group, 1]


def select_kernel(bounds, routes, tokens, packet):
    count, width = tokens.shape
    lead, first, last = place(count, bounds)
    row = routes[1:2, :]
    chosen = slots_by_tokens(row, count).astype(BF16)
    packet[:, :width] = dot(chosen, tokens[...]).astype(BF16)
    column = column_of(row)
    tag = jnp.where(column >= 0, segment(column.astype(jnp.int32) + lead, first, last), -1.0)
    packet[:, width:] = jnp.broadcast_to(tag, (tag.shape[0], 128)).astype(BF16)


def project_kernel(
    routes, tokens, gain, router, light_query, light_keyval, heavy_query,
    low, query, keyval, rows_query, rows_keyval, query_heavy, score_query,
):
    count = tokens.shape[0]
    width = tokens.shape[1]
    low[...] = normed(tokens[...].astype(F32), gain[...]).astype(BF16)
    widen(query, slice(None), 0, dot(low[...], light_query[...]).astype(BF16), 0.0)
    pair = dot(low[...], light_keyval[...]).astype(BF16)
    widen(keyval, slice(None), 0, pair[:, :width], 0.0)
    widen(keyval, slice(None), LH * 128, pair[:, width:], 1.0)
    chosen = slots_by_tokens(routes[0:1, :], count).astype(BF16)
    raw = dot(chosen, tokens[...])
    rows = normed(raw, gain[...])
    logit = jnp.sum(rows * router[0:1, :], -1, keepdims=True)
    score_query[...] = jnp.broadcast_to(sigmoid(logit), score_query.shape)
    rows_query[...] = dot(chosen, low[...]).astype(BF16)
    query_heavy[...] = dot(rows_query[...], heavy_query[...]).astype(BF16)
    chosen = slots_by_tokens(routes[1:2, :], count).astype(BF16)
    rows_keyval[...] = dot(chosen, low[...]).astype(BF16)


def widen(ref, rows, start, value, filler):
    size = value.shape[1] // LH
    rest = jnp.full((value.shape[0], 128 - size), filler, BF16)
    for head in range(LH):
        base = start + head * 128
        ref[rows, base : base + size] = value[:, head * size : (head + 1) * size]
        ref[rows, base + size : base + 128] = rest


def light_mask(tok_rows, length, bounds, step):
    lead, first, last = place(tok_rows, bounds)
    shape = (3 * WINDOW, WINDOW)
    query_place = lead + step * WINDOW + lax.broadcasted_iota(jnp.int32, shape, 1)
    key_place = lead + (step - 1) * WINDOW + lax.broadcasted_iota(jnp.int32, shape, 0)
    allowed = (key_place >= 0) & (key_place < length)
    allowed = allowed & (jnp.abs(query_place - key_place) <= WINDOW)
    return allowed & (segment(query_place, first, last) == segment(key_place, first, last))


def light_forward_kernel(
    length, bounds, query, keyval, low, above, below, gain, light_keyval,
    attended, peaks, span_low, span,
):
    tok_rows, width = low.shape
    size = width // LH
    values_start = LH * 128
    scale = size ** (-0.5) / math.log(2.0)
    own = slice(WINDOW, WINDOW + tok_rows)
    span_low[own] = low[...]
    span[own] = keyval[...]
    for rows, signal in ((slice(0, WINDOW), above), (slice(WINDOW + tok_rows, None), below)):
        span_low[rows] = normed(signal[...].astype(F32), gain[...]).astype(BF16)
        pair = dot(span_low[rows], light_keyval[...]).astype(BF16)
        widen(span, rows, 0, pair[:, :width], 0.0)
        widen(span, rows, values_start, pair[:, width:], 1.0)
    for step in range(tok_rows // WINDOW):
        rows = slice(step * WINDOW, (step + 1) * WINDOW)
        keys = slice(step * WINDOW, (step + 3) * WINDOW)
        allowed = light_mask(tok_rows, length, bounds, step)
        for head in range(LH):
            wide = slice(head * 128, (head + 1) * 128)
            values = slice(values_start + head * 128, values_start + (head + 1) * 128)
            scores = jnp.where(allowed, dot_right(span[keys, wide], query[rows, wide]), MASKED)
            peak = jnp.max(scores, 0, keepdims=True)
            exponent = jnp.exp2((scores - peak) * scale)
            total = jnp.sum(exponent, 0, keepdims=True)
            result = dot_left(exponent.astype(BF16), span[keys, values])
            result = result[:, :size] * (1.0 / result[:, size : size + 1])
            attended[rows, head * size : (head + 1) * size] = result.astype(BF16)
            peaks[head : head + 1, rows] = peak * scale + jnp.log2(total)


def light_half(
    half, length, bounds, query, span, peaks, grad, attended, grad_query, grad_keys, grad_values,
):
    tok_rows, width = grad.shape
    size = width // LH
    heads = LH // 2
    scale = size ** (-0.5) / math.log(2.0)
    lanes = slice(half * heads * size, (half + 1) * heads * size)
    product = grad[:, lanes].astype(F32) * attended[:, lanes].astype(F32)
    high = product.astype(BF16)
    rest = (product - high.astype(F32)).astype(BF16)
    shape = (8, heads * size)
    column = lax.broadcasted_iota(jnp.int32, shape, 1)
    row = lax.broadcasted_iota(jnp.int32, shape, 0)
    pickers = ((column >= row * size) & (column < (row + 1) * size)).astype(BF16)
    inners = dot_right(pickers, high) + dot_right(pickers, rest)
    grad_keys[...] = jnp.zeros_like(grad_keys)
    grad_values[...] = jnp.zeros_like(grad_values)
    for step in range(tok_rows // WINDOW):
        rows = slice(step * WINDOW, (step + 1) * WINDOW)
        keys = slice(step * WINDOW, (step + 3) * WINDOW)
        allowed = light_mask(tok_rows, length, bounds, step)
        for index in range(heads):
            head = half * heads + index
            wide = slice(head * 128, (head + 1) * 128)
            start = LH * 128 + head * 128
            here = slice(index * 128, (index + 1) * 128)
            columns = slice(head * size, (head + 1) * size)
            scores = dot_right(span[keys, wide], query[rows, wide]) * scale
            weights = jnp.exp2(
                jnp.where(allowed, scores, MASKED) - peaks[head : head + 1, rows]
            )
            given = grad[rows, columns]
            grad_weights = dot_right(span[keys, start : start + size], given)
            inner = inners[index : index + 1, rows]
            grad_scores = (weights * (grad_weights - inner)).astype(BF16)
            result = dot_left(grad_scores, span[keys, wide])[:, :size] * size ** (-0.5)
            grad_query[rows, index * size : (index + 1) * size] = result.astype(BF16)
            grad_keys[keys, here] += dot(grad_scores, query[rows, wide])
            grad_values[keys, index * 128 : index * 128 + size] += dot(weights.astype(BF16), given)


def narrow(grad_span, grad_keys, grad_values):
    half = grad_span.shape[1] // 2
    size = 2 * half // LH
    for head in range(LH // 2):
        here = slice(head * 128, head * 128 + size)
        columns = slice(head * size, (head + 1) * size)
        grad_span[:, columns] = (grad_keys[:, here] * size ** (-0.5)).astype(BF16)
        columns = slice(half + head * size, half + (head + 1) * size)
        grad_span[:, columns] = grad_values[:, here].astype(BF16)


def light_first_kernel(
    length, bounds, query, span, peaks, grad, attended, grad_query, grad_span, grad_keys, grad_values
):
    light_half(
        0, length, bounds, query, span, peaks, grad, attended, grad_query, grad_keys, grad_values
    )
    narrow(grad_span, grad_keys, grad_values)


def light_second_kernel(
    length, bounds, query, span, peaks, grad, attended, first_span,
    grad_query, grad_span, grad_above, grad_below, grad_keys, grad_values,
):
    light_half(
        1, length, bounds, query, span, peaks, grad, attended, grad_query, grad_keys, grad_values
    )
    narrow(grad_span, grad_keys, grad_values)
    half = grad_span.shape[1] // 2
    count = grad_span.shape[0]
    for ref, rows in ((grad_above, slice(0, WINDOW)), (grad_below, slice(count - WINDOW, count))):
        ref[:, :half] = first_span[rows, :half]
        ref[:, half : 2 * half] = grad_span[rows, :half]
        ref[:, 2 * half : 3 * half] = first_span[rows, half:]
        ref[:, 3 * half :] = grad_span[rows, half:]


def light_products_kernel(
    span_low, first_query, second_query, first_span, second_span, attended, grad_residual, kept, sent
):
    tok_rows, width = attended.shape
    quarter = width // 4
    half = width // 2
    core = lax.axis_index("dp") % 2
    own = slice(WINDOW, WINDOW + tok_rows)
    for part in range(4):
        grad_span = (first_span, second_span)[part % 2]
        columns = slice((part // 2) * half, (part // 2 + 1) * half)
        keyval_part = dot_left(span_low[...], grad_span[:, columns]).astype(BF16)
        grad_query = (first_query, second_query)[part // 2]
        columns = slice((part % 2) * quarter, (part % 2 + 1) * quarter)
        query_part = dot_left(span_low[own], grad_query[:, columns]).astype(BF16)
        columns = slice(part * quarter, (part + 1) * quarter)
        output_part = dot_left(attended[...], grad_residual[:, columns]).astype(BF16)
        for ref, chosen in ((kept, core == part % 2), (sent, core != part % 2)):

            @pl.when(chosen)
            def _(ref=ref, x=part // 2, parts=(keyval_part, query_part, output_part)):
                ref[x, :, : 2 * quarter] = parts[0]
                ref[x, :, 2 * quarter : 3 * quarter] = parts[1]
                ref[x, :, 3 * quarter :] = parts[2]


def heavy_forward_kernel(
    count, bounds, routes, gathered, query_heavy, score_query, gain, router, heavy_keyval,
    keyval, attended, scaled, peaks, own_values, score_keyval,
):
    width = query_heavy.shape[1]
    slots = query_heavy.shape[0]
    total_rows = gathered.shape[0]
    part = min(512, total_rows)
    for start in range(0, total_rows, part):
        rows = slice(start, start + part)
        signal = normed(gathered[rows, :width].astype(F32), gain[...])
        logit = jnp.sum(signal * router[1:2, :], -1, keepdims=True)
        score = sigmoid(logit)
        raw = dot(signal.astype(BF16), heavy_keyval[...])
        keyval[rows, :width] = raw[:, :width].astype(BF16)
        keyval[rows, width:] = (score * raw[:, width:]).astype(BF16)
        if start == 0:
            own_values[...] = raw[:slots, width:]
            score_keyval[...] = jnp.broadcast_to(score[:slots], score_keyval.shape)
    allowed = heavy_mask(count, bounds, routes, gathered, width)
    lanes = lax.broadcasted_iota(jnp.int32, (slots, 128), 1)
    kept = jnp.zeros((slots, 128), F32)
    for head in range(width // HHS):
        columns = slice(head * HHS, (head + 1) * HHS)
        values = slice(width + head * HHS, width + (head + 1) * HHS)
        scores = dot_right(query_heavy[:, columns], keyval[:, columns])
        scores = jnp.where(allowed, scores, MASKED)
        peak = jnp.max(scores, -1, keepdims=True)
        exponent = jnp.where(allowed, jnp.exp2((scores - peak) * HEAVY_SCALE), 0.0)
        total = jnp.sum(exponent, -1, keepdims=True)
        total = jnp.where(total > 0, total, 1.0)
        weights = (exponent * (1.0 / total)).astype(BF16)
        result = dot(weights, keyval[:, values])
        attended[:, columns] = result
        scaled[:, columns] = (score_query[:, :1] * result).astype(BF16)
        kept = jnp.where(lanes == head, peak * HEAVY_SCALE + jnp.log2(total), kept)
    peaks[...] = kept


def heavy_mask(count, bounds, routes, gathered, width):
    lead, first, last = place(count, bounds)
    pickers = (lax.broadcasted_iota(jnp.int32, (8, 128), 1) == 0).astype(BF16)
    key_segment = dot_right(pickers, gathered[:, width:])[:1]
    return own_segment(routes, lead, first, last) == key_segment


def own_segment(routes, lead, first, last):
    column = column_of(routes[0:1, :])
    spot = jnp.where(column >= 0, column.astype(jnp.int32) + lead, -1)
    return segment(spot, first, last)


def residual_kernel(
    routes, tokens, attended, light_output, scaled, heavy_output, gain, router, cotangent,
    residual, low, rows_feed, score_feed, cotangent_rows, grad_raw,
):
    count = tokens.shape[0]
    spread = tokens_by_slots(routes[0:1, :], count).astype(BF16)
    scattered = dot(spread, scaled[...]).astype(BF16)
    residual[...] = (
        tokens[...].astype(F32)
        + dot(attended[...], light_output[...])
        + dot(scattered, heavy_output[...])
    )
    signal = normed(residual[...], gain[...])
    low[...] = signal.astype(BF16)
    logit = jnp.sum(signal * router[2:3, :], -1, keepdims=True)
    chosen = slots_by_tokens(routes[2:3, :], count)
    logit = dot_exact(chosen, jnp.broadcast_to(logit, (count, 128)))
    score = sigmoid(logit)
    score_feed[...] = score
    chosen = chosen.astype(BF16)
    rows_feed[...] = dot(chosen, low[...]).astype(BF16)
    rows = dot(chosen, cotangent[...])
    cotangent_rows[...] = rows
    grad_raw[...] = (score[:, :1] * rows).astype(BF16)


def feed_step(rows_feed, grad_raw, gate_weight, up_weight, reduce_weight, raw, grad_rows):
    @pl.when(pl.program_id(0) == 0)
    def _():
        raw[...] = jnp.zeros_like(raw)
        grad_rows[...] = jnp.zeros_like(grad_rows)

    gate = dot(rows_feed[...], gate_weight[...])
    up = dot(rows_feed[...], up_weight[...])
    bent, rise = gelu_parts(gate)
    gated_low = (bent * up).astype(BF16)
    raw[...] += dot(gated_low, reduce_weight[...])
    grad_gated = dot_right(grad_raw[...], reduce_weight[...])
    gate_low = (grad_gated * up * rise).astype(BF16)
    up_low = (grad_gated * bent).astype(BF16)
    grad_rows[...] += dot_right(gate_weight[...], gate_low) + dot_right(up_weight[...], up_low)
    return gated_low, gate_low, up_low


def heavy_feed_kernel(
    rows_feed, grad_raw, gate_weight, up_weight, reduce_weight,
    raw, grad_rows, gated, grad_gate, grad_up,
):
    gated_low, gate_low, up_low = feed_step(
        rows_feed, grad_raw, gate_weight, up_weight, reduce_weight, raw, grad_rows
    )
    gated[...] = gated_low
    grad_gate[...] = gate_low
    grad_up[...] = up_low


def heavy_feed_split_kernel(
    rows_feed, grad_raw, gate_weight, up_weight, reduce_weight,
    raw, grad_rows, kept, sent, own, moved,
):
    gated_low, gate_low, up_low = feed_step(
        rows_feed, grad_raw, gate_weight, up_weight, reduce_weight, raw, grad_rows
    )
    step = pl.program_id(0)
    width, part = rows_feed.shape[1], gated_low.shape[1]
    half = kept.shape[1] // 2
    start = pl.multiple_of((step % 2) * part, part)
    mine = step // 2 == lax.axis_index("dp") % 2

    @pl.when(mine)
    def _():
        kept[:, pl.ds(start, part)] = gate_low
        kept[:, pl.ds(half + start, part)] = up_low

    @pl.when(jnp.logical_not(mine))
    def _():
        sent[:, pl.ds(width + start, part)] = gate_low
        sent[:, pl.ds(width + half + start, part)] = up_low

    y = lax.axis_index("seq") % 2
    spot = pl.multiple_of(step * (part // 2), part // 2)
    even, odd = gated_low[:, : part // 2], gated_low[:, part // 2 :]
    own[:, pl.ds(spot, part // 2)] = jnp.where(y == 0, even, odd)
    moved[:, pl.ds(spot, part // 2)] = jnp.where(y == 0, odd, even)

    @pl.when(step == 0)
    def _():
        sent[:, :width] = rows_feed[...]
        moved[:, 2 * part :] = grad_raw[...]


def light_feed_kernel(
    low, cotangent, gate_weight, up_weight, reduce_weight, result, grad_low, gated, grad_gate, grad_up
):
    @pl.when(pl.program_id(0) == 0)
    def _():
        result[...] = jnp.zeros_like(result)
        grad_low[...] = jnp.zeros_like(grad_low)

    gate = dot(low[...], gate_weight[...])
    up = dot(low[...], up_weight[...])
    bent, rise = gelu_parts(gate)
    gated_low = (bent * up).astype(BF16)
    gated[...] = gated_low
    result[...] += dot(gated_low, reduce_weight[...])
    grad_gated = dot_right(cotangent[...], reduce_weight[...])
    gate_low = (grad_gated * up * rise).astype(BF16)
    up_low = (grad_gated * bent).astype(BF16)
    grad_gate[...] = gate_low
    grad_up[...] = up_low
    grad_low[...] += dot_right(gate_low, gate_weight[...]) + dot_right(up_low, up_weight[...])


def feed_products_kernel(low, cotangent, gated, grad_gate, grad_up, kept, sent, turned):
    width = cotangent.shape[1]
    quarter = width // 4
    hidden = gated.shape[1] // 2
    seq, rows = kept.shape[1:3]
    more = rows // 3
    core = lax.axis_index("dp") % 2
    for part in range(4):
        turned[:, part * 256 : part * 256 + quarter] = cotangent[
            :, part * quarter : (part + 1) * quarter
        ]
        turned[:, part * 256 + quarter : (part + 1) * 256] = jnp.zeros(
            (cotangent.shape[0], 256 - quarter), BF16
        )
    for part in range(4):
        grad = (grad_gate, grad_up)[part // 2]
        columns = slice((part % 2) * hidden, (part % 2 + 1) * hidden)
        product = dot_left(low[...], grad[:, columns]).astype(BF16)
        for ref, chosen in ((kept, core == part % 2), (sent, core != part % 2)):

            @pl.when(chosen)
            def _(ref=ref, x=part // 2, product=product):
                for i in range(seq):
                    ref[x, i, :, :hidden] = product[i * rows : (i + 1) * rows]

    for half in range(2):
        columns = slice(half * hidden, (half + 1) * hidden)
        every = dot_left(gated[:, columns], turned[...]).astype(BF16)
        for part in range(4):
            product = every[:, part * 256 : part * 256 + quarter]
            for ref, chosen in ((kept, core == part % 2), (sent, core != part % 2)):

                @pl.when(chosen)
                def _(ref=ref, x=part // 2, product=product, half=half):
                    for i in range(seq // 2):
                        spot = half * (seq // 2) + i
                        start = i * (rows + more)
                        ref[x, spot, :, hidden : hidden + quarter] = product[start : start + rows]
                        rest = product[start + rows : start + rows + more]
                        for piece in range(3):
                            ref[
                                x, spot, piece * more : (piece + 1) * more, hidden + quarter :
                            ] = rest[:, piece * 64 : (piece + 1) * 64]


def turn_kernel(
    routes, residual, gain, result, grad_low, raw, grad_rows, score_feed, cotangent_rows, cotangent,
    router, light_output, heavy_output, heavy_attended, score_query,
    output, grad_residual, grad_residual_low, grad_attended, grad_heavy_rows, grad_heavy_attended,
    logit_query, small,
):
    count = residual.shape[0]
    spread = tokens_by_slots(routes[2:3, :], count)
    score = score_feed[:, :1]
    output[...] = (
        residual[...] + result[...] + dot_exact(spread, score * raw[...])
    ).astype(BF16)
    logit = score * (1.0 - score) * jnp.sum(cotangent_rows[...] * raw[...], -1, keepdims=True)
    grad = grad_low[...] + dot_exact(spread, grad_rows[...].T + logit * router[2:3, :])
    back, gain_grad = norm_back(residual[...], gain[...], grad)
    token_logit = dot_exact(spread, jnp.broadcast_to(logit, (logit.shape[0], 128)))[:, :1]
    signal = normed(residual[...], gain[...])
    small[0:1] = gain_grad
    small[1:2] = jnp.sum(token_logit * signal, 0, keepdims=True)
    total = cotangent[...].astype(F32) + back
    grad_residual[...] = total
    grad_residual_low[...] = total.astype(BF16)
    grad_attended[...] = dot_right(grad_residual_low[...], light_output[...]).astype(BF16)
    chosen = slots_by_tokens(routes[0:1, :], count).astype(BF16)
    grad_heavy_rows[...] = dot(chosen, grad_residual_low[...]).astype(BF16)
    scaled = dot_right(grad_heavy_rows[...], heavy_output[...])
    score = score_query[:, :1]
    logit = score * (1.0 - score) * jnp.sum(scaled * heavy_attended[...], -1, keepdims=True)
    logit_query[...] = jnp.broadcast_to(logit, logit_query.shape)
    grad_heavy_attended[...] = (score * scaled).astype(BF16)


def heavy_query_kernel(
    count, bounds, routes, gathered, query_heavy, keyval, peaks, grad, grad_query, packet
):
    slots, width = query_heavy.shape
    heads = width // HHS
    allowed = heavy_mask(count, bounds, routes, gathered, width)
    lanes = lax.broadcasted_iota(jnp.int32, (slots, 128), 1)
    kept = peaks[...]
    lead, first, last = place(count, bounds)
    tag = jnp.where(lanes == 4 * heads, own_segment(routes, lead, first, last), 0.0)
    for head in range(heads):
        columns = slice(head * HHS, (head + 1) * HHS)
        values = slice(width + head * HHS, width + (head + 1) * HHS)
        scores = dot_right(query_heavy[:, columns], keyval[:, columns]) * HEAVY_SCALE
        peak = jnp.sum(jnp.where(lanes == head, kept, 0.0), -1, keepdims=True)
        weights = jnp.where(allowed, jnp.exp2(scores - peak), 0.0)
        grad_weights = dot_right(grad[:, columns], keyval[:, values])
        inner = jnp.sum(weights * grad_weights, -1, keepdims=True)
        grad_scores = (weights * (grad_weights - inner)).astype(BF16)
        grad_query[:, columns] = (dot(grad_scores, keyval[:, columns]) * HHS ** (-0.5)).astype(BF16)
        for lane, value in ((head, peak), (heads + head, inner)):
            high = value.astype(BF16).astype(F32)
            tag = jnp.where(lanes == lane, high, tag)
            tag = jnp.where(lanes == 2 * heads + lane, value - high, tag)
    packet[:, :width] = query_heavy[...]
    packet[:, width : 2 * width] = grad[...]
    packet[:, 2 * width :] = tag.astype(BF16)


def heavy_key_kernel(
    count, bounds, routes, first, second, keyval, own_values, score_keyval, grad_raw, logit_keyval, packets
):
    half = first.shape[0]
    packets[:half] = first[...]
    packets[half:] = second[...]
    slots = own_values.shape[0]
    width = own_values.shape[1]
    heads = width // HHS
    lead, first, last = place(count, bounds)
    column = column_of(routes[1:2, :])
    key_segment = jnp.where(
        column >= 0, segment(column.astype(jnp.int32) + lead, first, last), -1.0
    )
    same = lax.broadcasted_iota(jnp.int32, (128, 128), 0) == lax.broadcasted_iota(
        jnp.int32, (128, 128), 1
    )
    tags = dot_right(same.astype(BF16), packets[:, 2 * width :])
    allowed = key_segment == tags[4 * heads : 4 * heads + 1]
    score = score_keyval[:, :1]
    logit = jnp.zeros((slots, 1), F32)
    for head in range(heads):
        columns = slice(head * HHS, (head + 1) * HHS)
        values = slice(width + head * HHS, width + (head + 1) * HHS)
        peak = tags[head : head + 1] + tags[2 * heads + head : 2 * heads + head + 1]
        inner = tags[heads + head : heads + head + 1] + tags[3 * heads + head : 3 * heads + head + 1]
        scores = dot_right(keyval[:slots, columns], packets[:, columns]) * HEAVY_SCALE
        weights = jnp.where(allowed, jnp.exp2(scores - peak), 0.0)
        grad_weights = dot_right(keyval[:slots, values], packets[:, values])
        grad_scores = (weights * (grad_weights - inner)).astype(BF16)
        key_grad = dot(grad_scores, packets[:, columns]) * HHS ** (-0.5)
        value_grad = dot(weights.astype(BF16), packets[:, values]).astype(BF16).astype(F32)
        logit += jnp.sum(value_grad * own_values[:, columns], -1, keepdims=True)
        grad_raw[:, columns] = key_grad.astype(BF16)
        grad_raw[:, values] = (score * value_grad).astype(BF16)
    logit_keyval[...] = jnp.broadcast_to(score * (1.0 - score) * logit, logit_keyval.shape)


def mixer_light_kernel(
    first_query, second_query, first_span, second_span, from_below, from_above, light_query,
    light_keyval, grad, total_keyval,
):
    count, half = first_query.shape
    own = slice(WINDOW, WINDOW + count)
    for i, (ref, base) in enumerate(
        ((first_span, 0), (second_span, 0), (first_span, half), (second_span, half))
    ):
        total_keyval[:, i * half : (i + 1) * half] = ref[own, base : base + half]
    for rows, more in (
        (slice(0, WINDOW), from_below),
        (slice(count - WINDOW, count), from_above),
    ):
        total_keyval[rows] = (total_keyval[rows].astype(F32) + more[...].astype(F32)).astype(BF16)
    grad[...] = (
        dot_right(first_query[...], light_query[:, :half])
        + dot_right(second_query[...], light_query[:, half:])
        + dot_right(total_keyval[...], light_keyval[...])
    )


def mixer_kernel(
    routes, tokens, gain, router, grad_residual, grad_light, grad_heavy_query, grad_raw_keyval,
    logit_query, logit_keyval, heavy_query, heavy_keyval, feed_small, tokens_grad, small,
):
    count = tokens.shape[0]
    spread_query = tokens_by_slots(routes[0:1, :], count)
    spread_keyval = tokens_by_slots(routes[1:2, :], count)
    query_rows = dot_right(grad_heavy_query[...], heavy_query[...])
    query_rows += logit_query[:, :1] * router[0:1, :]
    keyval_rows = dot_right(grad_raw_keyval[...], heavy_keyval[...])
    keyval_rows += logit_keyval[:, :1] * router[1:2, :]
    grad = (
        grad_light[...]
        + dot_exact(spread_query, query_rows)
        + dot_exact(spread_keyval, keyval_rows)
    )
    signal = tokens[...].astype(F32)
    back, gain_grad = norm_back(signal, gain[...], grad)
    tokens_grad[...] = (grad_residual[...] + back).astype(BF16)
    signal = normed(signal, gain[...])
    small[0:1] = gain_grad
    small[1:2] = feed_small[0:1]
    small[2:3] = jnp.sum(dot_exact(spread_query, logit_query[...])[:, :1] * signal, 0, keepdims=True)
    small[3:4] = jnp.sum(dot_exact(spread_keyval, logit_keyval[...])[:, :1] * signal, 0, keepdims=True)
    small[4:5] = feed_small[1:2]
    small[5:8] = jnp.zeros((3, small.shape[1]), F32)


def estimate(weight, size):
    return pl.CostEstimate(
        flops=int(weight * 1e9), bytes_accessed=20 * size, transcendentals=0
    )


def without(body, start, count):
    def inner(*refs):
        return body(*refs[:start], *refs[start + count :])

    return inner


def run(body, outs, ins, limit, weight=0, scratch=(), smem=0, deps=()):
    vmem = pl.BlockSpec(memory_space=pltpu.VMEM)
    size = sum(v.size * v.dtype.itemsize for v in ins) + sum(
        math.prod(shape) * jnp.dtype(kind).itemsize for shape, kind in outs
    )
    return pl.pallas_call(
        without(body, len(ins), len(deps)),
        out_shape=[jax.ShapeDtypeStruct(shape, kind) for shape, kind in outs],
        in_specs=[pl.BlockSpec(memory_space=pltpu.SMEM)] * smem
        + [vmem] * (len(ins) - smem)
        + [pl.BlockSpec(memory_space=pl.ANY)] * len(deps),
        out_specs=[vmem] * len(outs),
        scratch_shapes=list(scratch),
        compiler_params=pltpu.CompilerParams(vmem_limit_bytes=int(limit * MIB)),
        cost_estimate=estimate(weight, size),
    )(*ins, *deps)


def heavy_feed(rows_feed, grad_raw, heavy_expand, heavy_reduce, seq, deps):
    slots, width = rows_feed.shape
    hidden = heavy_reduce.shape[0]
    steps = 4
    part = hidden // steps
    fixed = pl.BlockSpec((slots, width), lambda j: (0, 0))
    moving = pl.BlockSpec((slots, part), lambda j: (0, j))
    split = seq == 8
    if split:
        columns = [hidden, width + hidden, 2 * part, 2 * part + width]
        specs = [pl.BlockSpec((slots, c), lambda j: (0, 0)) for c in columns]
    else:
        columns, specs = [hidden] * 3, [moving] * 3
    return pl.pallas_call(
        without(heavy_feed_split_kernel if split else heavy_feed_kernel, 5, len(deps)),
        grid=(steps,),
        out_shape=[
            jax.ShapeDtypeStruct((slots, width), F32),
            jax.ShapeDtypeStruct((width, slots), F32),
        ]
        + [jax.ShapeDtypeStruct((slots, c), BF16) for c in columns],
        in_specs=[
            fixed,
            fixed,
            pl.BlockSpec((width, part), lambda j: (0, j)),
            pl.BlockSpec((width, part), lambda j: (0, steps + j)),
            pl.BlockSpec((part, width), lambda j: (j, 0)),
        ]
        + [pl.BlockSpec(memory_space=pl.ANY)] * len(deps),
        out_specs=[fixed, pl.BlockSpec((width, slots), lambda j: (0, 0))] + specs,
        compiler_params=pltpu.CompilerParams(vmem_limit_bytes=32 * MIB),
        cost_estimate=estimate(75, 20 << 20),
    )(rows_feed, grad_raw, heavy_expand, heavy_expand, heavy_reduce, *deps)


def light_feed(low, cotangent, light_expand, light_reduce, deps):
    count, width = low.shape
    hidden = light_reduce.shape[0]
    part = hidden // 2
    fixed = pl.BlockSpec((count, width), lambda j: (0, 0))
    moving = pl.BlockSpec((count, part), lambda j: (0, j))
    return pl.pallas_call(
        without(light_feed_kernel, 5, len(deps)),
        grid=(2,),
        out_shape=[jax.ShapeDtypeStruct((count, width), F32)] * 2
        + [jax.ShapeDtypeStruct((count, hidden), BF16)] * 3,
        in_specs=[
            fixed,
            fixed,
            pl.BlockSpec((width, part), lambda j: (0, j)),
            pl.BlockSpec((width, part), lambda j: (0, 2 + j)),
            pl.BlockSpec((part, width), lambda j: (j, 0)),
        ]
        + [pl.BlockSpec(memory_space=pl.ANY)] * len(deps),
        out_specs=[fixed] * 2 + [moving] * 3,
        compiler_params=pltpu.CompilerParams(vmem_limit_bytes=32 * MIB),
        cost_estimate=estimate(LONG, 8 << 20),
    )(low, cotangent, light_expand, light_expand, light_reduce, *deps)


def products_kernel(formers, latters, small, products):
    width = formers.shape[1] // 3
    quarter = width // 4
    offsets = ((0, 0, quarter), (1, quarter, quarter), (2, 2 * quarter, 2 * quarter))
    for part, start, columns in offsets:
        products[:, start : start + columns] = dot_left(
            formers[:, part * width : (part + 1) * width], latters[:, start : start + columns]
        ).astype(BF16)
    products[:, width:] = turn_small(small[...])


def outer_kernel(former, latter, product):
    product[...] = dot_left(former[...], latter[...]).astype(BF16)


def fold_kernel(kept, got, left, sent):
    total = (kept[...].astype(F32) + got[...].astype(F32)).astype(BF16)
    half = total.shape[1] // 2
    x = lax.axis_index("dp") // 2
    left[...] = jnp.where(x == 0, total[:, :half], total[:, half:])
    sent[...] = jnp.where(x == 0, total[:, half:], total[:, :half])


def expand_x_kernel(former, kept, got, sent, left):
    slots, width = former.shape
    half = kept.shape[1] // 2
    x = lax.axis_index("dp") // 2
    sent[:slots, :width] = former[...]
    sent[slots:, :width] = got[:, :width]
    for rows, source, base in ((slice(0, slots), kept, 0), (slice(slots, None), got, width)):
        gate, up = source[:, base : base + half], source[:, base + half : base + 2 * half]
        left[rows] = jnp.where(x == 0, gate, up)
        sent[rows, width:] = jnp.where(x == 0, up, gate)


def expand_y_kernel(sent_x, left, got, sent, former):
    rows, wide = left.shape
    part = former.shape[1] // 4
    y = lax.axis_index("seq") % 2
    for start, source in ((0, sent_x), (rows, got)):
        here = slice(start, start + rows)
        for i in range(4):
            even = source[:, 2 * i * part : (2 * i + 1) * part]
            odd = source[:, (2 * i + 1) * part : (2 * i + 2) * part]
            columns = slice(i * part, (i + 1) * part)
            former[here, columns] = jnp.where(y == 0, even, odd)
            sent[here, columns] = jnp.where(y == 0, odd, even)
    sent[:rows, 4 * part :] = left[...]
    sent[rows:, 4 * part :] = got[:, 8 * part :]


def reduce_z_kernel(own, grad_raw, got, kept, first, second, third):
    slots, wide = own.shape
    part = wide // 4
    z = lax.axis_index("seq") // 2
    for step, ref in enumerate((kept, first, second, third)):
        spot = pl.multiple_of(((z + step) % 4) * part, part)
        ref[:slots, :part] = own[:, pl.ds(spot, part)]
        ref[slots:, :part] = got[:, pl.ds(spot, part)]
        ref[:slots, part:] = grad_raw[...]
        ref[slots:, part:] = got[:, wide:]


def expand_product_kernel(sent, got, former, own, first, second, third, slices):
    base = former.shape[1]
    product = dot_left(former[...], sent[:, base:])
    product += dot_left(got[:, :base], got[:, base:])
    part = own.shape[0]
    for i in range(4):
        slices[i] = product[i * part : (i + 1) * part].astype(BF16)
    z = lax.axis_index("seq") // 2
    for step, ref in enumerate((own, first, second, third)):
        ref[...] = slices[(z + step) % 4]


def reduce_product_kernel(own, first, second, third, kept, moved, turned):
    half = kept.shape[0]
    quarter = (own.shape[1] - half) // 4
    product = None
    for source in (own, first, second, third):
        for spot, i in enumerate((0, 2, 1, 3)):
            start = half + i * quarter
            turned[:, spot * quarter : (spot + 1) * quarter] = source[:, start : start + quarter]
        term = dot_left(source[:, :half], turned[...])
        product = term if product is None else product + term
    core = lax.axis_index("dp") % 2
    low, high = product[:, : 2 * quarter], product[:, 2 * quarter :]
    kept[...] = jnp.where(core == 0, low, high).astype(BF16)
    moved[...] = jnp.where(core == 0, high, low).astype(BF16)


def stack_kernel(own, first, second, third, stacked):
    rows = own.shape[0]
    for i, ref in enumerate((own, first, second, third)):
        stacked[i * rows : (i + 1) * rows] = ref[...]


def rows_kernel(rows_query, scaled, rows_keyval, joined):
    width = rows_query.shape[1]
    for i, ref in enumerate((rows_query, scaled, rows_keyval)):
        joined[:, i * width : (i + 1) * width] = ref[...]


def stack_two_kernel(first, second, stacked):
    rows = first.shape[0]
    stacked[:rows] = first[...]
    stacked[rows:] = second[...]


def heavy_core_kernel(grad_query, grad_rows, grad_keyval, sent, kept):
    width = grad_query.shape[1]
    quarter = width // 4
    core = lax.axis_index("dp") % 2
    for x in range(2):
        spot = x * width
        for source, columns in ((grad_query, quarter), (grad_rows, quarter), (grad_keyval, 2 * quarter)):
            even = source[:, 2 * x * columns : (2 * x + 1) * columns]
            odd = source[:, (2 * x + 1) * columns : (2 * x + 2) * columns]
            kept[:, spot : spot + columns] = jnp.where(core == 0, even, odd)
            sent[:, spot : spot + columns] = jnp.where(core == 0, odd, even)
            spot += columns


def heavy_x_kernel(kept, got, sent, left):
    slots = kept.shape[0]
    width = kept.shape[1] // 2
    x = lax.axis_index("dp") // 2
    for rows, source in ((slice(0, slots), kept), (slice(slots, None), got)):
        low, high = source[:, :width], source[:, width:]
        left[rows] = jnp.where(x == 0, low, high)
        sent[rows] = jnp.where(x == 0, high, low)


def pair_x_kernel(kept, got, left, sent):
    x = lax.axis_index("dp") // 2
    left[...] = (kept[x].astype(F32) + got[x].astype(F32)).astype(BF16)
    sent[...] = (kept[1 - x].astype(F32) + got[1 - x].astype(F32)).astype(BF16)


def pair_y_kernel(left, got, kept, sent):
    y = lax.axis_index("seq") % 2
    for i in range(4):
        mine, other = 2 * i + y, 2 * i + 1 - y
        kept[i] = (left[mine].astype(F32) + got[mine].astype(F32)).astype(BF16)
        sent[i] = (left[other].astype(F32) + got[other].astype(F32)).astype(BF16)


def pair_z_kernel(kept, got, own, first, second, third):
    z = lax.axis_index("seq") // 2
    for step, ref in enumerate((own, first, second, third)):
        spot = (z + step) % 4
        ref[...] = (kept[spot].astype(F32) + got[spot].astype(F32)).astype(BF16)


def heavy_y_kernel(own_rows, got_rows, left, got, small, kept, sent, total):
    width = left.shape[1]
    quarter = width // 4
    for part, start, columns in ((0, 0, quarter), (1, quarter, quarter), (2, 2 * quarter, 2 * quarter)):
        former = slice(part * width, (part + 1) * width)
        here = slice(start, start + columns)
        product = dot_left(own_rows[:, former], left[:, here])
        product += dot_left(got_rows[:, former], got[:, here])
        total[:, here] = product.astype(BF16)
    total[:, width:] = turn_small(small[...])
    y = lax.axis_index("seq") % 2
    rows = width // 8
    for i in range(4):
        even = total[2 * i * rows : (2 * i + 1) * rows]
        odd = total[(2 * i + 1) * rows : (2 * i + 2) * rows]
        kept[i] = jnp.where(y == 0, even, odd)
        sent[i] = jnp.where(y == 0, odd, even)


def turn_small(small):
    high = small.astype(BF16)
    low = (small - high.astype(F32)).astype(BF16)
    same = (
        lax.broadcasted_iota(jnp.int32, (small.shape[0], 128), 0)
        == lax.broadcasted_iota(jnp.int32, (small.shape[0], 128), 1)
    ).astype(BF16)
    return (dot_left(high, same) + dot_left(low, same)).astype(BF16)


def total_of(blocks):
    total = blocks[0][...].astype(F32)
    for block in blocks[1:]:
        total = total + block[...].astype(F32)
    return total


def light_end_kernel(own, first, second, third, query, keyval, output):
    total = total_of((own, first, second, third))
    quarter = query.shape[1]
    keyval[...] = total[:, : 2 * quarter]
    query[...] = total[:, 2 * quarter : 3 * quarter]
    output[...] = total[:, 3 * quarter :]


def heavy_end_kernel(own, first, second, third, query, keyval, output, small):
    total = total_of((own, first, second, third))
    quarter = query.shape[1]
    query[...] = total[:, :quarter]
    output[...] = total[:, quarter : 2 * quarter]
    keyval[...] = total[:, 2 * quarter : 4 * quarter]
    same = (
        lax.broadcasted_iota(jnp.int32, (8, 128), 0)
        == lax.broadcasted_iota(jnp.int32, (8, 128), 1)
    ).astype(F32)
    small[...] = lax.dot_general(
        same,
        total[:, 4 * quarter :],
        (((1,), (1,)), ((), ())),
        preferred_element_type=F32,
        precision=HIGHEST,
    )


def feed_end_kernel(own, first, second, third, expand, reduce):
    total = total_of((own, first, second, third))
    hidden, quarter = expand.shape[1], reduce.shape[1]
    rows = total.shape[0]
    more = rows // 3
    expand[...] = total[:, :hidden]
    reduce[:rows] = total[:, hidden : hidden + quarter]
    for piece in range(3):
        reduce[rows:, piece * 64 : (piece + 1) * 64] = total[
            piece * more : (piece + 1) * more, hidden + quarter :
        ]


def stages(count):
    found, stride = [], 1
    while count > 1:
        size = 4 if count % 4 == 0 and count != 8 else 2
        found.append((size, stride))
        stride, count = stride * size, count // size
    return found


def shifted(block, axis, size, stride, step):
    route = []
    for i in range(lax.axis_size(axis)):
        member = (i // stride) % size
        route.append((i, i + ((member + step) % size - member) * stride))
    return lax.ppermute(block, axis, route)


def neighbours(block, distance):
    devices = range(lax.axis_size("seq"))
    return lax.ppermute(
        block, "seq", [(i - distance, i) for i in devices if i - distance in devices]
    )


def member_of(axis, size, stride):
    return (lax.axis_index(axis) // stride) % size


def pick(block, index, dim):
    return lax.dynamic_index_in_dim(block, index, dim, keepdims=False)


def reduce_stage(block, axis, size, stride, dim):
    me = member_of(axis, size, stride)
    total = pick(block, me, dim).astype(F32)
    for step in range(1, size):
        sent = pick(block, (me + step) % size, dim)
        total = total + shifted(sent, axis, size, stride, step).astype(F32)
    return total.astype(BF16)


def reduce_dp(block):
    block = reduce_stage(block, "dp", 2, 1, 0)
    half = block.shape[1] // 2
    first, second = block[:, :half], block[:, half:]
    x = member_of("dp", 2, 2)
    got = shifted(jnp.where(x == 0, second, first), "dp", 2, 2, 1)
    return (jnp.where(x == 0, first, second).astype(F32) + got.astype(F32)).astype(BF16)


def reduce_seq(block, skip=0):
    for size, stride in stages(lax.axis_size("seq"))[skip:]:
        count = lax.axis_size("seq") // stride
        block = block.reshape(count // size, size, block.shape[0] // count, block.shape[1])
        block = reduce_stage(block, "seq", size, stride, 1)
        block = block.reshape(-1, block.shape[-1])
    return block


def gather_part(block, size, stride):
    return jnp.concatenate(
        [block] + [shifted(block, "seq", size, stride, step) for step in range(1, size)], 0
    )


def gather_seq(block):
    for size, stride in stages(lax.axis_size("seq"))[::-1]:
        block = gather_part(block, size, stride)
    return block


def total_parts(parts):
    total = parts[0].astype(F32)
    for part in parts[1:]:
        total = total + part.astype(F32)
    return total


def reduce_pair(kept, sent):
    block = (kept.astype(F32) + shifted(sent, "dp", 2, 1, 1).astype(F32)).astype(BF16)
    return reduce_stage(block, "dp", 2, 2, 0).reshape(-1, block.shape[3])


def swap_rows(axis, stride, whole, mine, other):
    got = shifted(jnp.concatenate([whole, other], 1), axis, 2, stride, 1)
    width = whole.shape[1]
    return (
        jnp.concatenate([whole, got[:, :width]], 0),
        jnp.concatenate([mine, got[:, width:]], 0),
    )


def gather_dp(former, first, second):
    core, x = member_of("dp", 2, 1), member_of("dp", 2, 2)
    half = first.shape[1] // 2

    def both(low, high):
        return jnp.concatenate([low, high], 1)

    lows = both(first[:, :half], second[:, :half])
    highs = both(first[:, half:], second[:, half:])
    former, latter = swap_rows(
        "dp", 1, former, jnp.where(core == 0, lows, highs), jnp.where(core == 0, highs, lows)
    )
    low, high = latter[:, :half], latter[:, half:]
    return swap_rows(
        "dp", 2, former, jnp.where(x == 0, low, high), jnp.where(x == 0, high, low)
    )


def split_rows(former, latter, size, stride):
    rows, width = former.shape
    count = lax.axis_size("seq") // stride
    former = former.reshape(rows, count // size, size, width // count)
    me = member_of("seq", size, stride)
    formers, latters = [pick(former, me, 2).reshape(rows, width // size)], [latter]
    for step in range(1, size):
        other = pick(former, (me + step) % size, 2).reshape(rows, width // size)
        got = shifted(jnp.concatenate([other, latter], 1), "seq", size, stride, step)
        formers.append(got[:, : width // size])
        latters.append(got[:, width // size :])
    return jnp.concatenate(formers, 0), jnp.concatenate(latters, 0)


def outer(former, latter):
    rows, width = former.shape
    columns = latter.shape[1]
    return run(
        outer_kernel, [((width, columns), BF16)], [former, latter], 24, 2e-9 * rows * width * columns
    )[0]


def expand_gradient(former, gate, up):
    former, latter = gather_dp(former, gate, up)
    size, stride = stages(lax.axis_size("seq"))[0]
    former, latter = split_rows(former, latter, size, stride)
    return reduce_seq(outer(former, latter), 1)


def reduce_gradient(former, latter):
    for size, stride in stages(lax.axis_size("seq")):
        former, latter = split_rows(former, latter, size, stride)
    quarter = latter.shape[1] // 4
    parts = [latter[:, i * quarter : (i + 1) * quarter] for i in (0, 2, 1, 3)]
    product = outer(former, jnp.concatenate(parts, 1))
    half = product.shape[1] // 2
    return reduce_dp(jnp.stack([product[:, :half], product[:, half:]]))


def sum_dp(block):
    for stride in (1, 2):
        block = block + shifted(block, "dp", 2, stride, 1)
    return block


def pair_x(kept, sent, deps=(), weight=0):
    got = shifted(sent, "dp", 2, 1, 1)
    left, sent = run(
        pair_x_kernel, [(kept.shape[1:], BF16)] * 2, [kept, got], 24, weight, deps=deps
    )
    return left, sent, shifted(sent, "dp", 2, 2, 1)


def pair_y(left, got, deps=(), weight=0):
    shape = (4,) + left.shape[1:]
    kept, sent = run(pair_y_kernel, [(shape, BF16)] * 2, [left, got], 16, weight, deps=deps)
    return kept, sent, shifted(sent, "seq", 2, 1, 1)


def pair_z(kept, got, deps=(), weight=0):
    own, *sent = run(
        pair_z_kernel, [(kept.shape[1:], BF16)] * 4, [kept, got], 16, weight, deps=deps
    )
    return [own] + [shifted(block, "seq", 4, 2, 1 + i) for i, block in enumerate(sent)]


def send_expand(rows_feed, kept, sent, deps):
    slots, width = rows_feed.shape
    wide = kept.shape[1] // 2
    got = shifted(sent, "dp", 2, 1, 1)
    sent, left = run(
        expand_x_kernel,
        [((2 * slots, width + wide), BF16), ((2 * slots, wide), BF16)],
        [rows_feed, kept, got],
        16,
        deps=deps,
    )
    return sent, left, shifted(sent, "dp", 2, 2, 1)


def send_expand_y(sent, left, got, deps=()):
    rows, wide = left.shape
    half = (sent.shape[1] - wide) // 2
    sent, former = run(
        expand_y_kernel,
        [((2 * rows, half + wide), BF16), ((2 * rows, half), BF16)],
        [sent, left, got],
        16,
        deps=deps,
    )
    return sent, shifted(sent, "seq", 2, 1, 1), former


def send_expand_z(sent, got, former, deps=()):
    wide = sent.shape[1] - former.shape[1]
    rows = former.shape[1] // 4
    own, *sent = run(
        expand_product_kernel,
        [((rows, wide), BF16)] * 4,
        [sent, got, former],
        24,
        0,
        [pltpu.VMEM((4, rows, wide), BF16)],
        deps=deps,
    )
    return [own] + [shifted(block, "seq", 4, 2, 1 + i) for i, block in enumerate(sent)]


def send_reduce_z(own, grad_raw, got, deps=()):
    slots, width = grad_raw.shape
    part = own.shape[1] // 4
    own, *sent = run(
        reduce_z_kernel,
        [((2 * slots, part + width), BF16)] * 4,
        [own, grad_raw, got],
        8,
        deps=deps,
    )
    return [own] + [shifted(block, "seq", 4, 2, 1 + i) for i, block in enumerate(sent)]


def send_reduce_core(parts, width, deps=()):
    rows, wide = parts[0].shape
    half = wide - width
    kept, sent = run(
        reduce_product_kernel,
        [((half, width // 2), BF16)] * 2,
        list(parts),
        12,
        0,
        [pltpu.VMEM((rows, width), BF16)],
        deps=deps,
    )
    return kept, sent, shifted(sent, "dp", 2, 1, 1)


def send_reduce_x(kept, got, deps=()):
    shape = (kept.shape[0], kept.shape[1] // 2)
    left, sent = run(fold_kernel, [(shape, BF16)] * 2, [kept, got], 8, deps=deps)
    return left, shifted(sent, "dp", 2, 2, 1)


def send_rows(rows_query, scaled, rows_keyval):
    slots, width = rows_query.shape
    (joined,) = run(
        rows_kernel, [((slots, 3 * width), BF16)], [rows_query, scaled, rows_keyval], 8
    )
    return joined, shifted(joined, "dp", 2, 1, 1)


def send_rows_x(own, got, deps):
    rows, width = own.shape
    (joined,) = run(stack_two_kernel, [((2 * rows, width), BF16)], [own, got], 8, deps=deps)
    return joined, shifted(joined, "dp", 2, 2, 1)


def on_device(
    tokens,
    cotangent,
    document_bounds,
    routes,
    attention_gain,
    feedforward_gain,
    router,
    light_query,
    light_keyval,
    light_output,
    heavy_query,
    heavy_keyval,
    heavy_output_weight,
    light_expand,
    light_reduce,
    heavy_expand,
    heavy_reduce,
):
    count, width = tokens.shape
    slots = routes.shape[1]
    seq = lax.axis_size("seq")
    length = count * seq
    gain, feed_gain = attention_gain[None], feedforward_gain[None]
    heavy_width = heavy_query.shape[1]

    above = neighbours(tokens[count - WINDOW :], 1)
    below = neighbours(tokens[:WINDOW], -1)
    (packet,) = run(
        select_kernel,
        [((slots, width + 128), BF16)],
        [document_bounds, routes, tokens],
        8,
        0,
        smem=1,
    )
    gathered = gather_seq(packet)
    wide = LH * 128
    low, query, keyval, rows_query, rows_keyval, query_heavy, score_query = run(
        project_kernel,
        [
            ((count, width), BF16),
            ((count, wide), BF16),
            ((count, 2 * wide), BF16),
            ((slots, width), BF16),
            ((slots, width), BF16),
            ((slots, heavy_width), BF16),
            ((slots, 128), F32),
        ],
        [routes, tokens, gain, router, light_query, light_keyval, heavy_query],
        20,
        50,
    )
    span_rows = count + 2 * WINDOW
    attended, peaks, span_low, span = run(
        functools.partial(light_forward_kernel, length),
        [
            ((count, width), BF16),
            ((8, count), F32),
            ((span_rows, width), BF16),
            ((span_rows, 2 * wide), BF16),
        ],
        [document_bounds, query, keyval, low, above, below, gain, light_keyval],
        18,
        60,
        smem=1,
    )
    keyval_heavy, heavy_attended, heavy_scaled, heavy_peaks, own_values, score_keyval = run(
        functools.partial(heavy_forward_kernel, count),
        [
            ((seq * slots, 2 * heavy_width), BF16),
            ((slots, heavy_width), F32),
            ((slots, heavy_width), BF16),
            ((slots, 128), F32),
            ((slots, heavy_width), F32),
            ((slots, 128), F32),
        ],
        [document_bounds, routes, gathered, query_heavy, score_query, gain, router, heavy_keyval],
        16 if seq <= 8 else 48,
        40,
        smem=1,
    )
    residual, feed_low, rows_feed, score_feed, cotangent_rows, grad_raw = run(
        residual_kernel,
        [
            ((count, width), F32),
            ((count, width), BF16),
            ((slots, width), BF16),
            ((slots, 128), F32),
            ((slots, width), F32),
            ((slots, width), BF16),
        ],
        [
            routes, tokens, attended, light_output, heavy_scaled, heavy_output_weight, feed_gain,
            router, cotangent,
        ],
        20,
        30,
    )
    fast = seq == 8
    deps = []
    if fast:
        heavy_rows = send_rows(rows_query, heavy_scaled, rows_keyval)
        deps = [heavy_rows[1]]
    feed = heavy_feed(rows_feed, grad_raw, heavy_expand, heavy_reduce, seq, deps)
    raw_feed, grad_rows = feed[:2]
    rows = width // seq
    if fast:
        expand_kept, expand_sent, reduce_own, reduce_sent = feed[2:]
        reduce_got = shifted(reduce_sent, "seq", 2, 1, 1)
        expand_moves = send_expand(rows_feed, expand_kept, expand_sent, ())
    light_result, grad_low, *feed_grads = light_feed(
        feed_low, cotangent, light_expand, light_reduce, [expand_moves[0]] if fast else []
    )
    deps = []
    if fast:
        reduce_parts = send_reduce_z(reduce_own, grad_raw, reduce_got, [light_result])
        expand_moves = send_expand_y(*expand_moves, reduce_parts[:1])
        heavy_rows = send_rows_x(*heavy_rows, [expand_moves[0]])
        deps = [heavy_rows[0]]
    half = light_reduce.shape[0] // 2
    feed_kept, feed_sent = run(
        feed_products_kernel,
        [((2, seq, rows, half + width // 4 + 64), BF16)] * 2,
        [feed_low, cotangent] + feed_grads,
        18,
        0,
        [pltpu.VMEM((count, 1024), BF16)],
        deps=deps,
    )
    (
        output,
        grad_residual,
        grad_residual_low,
        grad_attended,
        grad_heavy_rows,
        grad_heavy_attended,
        logit_query,
        feed_small,
    ) = run(
        turn_kernel,
        [
            ((count, width), BF16),
            ((count, width), F32),
            ((count, width), BF16),
            ((count, width), BF16),
            ((slots, width), BF16),
            ((slots, heavy_width), BF16),
            ((slots, 128), F32),
            ((2, width), F32),
        ],
        [
            routes, residual, feed_gain, light_result, grad_low, raw_feed, grad_rows, score_feed,
            cotangent_rows, cotangent, router, light_output, heavy_output_weight, heavy_attended,
            score_query,
        ],
        26,
        LONG,
        deps=[feed_sent],
    )
    deps = []
    if fast:
        deps = [heavy_rows[1]]
    deps = []
    if fast:
        feed_left, feed_moved, feed_got = pair_x(feed_kept, feed_sent, [feed_small])
        deps = [feed_moved]
    grad_heavy_query, packet = run(
        functools.partial(heavy_query_kernel, count),
        [((slots, heavy_width), BF16), ((slots, 2 * heavy_width + 128), BF16)],
        [
            document_bounds, routes, gathered, query_heavy, keyval_heavy, heavy_peaks,
            grad_heavy_attended,
        ],
        10 if seq <= 8 else 48,
        LONG,
        smem=1,
        deps=deps,
    )
    sums = [pltpu.VMEM((span_rows, wide // 2), F32)] * 2
    light_ins = [document_bounds, query, span, peaks, grad_attended, attended]
    first_query, first_span = run(
        functools.partial(light_first_kernel, length),
        [((count, width // 2), BF16), ((span_rows, width), BF16)],
        light_ins,
        18,
        0,
        sums,
        smem=1,
        deps=[packet] + ([heavy_rows[1]] if fast else []),
    )
    second_query, second_span, grad_above, grad_below = run(
        functools.partial(light_second_kernel, length),
        [
            ((count, width // 2), BF16),
            ((span_rows, width), BF16),
            ((WINDOW, 2 * width), BF16),
            ((WINDOW, 2 * width), BF16),
        ],
        light_ins + [first_span],
        18,
        0,
        sums,
        smem=1,
    )
    from_above = neighbours(grad_above, -1)
    from_below = neighbours(grad_below, 1)
    mixer_kept, mixer_sent = run(
        light_products_kernel,
        [((2, width, width), BF16)] * 2,
        [
            span_low, first_query, second_query, first_span, second_span, attended,
            grad_residual_low,
        ],
        20,
        0,
    )
    shape = (2, seq, rows, width)
    mixer_kept, mixer_sent = mixer_kept.reshape(shape), mixer_sent.reshape(shape)
    deps = []
    if fast:
        moved_packets = [shifted(packet, "seq", 4, 2, 1 + i) for i in range(3)]
        (stacked,) = run(
            stack_kernel,
            [((4 * slots, packet.shape[1]), BF16)],
            [packet] + moved_packets,
            8,
            LONG,
            deps=[mixer_sent, expand_moves[1], feed_got] + reduce_parts[1:],
        )
        packets = (stacked, shifted(stacked, "seq", 2, 1, 1))
        expand_parts = send_expand_z(*expand_moves, [stacked])
        mixer_left, mixer_sent, mixer_got = pair_x(
            mixer_kept, mixer_sent, expand_parts[:1], LONG
        )
        reduce_moves = send_reduce_core(reduce_parts, width, [mixer_sent])
        deps = list(reduce_moves[:1])
    else:
        packets = gather_seq(packet)
        packets = (packets[: packets.shape[0] // 2], packets[packets.shape[0] // 2 :])
    grad_raw_keyval, logit_keyval = run(
        functools.partial(heavy_key_kernel, count),
        [((slots, 2 * heavy_width), BF16), ((slots, 128), F32)],
        [document_bounds, routes, *packets, keyval_heavy[:slots], own_values, score_keyval],
        16 if seq <= 8 else 56,
        0,
        [pltpu.VMEM((seq * slots, 2 * heavy_width + 128), BF16)],
        smem=1,
        deps=deps,
    )
    deps = []
    if fast:
        heavy_sent, heavy_kept = run(
            heavy_core_kernel,
            [((slots, 2 * width), BF16)] * 2,
            [grad_heavy_query, grad_heavy_rows, grad_raw_keyval],
            8,
        )
        feed_kept, feed_sent, feed_got = pair_y(
            feed_left,
            feed_got,
            [heavy_sent, mixer_got] + expand_parts[1:],
            LONG,
        )
        got = shifted(heavy_sent, "dp", 2, 1, 1)
        heavy_sent, heavy_left = run(
            heavy_x_kernel,
            [((2 * slots, width), BF16)] * 2,
            [heavy_kept, got],
            8,
            deps=[feed_sent],
        )
        heavy_got = shifted(heavy_sent, "dp", 2, 2, 1)
        deps = [heavy_sent]
    (grad_light,) = run(
        mixer_light_kernel,
        [((count, width), F32)],
        [
            first_query, second_query, first_span, second_span, from_below, from_above,
            light_query, light_keyval,
        ],
        16,
        5,
        [pltpu.VMEM((count, 2 * width), BF16)],
        deps=deps,
    )
    deps = []
    if fast:
        light_kept, light_sent, light_got = pair_y(mixer_left, mixer_got, [heavy_sent])
        feed_parts = pair_z(feed_kept, feed_got, [light_sent])
        deps = [heavy_got, feed_parts[0]]
    tokens_grad, small = run(
        mixer_kernel,
        [((count, width), BF16), ((8, width), F32)],
        [
            routes, tokens, gain, router, grad_residual, grad_light, grad_heavy_query,
            grad_raw_keyval, logit_query, logit_keyval, heavy_query, heavy_keyval, feed_small,
        ],
        20,
        LONG,
        deps=deps,
    )
    quarter = width // 4
    hidden = light_reduce.shape[0] // 2
    if fast:
        small = small + shifted(small, "dp", 2, 1, 1)
        light_parts = pair_z(light_kept, light_got, [small] + feed_parts[1:], LONG)
        small = small + shifted(small, "dp", 2, 2, 1)
        kept, sent = run(
            heavy_y_kernel,
            [((4, rows, width + 128), BF16)] * 2,
            [*heavy_rows, heavy_left, heavy_got, small],
            16,
            0,
            [pltpu.VMEM((width, width + 128), BF16)],
            deps=[light_parts[0]],
        )
        got = shifted(sent, "seq", 2, 1, 1)
        reduce_left, reduce_got = send_reduce_x(reduce_moves[0], reduce_moves[2], [heavy_sent])
        grad_heavy_reduce = reduce_left.astype(F32) + reduce_got.astype(F32)
        heavy_parts = pair_z(kept, got, light_parts[1:])
        grad_light_expand, grad_light_reduce = run(
            feed_end_kernel,
            [((rows, hidden), F32), ((light_reduce.shape[0] // seq, quarter), F32)],
            feed_parts,
            8,
        )
        grad_heavy_expand = total_parts(expand_parts)
        grad_light_query, grad_light_keyval, grad_light_output = run(
            light_end_kernel,
            [((rows, quarter), F32), ((rows, 2 * quarter), F32), ((rows, quarter), F32)],
            light_parts,
            8,
        )
        grad_heavy_query, grad_heavy_keyval, grad_heavy_output, small = run(
            heavy_end_kernel,
            [
                ((rows, quarter), F32),
                ((rows, 2 * quarter), F32),
                ((rows, quarter), F32),
                ((8, rows), F32),
            ],
            heavy_parts,
            8,
        )
        smalls = (small[0], small[1], small[2:5])
    else:
        small = sum_dp(small)
        gated_heavy, grad_gate, grad_up = feed[2:]
        grad_heavy_expand = expand_gradient(rows_feed, grad_gate, grad_up).astype(F32)
        grad_heavy_reduce = reduce_gradient(gated_heavy, grad_raw).astype(F32)
        formers = jnp.concatenate([rows_query, heavy_scaled, rows_keyval], 1)

        def mine(part):
            low_columns = slice(part * quarter, (part + 1) * quarter)
            high_columns = slice(2 * part * quarter, 2 * (part + 1) * quarter)
            return [
                grad_heavy_query[:, low_columns],
                grad_heavy_rows[:, low_columns],
                grad_raw_keyval[:, high_columns],
            ]

        first = jnp.concatenate(mine(0) + mine(1), 1)
        second = jnp.concatenate(mine(2) + mine(3), 1)
        formers, latters = gather_dp(formers, first, second)
        (heavy_products,) = run(
            products_kernel,
            [((width, width + 128), BF16)],
            [formers, latters, small],
            16,
            0.6,
        )
        heavy = reduce_seq(heavy_products).astype(F32)
        light = reduce_seq(reduce_pair(mixer_kept, mixer_sent)).astype(F32)
        packed = reduce_seq(reduce_pair(feed_kept, feed_sent)).astype(F32)
        grad_light_query = light[:, 2 * quarter : 3 * quarter]
        grad_light_keyval = light[:, : 2 * quarter]
        grad_light_output = light[:, 3 * quarter :]
        grad_light_expand = packed[:, :hidden]
        rest = packed[:, hidden + quarter :].reshape(3, rows // 3, 64)
        rest = rest.transpose(1, 0, 2).reshape(rows // 3, quarter)
        grad_light_reduce = jnp.concatenate([packed[:, hidden : hidden + quarter], rest], 0)
        grad_heavy_query = heavy[:, :quarter]
        grad_heavy_output = heavy[:, quarter : 2 * quarter]
        grad_heavy_keyval = heavy[:, 2 * quarter : 4 * quarter]
        smalls = (heavy[:, width], heavy[:, width + 1], heavy[:, width + 2 : width + 5].T)
    return (
        output,
        tokens_grad,
        *smalls,
        grad_light_query,
        grad_light_keyval,
        grad_light_output,
        grad_heavy_query,
        grad_heavy_keyval,
        grad_heavy_output,
        grad_light_expand,
        grad_light_reduce,
        grad_heavy_expand,
        grad_heavy_reduce,
    )


def solution(mesh):
    whole, rows = P(), P(("dp", "seq"), None)
    return jax.shard_map(
        on_device,
        mesh=mesh,
        in_specs=(rows, rows, whole, P(None, ("dp", "seq"))) + (whole,) * 13,
        out_specs=(rows, rows, P("seq"), P("seq"), P(None, "seq")) + (P("seq", "dp"),) * 10,
        check_vma=False,
    )
```
